32 devices in a mesh: fsdp: 2 (over y), ctx: 4 (over x, core), tp: 4 (over z).
Axes of the slice: x: 2, y: 2, z: 4, core: 2. Of those that a mesh axis runs over, the one named last changes fastest.
Arguments:
- tokens: bfloat16 [2, 4096, 1536], P('fsdp', 'ctx'), may hold values from -6 to 6
- teacher: bfloat16 [2, 4096, 1536], P('fsdp', 'ctx'), may hold values from -6 to 6
- segment_ids: int32 [2, 4096], P('fsdp', 'ctx'), may hold values from 0 to 4095, as said below
- positions: int32 [2, 4096], P('fsdp', 'ctx'), may hold values from 0 to 6143, as said below
- valid_mask: int32 [2, 4096], P('fsdp', 'ctx'), may hold values 0 or 1
- valid_count: int32 [], replicated, may hold values from 8192 to 32767
- gain_attn: bfloat16 [1536], P(('fsdp', 'ctx')), may hold values from 0.5 to 1.5
- w_query: bfloat16 [1536, 1536], P(('fsdp', 'ctx'), 'tp'), may hold values from -0.15625 to 0.15625
- w_key: bfloat16 [1536, 768], P(('fsdp', 'ctx'), 'tp'), may hold values from -0.15625 to 0.15625
- w_value: bfloat16 [1536, 768], P(('fsdp', 'ctx'), 'tp'), may hold values from -0.15625 to 0.15625
- w_out: bfloat16 [1536, 1536], P('tp', ('fsdp', 'ctx')), may hold values from -6 to 6
- gain_ffn: bfloat16 [1536], P(('fsdp', 'ctx')), may hold values from 0.5 to 1.5
- w_gate: bfloat16 [1536, 4096], P(('fsdp', 'ctx'), 'tp'), may hold values from -0.15625 to 0.15625
- w_up: bfloat16 [1536, 4096], P(('fsdp', 'ctx'), 'tp'), may hold values from -0.15625 to 0.15625
- w_down: bfloat16 [4096, 1536], P('tp', ('fsdp', 'ctx')), may hold values from -0.09375 to 0.09375
Outputs:
- mixed: bfloat16 [2, 4096, 1536], P('fsdp', 'ctx')
- loss: float32 [], replicated
- grad_tokens: float32 [2, 4096, 1536], P('fsdp', 'ctx')
- grad_gain_attn: float32 [1536], P(('fsdp', 'ctx'))
- grad_w_query: float32 [1536, 1536], P(('fsdp', 'ctx'), 'tp')
- grad_w_key: float32 [1536, 768], P(('fsdp', 'ctx'), 'tp')
- grad_w_value: float32 [1536, 768], P(('fsdp', 'ctx'), 'tp')
- grad_w_out: float32 [1536, 1536], P('tp', ('fsdp', 'ctx'))
- grad_gain_ffn: float32 [1536], P(('fsdp', 'ctx'))
- grad_w_gate: float32 [1536, 4096], P(('fsdp', 'ctx'), 'tp')
- grad_w_up: float32 [1536, 4096], P(('fsdp', 'ctx'), 'tp')
- grad_w_down: float32 [4096, 1536], P('tp', ('fsdp', 'ctx'))
The draws below stay inside these ranges and needn't reach their ends.
Inputs may be any that keep to these rules, and one draw needn't show every extreme that they name: `segment_ids`: along each sequence the ids start at 0 and never fall; a run of equal ids is one document, and the last document of every sequence has the id 4096 - 1. In every sequence one document begins within its first 1024 tokens and ends within its last 1024. `positions`: inside a document the position rises by one from token to token.
All inputs are finite; a program needn't handle non-finite values. No bound on the sum of `valid_mask` on one device may be relied on, other than what follows from the above.
Results may differ from the reference program's by a relative error of at most 0.02.
Values may be sent and summed in bfloat16 or wider, within the bound.
No kernel may reach another device: no remote copies, remote signals or barrier semaphores. Data moves between devices by JAX's collectives and lax.ppermute only.
A program may use at most 192 MiB of HBM per device.

```python
import math
import jax
import jax.numpy as jnp
from jax import lax

D = 1536
HQ = 16
HK = 8
HD = 96
FF = 4096
TOK_DEV = 1024
SEQS = 2
SEQ_LEN = 4096
TOKENS = 8192
N_CTX = 4


def document_layout(key):
    key_first, key_last, key_level, key_break = jax.random.split(key, 4)
    opening = jax.random.randint(key_first, (SEQS, 1), 1, TOK_DEV)
    closing = SEQ_LEN - jax.random.randint(key_last, (SEQS, 1), 1, TOK_DEV)
    levels = jax.random.randint(key_level, (SEQS, SEQ_LEN // 16), 1, 8)
    levels = jnp.repeat(levels, 16, axis=1)
    coin_draws = jax.random.randint(key_break, (SEQS, SEQ_LEN), 0, 2 ** levels)
    places = jnp.arange(SEQ_LEN, dtype=jnp.int32)[None, :]
    breaks = (coin_draws == 0) & (places > 0)
    breaks = jnp.where((places > opening) & (places < closing), False, breaks)
    breaks = breaks | (places == opening) | (places == closing)
    segments = jnp.cumsum(breaks.astype(jnp.int32), axis=1).astype(jnp.int32)
    starts = lax.cummax(jnp.where(breaks, places, 0), axis=1)
    return (segments, starts, opening)


def draw_segment_ids(key, part):
    segments, starts, opening = document_layout(key)
    final_id = segments[:, SEQ_LEN - 1:]
    return jnp.where(segments == final_id, SEQ_LEN - 1, segments).astype(jnp.int32)


def draw_positions(key, part):
    segments, starts, opening = document_layout(key)
    key = jax.random.fold_in(key, 12)
    offsets = jax.random.randint(key, (SEQS, SEQ_LEN), 0, 2048)
    own_offset = jnp.take_along_axis(offsets, segments, axis=1)
    places = jnp.arange(SEQ_LEN, dtype=jnp.int32)[None, :]
    long_id = jnp.take_along_axis(segments, opening, axis=1)
    final_id = segments[:, SEQ_LEN - 1:]
    inside = places - starts
    placed = jnp.where(segments == long_id, inside, own_offset + inside)
    return jnp.where(segments == final_id, places + 2048, placed).astype(jnp.int32)


def touch_ends(entries, rng, least, high):
    longest = entries.shape.index(max(entries.shape))
    spots = []
    for shift in (0, 1):
        where = [jax.random.randint(jax.random.fold_in(rng, axis), (), 0, length) for axis, length in enumerate(entries.shape)]
        where[longest] = (where[longest] + shift) % entries.shape[longest]
        spots.append(tuple(where))
    return entries.at[spots[0]].set(least).at[spots[1]].set(high)


def block_levels(own_key, shape, cuts, smallest, largest):
    def one(dim, shards_of):
        draws = jax.random.uniform(jax.random.fold_in(jax.random.fold_in(own_key, 6), dim), (shards_of,), jnp.float32, smallest / len(cuts), largest / len(cuts))
        return jnp.repeat(jnp.exp(draws), shape[dim] // shards_of).reshape((-1,) + (1,) * (len(shape) - dim - 1))

    loudness = one(*cuts[0])
    for cut in cuts[1:]:
        loudness = loudness * one(*cut)
    return loudness


def noise(own_key, extent, spread, reach, shards=(), kind=jnp.bfloat16):
    entries = spread * jax.random.normal(own_key, extent, jnp.float32)
    if shards:
        entries = entries * block_levels(own_key, extent, shards, -0.22, 0.18)
    return jnp.clip(entries, -reach, reach).astype(kind)


def setup_inputs(seed: int = 0) -> dict:
    keys = jax.random.split(jax.random.key(seed), 16)
    return {
        "tokens": noise(keys[0], (SEQS, SEQ_LEN, D), 1.0, 6.0, ((0, 2), (1, 4))),
        "teacher": noise(keys[1], (SEQS, SEQ_LEN, D), 1.0, 6.0, ((0, 2), (1, 4))),
        "segment_ids": draw_segment_ids(jax.random.fold_in(keys[15], 71), 0),
        "positions": draw_positions(jax.random.fold_in(keys[15], 71), 0),
        "valid_mask": touch_ends((jax.random.randint(keys[4], (SEQS, SEQ_LEN), 0, 8) < 7).astype(jnp.int32), jax.random.fold_in(keys[4], 1), 0, 1),
        "valid_count": jax.random.randint(keys[5], (), TOKENS, 4 * TOKENS).astype(jnp.int32),
        "gain_attn": jnp.clip(1.0 + 0.1 * jax.random.normal(keys[6], (D,), jnp.float32), 0.5, 1.5).astype(jnp.bfloat16),
        "w_query": noise(keys[7], (D, HQ * HD), D ** -0.5, 0.15625, ((0, 8), (1, 4))),
        "w_key": noise(keys[8], (D, HK * HD), D ** -0.5, 0.15625, ((0, 8), (1, 4))),
        "w_value": noise(keys[9], (D, HK * HD), D ** -0.5, 0.15625, ((0, 8), (1, 4))),
        "w_out": noise(keys[10], (HQ * HD, D), (max(1, HQ * HD * 4 // (TOK_DEV * N_CTX))) ** -0.5, 6.0, ((0, 4), (1, 8))),
        "gain_ffn": jnp.clip(1.0 + 0.1 * jax.random.normal(keys[11], (D,), jnp.float32), 0.5, 1.5).astype(jnp.bfloat16),
        "w_gate": noise(keys[12], (D, FF), D ** -0.5, 0.15625, ((0, 8), (1, 4))),
        "w_up": noise(keys[13], (D, FF), D ** -0.5, 0.15625, ((0, 8), (1, 4))),
        "w_down": noise(keys[14], (FF, D), FF ** -0.5, 0.09375, ((0, 4), (1, 8))),
    }


EPSILON = 1e-05
ROPE_BASE = 100000.0
MASKED = -1e+30

@jax.custom_vjp
def low(v):
    return lax.optimization_barrier(v.astype(jnp.bfloat16)).astype(jnp.float32)

@jax.custom_vjp
def low_back(v):
    return v

def low_keep(v):
    return (low(v), None)

def low_pass(kept, grad):
    return (grad,)

def back_keep(v):
    return (v, None)

def back_low(kept, grad):
    return (low(grad),)
low.defvjp(low_keep, low_pass)
low_back.defvjp(back_keep, back_low)

def matmul(left_op, right_op):
    return jnp.dot(left_op, right_op, precision=lax.Precision.HIGHEST)

def normalize(values, gain_vec):
    factor = lax.rsqrt(lax.optimization_barrier(jnp.mean(values * values, axis=-1, keepdims=True)) + EPSILON)
    return values * factor * gain_vec

def rope_tables(places):
    half_dim = HD // 2
    frequency = jnp.exp(jnp.arange(half_dim).astype(jnp.float32) * (-2.0 * math.log(ROPE_BASE) / HD))
    angles = places.astype(jnp.float32)[..., None] * frequency
    return (jnp.cos(angles), jnp.sin(angles))

def rotate(values, cos_table, sin_table):
    half_dim = values.shape[-1] // 2
    lower_half = values[..., :half_dim]
    upper_half = values[..., half_dim:]
    return jnp.concatenate([lower_half * cos_table - upper_half * sin_table, upper_half * cos_table + lower_half * sin_table], axis=-1)

def attend_sequence(sequence_item):
    queries, key_rows, values, seg_ids = sequence_item
    length = queries.shape[0]
    block_rows = 512 if length % 512 == 0 else length
    count_blocks = length // block_rows
    where_key = jnp.arange(length)

    def one_block(block_item):
        q_block, q_seg, q_start = block_item
        grouped = q_block.reshape(block_rows, HK, HQ // HK, HD)
        scores = jnp.einsum('qkgd,nkd->kgqn', grouped, key_rows, precision=lax.Precision.HIGHEST) * HD ** (-0.5)
        scores = low_back(scores)
        where_query = q_start + jnp.arange(block_rows)
        allowed = (q_seg[:, None] == seg_ids[None, :]) & (where_key[None, :] <= where_query[:, None])
        scores = jnp.where(allowed, scores, MASKED)
        row_max = lax.optimization_barrier(jnp.max(scores, axis=-1, keepdims=True))
        exp_scores = jnp.exp(scores - row_max)
        prob_rows = exp_scores / lax.optimization_barrier(jnp.sum(exp_scores, axis=-1, keepdims=True))
        mixed_block = jnp.einsum('kgqn,nkd->qkgd', low(prob_rows), values, precision=lax.Precision.HIGHEST)
        return mixed_block.reshape(block_rows, HQ, HD)
    block_items = (queries.reshape(count_blocks, block_rows, HQ, HD), seg_ids.reshape(count_blocks, block_rows), jnp.arange(count_blocks) * block_rows)
    return lax.map(jax.checkpoint(one_block), block_items).reshape(length, HQ, HD)

def reference(tokens, teacher, segment_ids, positions, valid_mask, valid_count, gain_attn, w_query, w_key, w_value, w_out, gain_ffn, w_gate, w_up, w_down):
    cos_table, sin_table = rope_tables(positions)
    cos_table = cos_table[:, :, None, :]
    sin_table = sin_table[:, :, None, :]
    target = teacher.astype(jnp.float32).reshape(-1, D)
    valid_rows = valid_mask.astype(jnp.float32).reshape(-1, 1)

    def forward(inputs, gain_att, query_w, key_w, value_w, out_w, gain_mlp, gate_w, up_w, down_w):
        rows_in = inputs.reshape(-1, D)
        hidden_a = low(normalize(rows_in, gain_att))
        query_lin = low_back(matmul(hidden_a, query_w)).reshape(SEQS, SEQ_LEN, HQ, HD)
        key_lin = low_back(matmul(hidden_a, key_w)).reshape(SEQS, SEQ_LEN, HK, HD)
        value_all = low(low_back(matmul(hidden_a, value_w))).reshape(SEQS, SEQ_LEN, HK, HD)
        query_rot = low(rotate(query_lin, cos_table, sin_table))
        key_rot = low(rotate(key_lin, cos_table, sin_table))
        heads_out = lax.map(attend_sequence, (query_rot, key_rot, value_all, segment_ids))
        attended = low(low_back(heads_out.reshape(-1, HQ * HD)))
        resid_mid = rows_in + low_back(matmul(attended, out_w))
        hidden_f = low(normalize(resid_mid, gain_mlp))
        gate_lin = low_back(matmul(hidden_f, gate_w))
        up_lin = low_back(matmul(hidden_f, up_w))
        inner_act = low(jax.nn.silu(gate_lin) * up_lin)
        result_rows = resid_mid + low_back(matmul(inner_act, down_w))
        error_rows = result_rows - target
        return (result_rows, 0.5 * jnp.sum(valid_rows * error_rows * error_rows))
    (result_rows, half_error), pullback = jax.vjp(forward, tokens.astype(jnp.float32), gain_attn.astype(jnp.float32), w_query.astype(jnp.float32), w_key.astype(jnp.float32), w_value.astype(jnp.float32), w_out.astype(jnp.float32), gain_ffn.astype(jnp.float32), w_gate.astype(jnp.float32), w_up.astype(jnp.float32), w_down.astype(jnp.float32))
    gradients = pullback((jnp.zeros_like(result_rows), jnp.ones_like(half_error)))
    loss_value = 2.0 * half_error / (valid_count.astype(jnp.float32) * D)
    return (result_rows.reshape(tokens.shape).astype(jnp.bfloat16), loss_value, gradients[0].reshape(tokens.shape), gradients[1], gradients[2], gradients[3], gradients[4], gradients[5], gradients[6], gradients[7], gradients[8], gradients[9])
```

```python
import functools
import math

import jax
import jax.numpy as jnp
from jax import lax
from jax.experimental import pallas as pl
from jax.experimental.pallas import tpu as pltpu
from jax.sharding import Mesh
from jax.sharding import PartitionSpec as P

HD=96
NEG=-1e30
F32=jnp.float32; BF=jnp.bfloat16
def dot(a,b,ca,cb):
    return lax.dot_general(a,b,(((ca,),(cb,)),((),())),preferred_element_type=F32)

def fwd_kernel(scale2, tq, tk, group, bounds, q_ref, k_ref, v_ref, st_ref, qp_ref, o_ref, of_ref, lse_ref, ks, m_s, l_s, acc):
    i = pl.program_id(1)
    @pl.when(i == 0)
    def _():
        ks[...] = k_ref[...].astype(F32).T.astype(BF)
    q2 = jnp.concatenate([q_ref[h*HD:(h+1)*HD, :] for h in range(group)], axis=1)
    st = jnp.concatenate([st_ref[...]]*group, axis=1)
    qp = jnp.concatenate([qp_ref[...]]*group, axis=1)
    m_s[...] = jnp.full_like(m_s, NEG)
    l_s[...] = jnp.zeros_like(l_s)
    acc[...] = jnp.zeros_like(acc)
    def step(masked, j, _):
        off = pl.multiple_of(j*tk, tk)
        s = dot(ks[pl.ds(off, tk), :], q2, 1, 0)
        if masked:
            kid = off + lax.broadcasted_iota(jnp.int32, s.shape, 0)
            s = jnp.where((kid >= st) & (kid <= qp), s, NEG)
        m_old = m_s[...]
        m_new = jnp.maximum(m_old, jnp.max(s, axis=0, keepdims=True))
        p = jnp.exp2((s - m_new)*scale2)
        al = jnp.exp2((m_old - m_new)*scale2)
        l_s[...] = l_s[...]*al + jnp.sum(p, axis=0, keepdims=True)
        m_s[...] = m_new
        acc[...] = acc[...]*al + dot(v_ref[:, pl.ds(off, tk)], p.astype(BF), 1, 0)
        return 0
    lo, a, b, hi = bounds[i,0], bounds[i,1], bounds[i,2], bounds[i,3]
    lax.fori_loop(lo, a, functools.partial(step, True), 0)
    lax.fori_loop(a, b, functools.partial(step, False), 0)
    lax.fori_loop(b, hi, functools.partial(step, True), 0)
    o = acc[...]/l_s[...]
    lse = m_s[...]*scale2 + jnp.log2(l_s[...])
    for h in range(group):
        oh = o[:, h*tq:(h+1)*tq]
        of_ref[h*HD:(h+1)*HD, :] = oh
        o_ref[h*HD:(h+1)*HD, :] = oh.astype(BF)
        lse_ref[0, h:h+1, :] = lse[:, h*tq:(h+1)*tq]

def attn_fwd(qT, kT, vT, start, qpos, bounds, tq=256, tk=512):
    T = qT.shape[1]; N = kT.shape[1]; kv = kT.shape[0]//HD; group = qT.shape[0]//kT.shape[0]
    scale2 = HD**-0.5*math.log2(math.e)
    qs = pl.BlockSpec((group*HD, tq), lambda g,i,b:(g,i))
    ksp = pl.BlockSpec((HD, N), lambda g,i,b:(g,0))
    row = pl.BlockSpec((1, tq), lambda g,i,b:(0,i))
    return pl.pallas_call(
        functools.partial(fwd_kernel, scale2, tq, tk, group),
        out_shape=(jax.ShapeDtypeStruct(qT.shape, BF), jax.ShapeDtypeStruct(qT.shape, F32), jax.ShapeDtypeStruct((kv, group, T), F32)),
        grid_spec=pltpu.PrefetchScalarGridSpec(num_scalar_prefetch=1, grid=(kv, T//tq),
            in_specs=[qs, ksp, ksp, row, row],
            out_specs=[qs, qs, pl.BlockSpec((1, group, tq), lambda g,i,b:(g,0,i))],
            scratch_shapes=[pltpu.VMEM((N,HD),BF), pltpu.VMEM((1,group*tq),F32), pltpu.VMEM((1,group*tq),F32), pltpu.VMEM((HD,group*tq),F32)]),
        compiler_params=pltpu.CompilerParams(vmem_limit_bytes=48*2**20),
        name="attend",
    )(bounds, qT, kT, vT, start, qpos)

def bwd_kernel(scale2, tq, tk, group, bounds, q_ref, k_ref, v_ref, st_ref, qp_ref, g_ref, of_ref, lse_ref, dq_ref, dk_ref, dv_ref, ks, vs, dks, dvs, dqs):
    i = pl.program_id(1)
    @pl.when(i == 0)
    def _():
        ks[...] = k_ref[...].astype(F32).T.astype(BF)
        vs[...] = v_ref[...].astype(F32).T.astype(BF)
        dks[...] = jnp.zeros_like(dks)
        dvs[...] = jnp.zeros_like(dvs)
    cat = lambda f: jnp.concatenate([f(h) for h in range(group)], axis=1)
    q2 = cat(lambda h: q_ref[h*HD:(h+1)*HD, :])
    g2 = cat(lambda h: g_ref[h*HD:(h+1)*HD, :])
    lse = cat(lambda h: lse_ref[0, h:h+1, :])
    delta = cat(lambda h: jnp.sum(g_ref[h*HD:(h+1)*HD, :].astype(F32)*of_ref[h*HD:(h+1)*HD, :], axis=0, keepdims=True))
    st = cat(lambda h: st_ref[...])
    qp = cat(lambda h: qp_ref[...])
    dqs[...] = jnp.zeros_like(dqs)
    def step(masked, j, _):
        off = pl.multiple_of(j*tk, tk)
        s = dot(ks[pl.ds(off, tk), :], q2, 1, 0)
        if masked:
            kid = off + lax.broadcasted_iota(jnp.int32, s.shape, 0)
            s = jnp.where((kid >= st) & (kid <= qp), s, NEG)
        p = jnp.exp2(s*scale2 - lse)
        dp = dot(vs[pl.ds(off, tk), :], g2, 1, 0)
        ds = (p*(dp - delta)).astype(BF)
        dvs[:, pl.ds(off, tk)] += dot(g2, p.astype(BF), 1, 1)
        dks[:, pl.ds(off, tk)] += dot(q2, ds, 1, 1)
        dqs[...] += dot(k_ref[:, pl.ds(off, tk)], ds, 1, 0)
        return 0
    lo, a, b, hi = bounds[i,0], bounds[i,1], bounds[i,2], bounds[i,3]
    lax.fori_loop(lo, a, functools.partial(step, True), 0)
    lax.fori_loop(a, b, functools.partial(step, False), 0)
    lax.fori_loop(b, hi, functools.partial(step, True), 0)
    for h in range(group):
        dq_ref[h*HD:(h+1)*HD, :] = dqs[:, h*tq:(h+1)*tq]
    @pl.when(i == pl.num_programs(1)-1)
    def _():
        dk_ref[...] = dks[...].astype(BF)
        dv_ref[...] = dvs[...].astype(BF)

def attn_bwd(qT, kT, vT, start, qpos, bounds, gT, of, lse, tq=256, tk=512):
    T = qT.shape[1]; N = kT.shape[1]; kv = kT.shape[0]//HD; group = qT.shape[0]//kT.shape[0]
    scale2 = HD**-0.5*math.log2(math.e)
    qs = pl.BlockSpec((group*HD, tq), lambda g,i,b:(g,i))
    ksp = pl.BlockSpec((HD, N), lambda g,i,b:(g,0))
    row = pl.BlockSpec((1, tq), lambda g,i,b:(0,i))
    return pl.pallas_call(
        functools.partial(bwd_kernel, scale2, tq, tk, group),
        out_shape=(jax.ShapeDtypeStruct(qT.shape, F32), jax.ShapeDtypeStruct(kT.shape, BF), jax.ShapeDtypeStruct(kT.shape, BF)),
        grid_spec=pltpu.PrefetchScalarGridSpec(num_scalar_prefetch=1, grid=(kv, T//tq),
            in_specs=[qs, ksp, ksp, row, row, qs, qs, pl.BlockSpec((1, group, tq), lambda g,i,b:(g,0,i))],
            out_specs=[qs, ksp, ksp],
            scratch_shapes=[pltpu.VMEM((N,HD),BF), pltpu.VMEM((N,HD),BF), pltpu.VMEM((HD,N),F32), pltpu.VMEM((HD,N),F32), pltpu.VMEM((HD,group*tq),F32)]),
        compiler_params=pltpu.CompilerParams(vmem_limit_bytes=56*2**20),
        name="attend_back",
    )(bounds, qT, kT, vT, start, qpos, gT, of, lse)

def make_bounds(start, q_first, T, tq, tk):
    s = start.reshape(-1, tq)
    first = q_first + jnp.arange(T//tq, dtype=jnp.int32)*tq
    lo = s[:,0]//tk
    hi = (first + tq - 1)//tk + 1
    a = jnp.minimum((s[:,-1] + tk - 1)//tk, hi)
    b = jnp.maximum(first//tk, a)
    return jnp.stack([lo,a,b,hi],axis=1).astype(jnp.int32)

EPSILON = 1e-05
ROPE_BASE = 100000.0
AXES = ("fsdp", "cx", "cc", "tp")


def swap(values, axis, step=1):
    size = lax.axis_size(axis)
    return lax.ppermute(values, axis, [(i, i ^ step) for i in range(size)])


def ordered(parts, index):
    if len(parts) == 1:
        return list(parts)
    if len(parts) == 2:
        first = index == 0
        return [jnp.where(first, parts[0], parts[1]), jnp.where(first, parts[1], parts[0])]
    stacked = jnp.stack(parts)
    return [
        lax.dynamic_index_in_dim(stacked, jnp.bitwise_xor(index, a), 0, keepdims=False)
        for a in range(len(parts))
    ]


def everyone(values, axis):
    return [values] + [swap(values, axis, k) for k in range(1, lax.axis_size(axis))]


def place_kernel(count, width, place, *refs):
    sources, out, sems = refs[:-2], refs[-2], refs[-1]
    copies = []
    n = 0
    for source in sources:
        for b in range(source.shape[0]):
            copies.append(
                pltpu.make_async_copy(source.at[b], out.at[place[n]], sems.at[n])
            )
            n += 1
    for copy in copies:
        copy.start()
    for copy in copies:
        copy.wait()


def put_blocks(sources, place):
    count = sum(s.shape[0] for s in sources)
    shape = sources[0].shape[1:]
    return pl.pallas_call(
        functools.partial(place_kernel, count, None),
        out_shape=jax.ShapeDtypeStruct((count,) + shape, sources[0].dtype),
        in_specs=[pl.BlockSpec(memory_space=pltpu.SMEM)]
        + [pl.BlockSpec(memory_space=pl.ANY)] * len(sources),
        out_specs=pl.BlockSpec(memory_space=pl.ANY),
        scratch_shapes=[pltpu.SemaphoreType.DMA((count,))],
        name="put_blocks",
    )(jnp.stack(place).astype(jnp.int32), *sources)


def gather_rows(shard):
    rows, width = shard.shape
    nf, nx, nc = (lax.axis_size(a) for a in ("fsdp", "cx", "cc"))
    y, x, c = (lax.axis_index(a) for a in ("fsdp", "cx", "cc"))
    half = rows // 2
    if nf == 2 and nx == 2:
        from_x = swap(shard, "cx")
        from_y = swap(shard, "fsdp")
        top = swap(from_y[:half], "cx")
        low = swap(from_x[half:], "fsdp")
        near = jnp.concatenate([shard, from_x, from_y, top, low], axis=0)
    else:
        near = jnp.concatenate(everyone(shard, "cx"), axis=0)
        near = jnp.concatenate(everyone(near, "fsdp"), axis=0)
    sources = [v.reshape(nf * nx, rows, width) for v in everyone(near, "cc")]
    place = [
        ((y ^ dy) * nc + (c ^ dc)) * nx + (x ^ dx)
        for dc in range(nc)
        for dy in range(nf)
        for dx in range(nx)
    ]
    return put_blocks(sources, place).reshape(nf * nc * nx * rows, width)


def scatter_rows(part):
    nf, nx, nc = (lax.axis_size(a) for a in ("fsdp", "cx", "cc"))
    y, x, c = (lax.axis_index(a) for a in ("fsdp", "cx", "cc"))
    width = part.shape[1]
    total = part.reshape(nf, nc, -1, width)
    total = summed(total, 1, "cc", c)
    total = summed(total.astype(jnp.bfloat16), 0, "fsdp", y)
    total = summed(total.astype(jnp.bfloat16).reshape(nx, -1, width), 0, "cx", x)
    return total


def summed(part, dim, axis, index):
    take = lambda k: lax.dynamic_index_in_dim(part, index ^ k, dim, keepdims=False)
    total = take(0).astype(jnp.float32)
    for k in range(1, lax.axis_size(axis)):
        total = total + swap(take(k), axis, k).astype(jnp.float32)
    return total


def reordered(values, nf, first, second):
    width = values.shape[1] // (nf * first * second)
    blocks = [
        (f * first + a) * second + b
        for f in range(nf)
        for b in range(second)
        for a in range(first)
    ]
    return jnp.concatenate([values[:, b * width : (b + 1) * width] for b in blocks], axis=1)


def norm_parts(values):
    factor = lax.rsqrt(jnp.mean(values * values, axis=-1, keepdims=True) + EPSILON)
    return (factor, values * factor)


def norm_back(grad_normed_in, normed, factor, gain_vec):
    grad_normed = grad_normed_in * gain_vec
    return factor * (grad_normed - normed * jnp.mean(grad_normed * normed, axis=-1, keepdims=True))


def turned(values, cos_table, sin_table):
    half = values.shape[1] // 2
    low, high = values[:, :half], values[:, half:]
    return jnp.concatenate(
        [low * cos_table - high * sin_table, high * cos_table + low * sin_table], axis=1
    )


def whole_block(ref):
    block = ref[...]
    return block.reshape(block.shape[1] * block.shape[3], block.shape[4])


def ffn_forward_kernel(own, h_ref, wg_ref, wu_ref, wd_ref, slope_ref, act_ref, inner_ref, out_ref, send_ref, acc):
    z = pl.program_id(0)
    hidden = h_ref[...]
    gate = dot(hidden, whole_block(wg_ref), 1, 0)
    up = dot(hidden, whole_block(wu_ref), 1, 0)
    sig = jax.nn.sigmoid(gate)
    act = gate * sig
    slope_ref[...] = up * (sig * (1.0 + gate * (1.0 - sig)))
    act_ref[...] = act
    inner = (act * up).astype(BF)
    inner_ref[...] = inner
    added = dot(inner, whole_block(wd_ref), 1, 1)

    @pl.when(z == 0)
    def _():
        acc[...] = added

    @pl.when(z > 0)
    def _():
        acc[...] += added

    @pl.when(z == pl.num_programs(0) - 1)
    def _():
        out_ref[...] = acc[:own, :]
        if send_ref.shape[0] == acc.shape[0] - own:
            send_ref[...] = acc[own:, :].astype(BF)


def ffn_forward(hidden, weights, own):
    rows, width = hidden.shape
    nz, nb, _, nr, hs = weights.shape
    wspec = lambda m: pl.BlockSpec((1, nb, 1, nr, hs), lambda z: (z, 0, m, 0, 0))
    full = lambda n: pl.BlockSpec((n, width), lambda z: (0, 0))
    col = pl.BlockSpec((rows, hs), lambda z: (0, z))
    shape = jax.ShapeDtypeStruct
    return pl.pallas_call(
        functools.partial(ffn_forward_kernel, own),
        out_shape=(
            shape((rows, nz * hs), F32),
            shape((rows, nz * hs), F32),
            shape((rows, nz * hs), BF),
            shape((own, width), F32),
            shape((max(rows - own, 16), width), BF),
        ),
        grid=(nz,),
        in_specs=[full(rows), wspec(0), wspec(1), wspec(2)],
        out_specs=[col, col, col, full(own), full(max(rows - own, 16))],
        scratch_shapes=[pltpu.VMEM((rows, width), F32)],
        compiler_params=pltpu.CompilerParams(vmem_limit_bytes=56 * 2**20),
        name="feed_forward",
    )(hidden, weights, weights, weights)


def ffn_backward_kernel(own, g_ref, wg_ref, wu_ref, wd_ref, slope_ref, act_ref, gg_ref, gu_ref, out_ref, send_ref, acc):
    z = pl.program_id(0)
    grad_inner = dot(g_ref[...], whole_block(wd_ref), 1, 0)
    gg = (grad_inner * slope_ref[...]).astype(BF)
    gu = (grad_inner * act_ref[...]).astype(BF)
    gg_ref[...] = gg
    gu_ref[...] = gu
    added = dot(gg, whole_block(wg_ref), 1, 1) + dot(gu, whole_block(wu_ref), 1, 1)

    @pl.when(z == 0)
    def _():
        acc[...] = added

    @pl.when(z > 0)
    def _():
        acc[...] += added

    @pl.when(z == pl.num_programs(0) - 1)
    def _():
        out_ref[...] = acc[:own, :]
        if send_ref.shape[0] == acc.shape[0] - own:
            send_ref[...] = acc[own:, :].astype(BF)


def ffn_backward(grad, weights, slope, act, own):
    rows, width = grad.shape
    nz, nb, _, nr, hs = weights.shape
    wspec = lambda m: pl.BlockSpec((1, nb, 1, nr, hs), lambda z: (z, 0, m, 0, 0))
    full = lambda n: pl.BlockSpec((n, width), lambda z: (0, 0))
    col = pl.BlockSpec((rows, hs), lambda z: (0, z))
    shape = jax.ShapeDtypeStruct
    return pl.pallas_call(
        functools.partial(ffn_backward_kernel, own),
        out_shape=(
            shape((rows, nz * hs), BF),
            shape((rows, nz * hs), BF),
            shape((own, width), F32),
            shape((max(rows - own, 16), width), BF),
        ),
        grid=(nz,),
        in_specs=[full(rows), wspec(0), wspec(1), wspec(2), col, col],
        out_specs=[col, col, full(own), full(max(rows - own, 16))],
        scratch_shapes=[pltpu.VMEM((rows, width), F32)],
        compiler_params=pltpu.CompilerParams(vmem_limit_bytes=56 * 2**20),
        name="feed_forward_back",
    )(grad, weights, weights, weights, slope, act)


def weight_grad_kernel(count, *refs):
    left, rights, outs, flipped = refs[0], refs[1 : 1 + count], refs[1 + count : 1 + 2 * count], refs[-1]

    @pl.when(pl.program_id(0) == 0)
    def _():
        flipped[...] = left[...].astype(F32).T.astype(BF)

    for right, out in zip(rights, outs):
        out[0] = dot(flipped[...], right[...], 1, 0).astype(BF)


def weight_grad(left, rights, nz):
    rows, width = left.shape
    hs = rights[0].shape[1] // nz
    count = len(rights)
    return pl.pallas_call(
        functools.partial(weight_grad_kernel, count),
        out_shape=(jax.ShapeDtypeStruct((nz, width, hs), BF),) * count,
        grid=(nz,),
        in_specs=[pl.BlockSpec((rows, width), lambda z: (0, 0))]
        + [pl.BlockSpec((rows, hs), lambda z: (0, z))] * count,
        out_specs=[pl.BlockSpec((1, width, hs), lambda z: (z, 0, 0))] * count,
        scratch_shapes=[pltpu.VMEM((width, rows), BF)],
        compiler_params=pltpu.CompilerParams(vmem_limit_bytes=56 * 2**20),
        name="weight_grad",
    )(left, *rights)


def on_device(
    tokens, teacher, segment_ids, positions, valid_mask, valid_count, gain_attn, w_query, w_key,
    w_value, w_out, gain_ffn, w_gate, w_up, w_down,
):
    nf, nx, nc, nz = (lax.axis_size(a) for a in AXES)
    y, x, c, z = (lax.axis_index(a) for a in AXES)
    place = x * nc + c
    rows, width = tokens.shape[1:]
    share = rows // nz
    feat = w_query.shape[0]
    q_cols, kv_cols = w_query.shape[1], w_key.shape[1]
    heads_k = kv_cols // HD
    hidden_dev = w_gate.shape[1]
    hs = hidden_dev // nx
    own_rows = lambda v: lax.dynamic_slice_in_dim(v, z * share, share, 0)
    att_scale = HD ** (-0.5)

    gains = jnp.stack([gain_attn, gain_ffn], axis=1)
    gains = jnp.pad(gains, ((0, 0), (0, 126)))
    in_weights = gather_rows(jnp.concatenate([w_query, w_key, w_value, gains], axis=1))
    w_qkv = in_weights[:, : q_cols + 2 * kv_cols]
    gain_att, gain_mlp = (
        in_weights[:, q_cols + 2 * kv_cols + i][None].astype(F32) for i in range(2)
    )

    ffn_stack = jnp.stack([w_gate, w_up, w_down.T])
    hidden_part = lambda k: lax.dynamic_slice_in_dim(ffn_stack, (x ^ k) * hs, hs, 2)
    pieces = [hidden_part(0)] + [swap(hidden_part(k), "cx", k) for k in range(1, nx)]
    ffn_shard = jnp.stack(ordered(pieces, x), axis=1).reshape(3 * nx * feat, hs)
    ffn_weights = lax.all_gather(ffn_shard, ("tp", "fsdp", "cc"), axis=0, tiled=True)
    ffn_weights = ffn_weights.reshape(nz, nf * nc, 3, nx * feat, hs)

    seg_own = segment_ids[0]
    seg_parts = everyone(seg_own[None], "cx")
    seg_near = jnp.concatenate(ordered(seg_parts, x), axis=0)
    seg_all = jnp.stack(ordered(everyone(seg_near, "cc"), c), axis=1).reshape(1, -1)
    doc_start = jnp.sum((seg_all < seg_own[:, None]).astype(jnp.int32), axis=1)[None]
    query_place = place * rows + jnp.arange(rows, dtype=jnp.int32)[None]
    half = HD // 2
    frequency = jnp.exp(
        jnp.arange(half).astype(F32) * (-2.0 * math.log(ROPE_BASE) / HD)
    )
    angles = frequency[:, None] * positions[0].astype(F32)[None]
    cos_table, sin_table = jnp.cos(angles)[None], jnp.sin(angles)[None]

    rows_bf = reordered(tokens[0], nf, nx, nc)
    rows_f = rows_bf.astype(F32)
    scale_a, normed_a = norm_parts(rows_f)
    hidden_a = (normed_a * gain_att).astype(BF)
    kv_lin = dot(w_qkv[:, q_cols:], hidden_a, 0, 1)
    k_rot = turned(kv_lin[:kv_cols].reshape(heads_k, HD, rows), cos_table, sin_table)
    kv_own = jnp.concatenate([k_rot.reshape(kv_cols, rows), kv_lin[kv_cols:]], axis=0).astype(BF)
    q_lin = dot(w_qkv[:, :q_cols], hidden_a, 0, 1)
    q_rot = turned(q_lin.reshape(-1, HD, rows), cos_table, sin_table).reshape(q_cols, rows).astype(BF)
    kv_near = jnp.stack(everyone(kv_own, "cx"))
    kv_all = put_blocks(
        everyone(kv_near, "cc"),
        [(x ^ dx) * nc + (c ^ dc) for dc in range(nc) for dx in range(nx)],
    )
    kv_all = jnp.concatenate([kv_all[i] for i in range(nx * nc)], axis=1)
    k_all, v_all = kv_all[:kv_cols], kv_all[kv_cols:]

    out_weights = gather_rows(jnp.concatenate(everyone(w_out.T, "tp"), axis=1))

    first_row = place * rows
    o_t, o_f, lse = attn_fwd(
        q_rot, k_all, v_all, doc_start, query_place,
        make_bounds(doc_start, first_row, rows, FWD_TQ, FWD_TK), FWD_TQ, FWD_TK,
    )

    chunk = lambda v, k: lax.dynamic_slice_in_dim(v, (z ^ k) * share, share, 1)
    att_t = jnp.concatenate(
        [chunk(o_t, 0)] + [swap(chunk(o_t, k), "tp", k) for k in range(1, nz)], axis=0
    )
    resid = own_rows(rows_f) + dot(att_t, out_weights, 0, 1)
    scale_f, normed_f = norm_parts(resid)
    hidden_own = (normed_f * gain_mlp).astype(BF)
    hidden_f = jnp.concatenate(everyone(hidden_own, "cx"), axis=0)
    slope, act, inner, ffn_own, ffn_send = ffn_forward(hidden_f, ffn_weights, share)

    def returned(own, send):
        for k in range(1, nx):
            own = own + swap(send[(k - 1) * share : k * share], "cx", k).astype(F32)
        return own

    result = resid + returned(ffn_own, ffn_send)
    target = reordered(own_rows(teacher[0]), nf, nx, nc).astype(F32)
    valid = own_rows(valid_mask[0].astype(F32)[:, None])
    error = result - target
    grad_out = valid * error
    loss_part = jnp.sum(grad_out * error)
    grad_ffn = jnp.concatenate(everyone(grad_out.astype(BF), "cx"), axis=0)
    (part_down,) = weight_grad(grad_ffn, [inner], nz)
    mixed_all = jnp.concatenate(ordered(everyone(result.astype(BF), "tp"), z), axis=0)
    mixed = reordered(mixed_all, nf, nc, nx)

    def scattered(parts):
        count = len(parts)
        stacked = jnp.stack([p.reshape(nz * nf * nc, nx * feat, hs) for p in parts], axis=1)
        done = lax.psum_scatter(
            stacked.reshape(nz * nf * nc * count * nx * feat, hs),
            ("tp", "fsdp", "cc"), scatter_dimension=0, tiled=True,
        ).reshape(count, nx, feat, hs)
        piece = lambda k: lax.dynamic_index_in_dim(done, x ^ k, 1, keepdims=False)
        pieces = [piece(0)] + [swap(piece(k), "cx", k) for k in range(1, nx)]
        whole = jnp.concatenate(ordered(pieces, x), axis=2).astype(F32)
        return [whole[i] for i in range(count)]

    (shard_down_t,) = scattered([part_down])
    grad_gate, grad_up, gh_own, gh_send = ffn_backward(grad_ffn, ffn_weights, slope, act, share)
    part_gate, part_up = weight_grad(hidden_f, [grad_gate, grad_up], nz)
    shard_gate, shard_up = scattered([part_gate, part_up])

    grad_hidden_f = returned(gh_own, gh_send)
    part_gain_mlp = jnp.sum(grad_hidden_f * normed_f, axis=0)
    grad_mid = grad_out + norm_back(grad_hidden_f, normed_f, scale_f, gain_mlp)
    grad_attn = grad_mid.astype(BF)
    g_att = dot(out_weights, grad_attn, 0, 1).astype(BF).reshape(nz, q_cols, share)
    g_parts = [g_att[0]] + [swap(g_att[k], "tp", k) for k in range(1, nz)]
    grad_heads = jnp.concatenate(ordered(g_parts, z), axis=1)
    part_out = dot(grad_attn, att_t, 0, 1).astype(BF)

    dq, dk, dv = attn_bwd(
        q_rot, k_all, v_all, doc_start, query_place,
        make_bounds(doc_start, first_row, rows, BWD_TQ, BWD_TK), grad_heads, o_f, lse, BWD_TQ, BWD_TK,
    )
    kv_grad = jnp.concatenate([dk, dv], axis=0).reshape(2 * kv_cols, nx, nc, rows)
    kv_grad = summed(kv_grad, 2, "cc", c).astype(BF)
    kv_grad = summed(kv_grad, 1, "cx", x)
    gk = turned(kv_grad[:kv_cols].reshape(heads_k, HD, rows) * att_scale, cos_table, -sin_table)
    gq = turned(dq.reshape(-1, HD, rows) * att_scale, cos_table, -sin_table)
    grad_qkv = jnp.concatenate(
        [gq.reshape(q_cols, rows), gk.reshape(kv_cols, rows), kv_grad[kv_cols:]], axis=0
    ).astype(BF)
    part_h1 = dot(grad_qkv, w_qkv, 0, 1).astype(BF).reshape(nz, share, width)
    part_qkv = dot(hidden_a, grad_qkv, 0, 1).astype(BF)
    grad_hidden_a = summed(part_h1, 0, "tp", z)
    normed_share = own_rows(normed_a)
    part_gain_att = jnp.sum(grad_hidden_a * normed_share, axis=0)
    grad_share = grad_mid + norm_back(grad_hidden_a, normed_share, own_rows(scale_a), gain_att)
    grad_all = jnp.concatenate(ordered(everyone(grad_share.astype(BF), "tp"), z), axis=0)
    grad_tokens = reordered(grad_all, nf, nc, nx).astype(F32)

    small = jnp.stack([part_gain_att, part_gain_mlp, jnp.broadcast_to(loss_part, (width,))])
    for axis in AXES:
        step = 1
        while step < lax.axis_size(axis):
            small = small + swap(small, axis, step)
            step *= 2
    small_own = lax.dynamic_slice_in_dim(small[:2], ((y * nc + c) * nx + x) * feat, feat, 1)
    loss = small[2, 0] / (valid_count.astype(F32) * width)

    shard_qkv = scatter_rows(part_qkv)
    shard_out_t = scatter_rows(part_out)
    shard_out_t = summed(
        shard_out_t.astype(BF).reshape(feat, nz, q_cols), 1, "tp", 0
    )
    return (
        mixed[None],
        loss,
        grad_tokens[None],
        small_own[0],
        shard_qkv[:, :q_cols],
        shard_qkv[:, q_cols : q_cols + kv_cols],
        shard_qkv[:, q_cols + kv_cols :],
        shard_out_t.T,
        small_own[1],
        shard_gate,
        shard_up,
        shard_down_t.T,
    )


FWD_TQ, FWD_TK = 256, 1024
BWD_TQ, BWD_TK = 256, 512


def solution(mesh):
    nf, nctx, nz = (mesh.shape[a] for a in ("fsdp", "ctx", "tp"))
    nc = 2 if nctx % 2 == 0 else 1
    fine = Mesh(mesh.devices.reshape(nf, nctx // nc, nc, nz), AXES)
    ctx = ("cx", "cc")
    rows = ("fsdp", "cx", "cc")
    return jax.shard_map(
        on_device,
        mesh=fine,
        in_specs=(
            P("fsdp", ctx, None),
            P("fsdp", ctx, None),
            P("fsdp", ctx),
            P("fsdp", ctx),
            P("fsdp", ctx),
            P(),
            P(rows),
            P(rows, "tp"),
            P(rows, "tp"),
            P(rows, "tp"),
            P("tp", rows),
            P(rows),
            P(rows, "tp"),
            P(rows, "tp"),
            P("tp", rows),
        ),
        out_specs=(
            P("fsdp", ctx, None),
            P(),
            P("fsdp", ctx, None),
            P(rows),
            P(rows, "tp"),
            P(rows, "tp"),
            P(rows, "tp"),
            P("tp", rows),
            P(rows),
            P(rows, "tp"),
            P(rows, "tp"),
            P("tp", rows),
        ),
        check_vma=False,
    )
```

```python
import functools
import math

import jax
import jax.numpy as jnp
from jax import lax
from jax.experimental import pallas as pl
from jax.experimental.pallas import tpu as pltpu
from jax.sharding import Mesh
from jax.sharding import PartitionSpec as P

HD=96
NEG=-1e30
F32=jnp.float32; BF=jnp.bfloat16
def dot(a,b,ca,cb):
    return lax.dot_general(a,b,(((ca,),(cb,)),((),())),preferred_element_type=F32)

def load_blocks(place, sources, keys_t, keys, values_t, values):
    n = 0
    for source in sources:
        width = source.shape[3]
        for b in range(source.shape[0]):
            at = pl.ds(pl.multiple_of(place[n]*width, width), width)
            n += 1
            if keys_t is not None:
                keys_t[:, at] = source[b, 0]
            keys[at, :] = source[b, 0].astype(F32).T.astype(BF)
            if values_t is not None:
                values_t[:, at] = source[b, 1]
            if values is not None:
                values[at, :] = source[b, 1].astype(F32).T.astype(BF)

def fwd_kernel(scale2, tq, tk, group, count, bounds, place, q_ref, *refs):
    sources, (st_ref, qp_ref, o_ref, of_ref, lse_ref, ks, v_ref, m_s, l_s, acc) = refs[:count], refs[count:]
    i = pl.program_id(1)
    @pl.when(i == 0)
    def _():
        load_blocks(place, sources, None, ks, v_ref, None)
    q2 = jnp.concatenate([q_ref[h*HD:(h+1)*HD, :] for h in range(group)], axis=1)
    st = jnp.concatenate([st_ref[...]]*group, axis=1)
    qp = jnp.concatenate([qp_ref[...]]*group, axis=1)
    m_s[...] = jnp.full_like(m_s, NEG)
    l_s[...] = jnp.zeros_like(l_s)
    acc[...] = jnp.zeros_like(acc)
    def step(masked, j, _):
        off = pl.multiple_of(j*tk, tk)
        s = dot(ks[pl.ds(off, tk), :], q2, 1, 0)
        if masked:
            kid = off + lax.broadcasted_iota(jnp.int32, s.shape, 0)
            s = jnp.where((kid >= st) & (kid <= qp), s, NEG)
        m_old = m_s[...]
        m_new = jnp.maximum(m_old, jnp.max(s, axis=0, keepdims=True))
        p = jnp.exp2((s - m_new)*scale2)
        al = jnp.exp2((m_old - m_new)*scale2)
        l_s[...] = l_s[...]*al + jnp.sum(p, axis=0, keepdims=True)
        m_s[...] = m_new
        acc[...] = acc[...]*al + dot(v_ref[:, pl.ds(off, tk)], p.astype(BF), 1, 0)
        return 0
    lo, a, b, hi = bounds[i,0], bounds[i,1], bounds[i,2], bounds[i,3]
    lax.fori_loop(lo, a, functools.partial(step, True), 0)
    lax.fori_loop(a, b, functools.partial(step, False), 0)
    lax.fori_loop(b, hi, functools.partial(step, True), 0)
    o = acc[...]/l_s[...]
    lse = m_s[...]*scale2 + jnp.log2(l_s[...])
    for h in range(group):
        oh = o[:, h*tq:(h+1)*tq]
        of_ref[h*HD:(h+1)*HD, :] = oh
        o_ref[h*HD:(h+1)*HD, :] = oh.astype(BF)
        lse_ref[0, h:h+1, :] = lse[:, h*tq:(h+1)*tq]

def kv_spec(source):
    return pl.BlockSpec((source.shape[0], 2, HD, source.shape[3]), lambda g,i,*_:(0,0,g,0))

def attn_fwd(qT, kv_sources, place, start, qpos, bounds, tq=256, tk=512):
    T = qT.shape[1]; kv = kv_sources[0].shape[2]//HD; group = qT.shape[0]//HD//kv
    N = sum(s.shape[0] for s in kv_sources)*T
    scale2 = HD**-0.5*math.log2(math.e)
    qs = pl.BlockSpec((group*HD, tq), lambda g,i,*_:(g,i))
    row = pl.BlockSpec((1, tq), lambda g,i,*_:(0,i))
    return pl.pallas_call(
        functools.partial(fwd_kernel, scale2, tq, tk, group, len(kv_sources)),
        out_shape=(jax.ShapeDtypeStruct(qT.shape, BF), jax.ShapeDtypeStruct(qT.shape, F32), jax.ShapeDtypeStruct((kv, group, T), F32)),
        grid_spec=pltpu.PrefetchScalarGridSpec(num_scalar_prefetch=2, grid=(kv, T//tq),
            in_specs=[qs] + [kv_spec(s) for s in kv_sources] + [row, row],
            out_specs=[qs, qs, pl.BlockSpec((1, group, tq), lambda g,i,*_:(g,0,i))],
            scratch_shapes=[pltpu.VMEM((N,HD),BF), pltpu.VMEM((HD,N),BF), pltpu.VMEM((1,group*tq),F32), pltpu.VMEM((1,group*tq),F32), pltpu.VMEM((HD,group*tq),F32)]),
        compiler_params=pltpu.CompilerParams(vmem_limit_bytes=48*2**20),
        cost_estimate=pl.CostEstimate(flops=24*10**9, bytes_accessed=8*10**6, transcendentals=0),
        name="attend",
    )(bounds, place, qT, *kv_sources, start, qpos)

def bwd_kernel(scale2, tq, tk, group, count, bounds, place, q_ref, *refs):
    sources, (st_ref, qp_ref, g_ref, of_ref, lse_ref, dq_ref) = refs[:count], refs[count:count+6]
    dkv_refs, (k_ref, ks, vs, dks, dvs, dqs) = refs[count+6:2*count+6], refs[2*count+6:]
    i = pl.program_id(1)
    @pl.when(i == 0)
    def _():
        load_blocks(place, sources, k_ref, ks, None, vs)
        dks[...] = jnp.zeros_like(dks)
        dvs[...] = jnp.zeros_like(dvs)
    cat = lambda f: jnp.concatenate([f(h) for h in range(group)], axis=1)
    q2 = cat(lambda h: q_ref[h*HD:(h+1)*HD, :])
    g2 = cat(lambda h: g_ref[h*HD:(h+1)*HD, :])
    lse = cat(lambda h: lse_ref[0, h:h+1, :])
    delta = cat(lambda h: jnp.sum(g_ref[h*HD:(h+1)*HD, :].astype(F32)*of_ref[h*HD:(h+1)*HD, :], axis=0, keepdims=True))
    st = cat(lambda h: st_ref[...])
    qp = cat(lambda h: qp_ref[...])
    dqs[...] = jnp.zeros_like(dqs)
    def step(masked, j, _):
        off = pl.multiple_of(j*tk, tk)
        s = dot(ks[pl.ds(off, tk), :], q2, 1, 0)
        if masked:
            kid = off + lax.broadcasted_iota(jnp.int32, s.shape, 0)
            s = jnp.where((kid >= st) & (kid <= qp), s, NEG)
        p = jnp.exp2(s*scale2 - lse)
        dp = dot(vs[pl.ds(off, tk), :], g2, 1, 0)
        ds = (p*(dp - delta)).astype(BF)
        dvs[:, pl.ds(off, tk)] += dot(g2, p.astype(BF), 1, 1)
        dks[:, pl.ds(off, tk)] += dot(q2, ds, 1, 1)
        dqs[...] += dot(k_ref[:, pl.ds(off, tk)], ds, 1, 0)
        return 0
    lo, a, b, hi = bounds[i,0], bounds[i,1], bounds[i,2], bounds[i,3]
    lax.fori_loop(lo, a, functools.partial(step, True), 0)
    lax.fori_loop(a, b, functools.partial(step, False), 0)
    lax.fori_loop(b, hi, functools.partial(step, True), 0)
    for h in range(group):
        dq_ref[h*HD:(h+1)*HD, :] = dqs[:, h*tq:(h+1)*tq]
    @pl.when(i == pl.num_programs(1)-1)
    def _():
        n = 0
        for dkv_ref in dkv_refs:
            width = dkv_ref.shape[3]
            for b in range(dkv_ref.shape[0]):
                at = pl.ds(pl.multiple_of(place[n]*width, width), width)
                n += 1
                dkv_ref[b, 0] = dks[:, at].astype(BF)
                dkv_ref[b, 1] = dvs[:, at].astype(BF)

def attn_bwd(qT, kv_sources, place, start, qpos, bounds, gT, of, lse, tq, tk, head):
    T = qT.shape[1]; kv = kv_sources[0].shape[2]//HD; group = qT.shape[0]//HD//kv
    N = sum(s.shape[0] for s in kv_sources)*T
    scale2 = HD**-0.5*math.log2(math.e)
    qs = pl.BlockSpec((group*HD, tq), lambda g,i,*_:(head,i))
    row = pl.BlockSpec((1, tq), lambda g,i,*_:(0,i))
    kv_in = [pl.BlockSpec((s.shape[0], 2, HD, T), lambda g,i,*_:(0,0,head,0)) for s in kv_sources]
    kv_out = [pl.BlockSpec((s.shape[0], 2, HD, T), lambda g,i,*_:(0,0,0,0)) for s in kv_sources]
    return pl.pallas_call(
        functools.partial(bwd_kernel, scale2, tq, tk, group, len(kv_sources)),
        out_shape=[jax.ShapeDtypeStruct((group*HD, T), F32)] + [jax.ShapeDtypeStruct((s.shape[0], 2, HD, T), BF) for s in kv_sources],
        grid_spec=pltpu.PrefetchScalarGridSpec(num_scalar_prefetch=2, grid=(1, T//tq),
            in_specs=[qs] + kv_in + [row, row, qs, qs, pl.BlockSpec((1, group, tq), lambda g,i,*_:(head,0,i))],
            out_specs=[pl.BlockSpec((group*HD, tq), lambda g,i,*_:(0,i))] + kv_out,
            scratch_shapes=[pltpu.VMEM((HD,N),BF), pltpu.VMEM((N,HD),BF), pltpu.VMEM((N,HD),BF), pltpu.VMEM((HD,N),F32), pltpu.VMEM((HD,N),F32), pltpu.VMEM((HD,group*tq),F32)]),
        compiler_params=pltpu.CompilerParams(vmem_limit_bytes=56*2**20),
        cost_estimate=pl.CostEstimate(flops=24*10**9, bytes_accessed=8*10**6, transcendentals=0),
        name="attend_back",
    )(bounds, place, qT, *kv_sources, start, qpos, gT, of, lse)

def make_bounds(start, q_first, T, tq, tk):
    s = start.reshape(-1, tq)
    first = q_first + jnp.arange(T//tq, dtype=jnp.int32)*tq
    lo = s[:,0]//tk
    hi = (first + tq - 1)//tk + 1
    a = jnp.minimum((s[:,-1] + tk - 1)//tk, hi)
    b = jnp.maximum(first//tk, a)
    return jnp.stack([lo,a,b,hi],axis=1).astype(jnp.int32)

EPSILON = 1e-05
ROPE_BASE = 100000.0
AXES = ("fsdp", "cx", "cc", "tp")


def swap(values, axis, step=1):
    size = lax.axis_size(axis)
    return lax.ppermute(values, axis, [(i, i ^ step) for i in range(size)])


def after_kernel(*refs):
    pass


def after(values, *others):
    values, tree = jax.tree.flatten(values)
    others = jax.tree.leaves(others)
    done = pl.pallas_call(
        after_kernel,
        out_shape=[jax.ShapeDtypeStruct(v.shape, v.dtype) for v in values],
        in_specs=[pl.BlockSpec(memory_space=pl.ANY)] * (len(values) + len(others)),
        out_specs=[pl.BlockSpec(memory_space=pl.ANY)] * len(values),
        input_output_aliases={i: i for i in range(len(values))},
        name="after",
    )(*values, *others)
    return jax.tree.unflatten(tree, list(done))


def ordered(parts, index):
    if len(parts) == 1:
        return list(parts)
    if len(parts) == 2:
        first = index == 0
        return [jnp.where(first, parts[0], parts[1]), jnp.where(first, parts[1], parts[0])]
    stacked = jnp.stack(parts)
    return [
        lax.dynamic_index_in_dim(stacked, jnp.bitwise_xor(index, a), 0, keepdims=False)
        for a in range(len(parts))
    ]


def everyone(values, axis):
    return [values] + [swap(values, axis, k) for k in range(1, lax.axis_size(axis))]


def place_kernel(counts, place, *refs):
    sources, outs = refs[: len(counts)], refs[len(counts) :]
    n = pl.program_id(0)
    first = 0
    for count, source in zip(counts, sources):

        @pl.when((n >= first) & (n < first + count))
        def _(source=source):
            at = 0
            for out in outs:
                out[...] = source[:, at : at + out.shape[1]]
                at += out.shape[1]

        first += count


def put_blocks(sources, place, cut=None):
    counts = [s.shape[0] for s in sources]
    shape = sources[0].shape[1:]
    cuts = [shape[0]] if cut is None else [cut, shape[0] - cut]
    specs = []
    first = 0
    for count in counts:
        specs.append(
            pl.BlockSpec(
                (1,) + shape,
                lambda n, place, first=first, count=count: (jnp.clip(n - first, 0, count - 1), 0, 0),
            )
        )
        first += count
    return pl.pallas_call(
        functools.partial(place_kernel, counts),
        out_shape=[jax.ShapeDtypeStruct((first, r, shape[1]), sources[0].dtype) for r in cuts],
        grid_spec=pltpu.PrefetchScalarGridSpec(
            num_scalar_prefetch=1,
            grid=(first,),
            in_specs=specs,
            out_specs=[
                pl.BlockSpec((1, r, shape[1]), lambda n, place: (place[n], 0, 0)) for r in cuts
            ],
        ),
        cost_estimate=pl.CostEstimate(flops=7*10**9, bytes_accessed=8*10**6, transcendentals=0),
        name="put_blocks",
    )(jnp.stack(place).astype(jnp.int32), *sources)


def gather_rows(shard, hold=None, hold_core=None, cut=None):
    rows, width = shard.shape
    nf, nx, nc = (lax.axis_size(a) for a in ("fsdp", "cx", "cc"))
    y, x, c = (lax.axis_index(a) for a in ("fsdp", "cx", "cc"))
    half = rows // 2
    if nf == 2 and nx == 2:
        from_x = swap(shard, "cx")
        from_y = swap(shard, "fsdp")
        x_parts = [shard, from_x]
        if hold is not None:
            from_x, from_y = after((from_x, from_y), hold)
        top = swap(from_y[:half], "cx")
        low = swap(from_x[half:], "fsdp")
        near = jnp.concatenate([shard, from_x, from_y, top, low], axis=0)
    else:
        x_parts = everyone(shard, "cx")
        near = jnp.concatenate(x_parts, axis=0)
        near = jnp.concatenate(everyone(near, "fsdp"), axis=0)
    parts = everyone(near, "cc")
    if hold_core is not None and nc > 1:
        parts[1:] = after(parts[1:], hold_core)
    sources = [v.reshape(nf * nx, rows, width) for v in parts]
    place = [
        ((y ^ dy) * nx + (x ^ dx)) * nc + (c ^ dc)
        for dc in range(nc)
        for dy in range(nf)
        for dx in range(nx)
    ]
    return put_blocks(sources, place, cut), near, x_parts


def scatter_rows(part):
    nf, nx, nc = (lax.axis_size(a) for a in ("fsdp", "cx", "cc"))
    y, x, c = (lax.axis_index(a) for a in ("fsdp", "cx", "cc"))
    width = part.shape[1]
    total = part.reshape(nf, nx, nc, -1, width)
    total = summed(total, 2, "cc", c)
    total = summed(total.astype(jnp.bfloat16), 0, "fsdp", y)
    total = summed(total.astype(jnp.bfloat16), 0, "cx", x)
    return total


def summed(part, dim, axis, index):
    take = lambda k: lax.dynamic_index_in_dim(part, index ^ k, dim, keepdims=False)
    total = take(0).astype(jnp.float32)
    for k in range(1, lax.axis_size(axis)):
        total = total + swap(take(k), axis, k).astype(jnp.float32)
    return total


def norm_parts(values):
    factor = lax.rsqrt(jnp.mean(values * values, axis=-1, keepdims=True) + EPSILON)
    return (factor, values * factor)


def norm_back(grad_normed_in, normed, factor, gain_vec):
    grad_normed = grad_normed_in * gain_vec
    return factor * (grad_normed - normed * jnp.mean(grad_normed * normed, axis=-1, keepdims=True))


def turned(values, cos_table, sin_table):
    half = values.shape[1] // 2
    low, high = values[:, :half], values[:, half:]
    return jnp.concatenate(
        [low * cos_table - high * sin_table, high * cos_table + low * sin_table], axis=1
    )


def whole_block(dims, ref):
    nf, nx, nc = dims
    feat = ref.shape[3] // nx
    return jnp.concatenate(
        [
            ref[0, f * nc + b, 0, a * feat : (a + 1) * feat, :]
            for f in range(nf)
            for a in range(nx)
            for b in range(nc)
        ],
        axis=0,
    )


def ffn_forward_kernel(dims, h_ref, wg_ref, wu_ref, wd_ref, slope_ref, act_ref, inner_ref, out_ref, acc):
    z = pl.program_id(0)
    hidden = h_ref[...]
    gate = dot(hidden, whole_block(dims, wg_ref), 1, 0)
    up = dot(hidden, whole_block(dims, wu_ref), 1, 0)
    sig = jax.nn.sigmoid(gate)
    act = gate * sig
    slope_ref[...] = up * (sig * (1.0 + gate * (1.0 - sig)))
    act_ref[...] = act
    inner = (act * up).astype(BF)
    inner_ref[...] = inner
    add_up(z, dot(inner, whole_block(dims, wd_ref), 1, 1), acc, out_ref)


def add_up(z, added, acc, out_ref):
    @pl.when(z == 0)
    def _():
        acc[...] = added

    @pl.when(z > 0)
    def _():
        acc[...] += added

    @pl.when(z == pl.num_programs(0) - 1)
    def _():
        out_ref[...] = acc[...].astype(out_ref.dtype)


def ffn_forward(hidden, weights, dims, kind):
    rows, width = hidden.shape
    nz, nb, _, nr, hs = weights.shape
    wspec = lambda m: pl.BlockSpec((1, nb, 1, nr, hs), lambda z: (z, 0, m, 0, 0))
    full = pl.BlockSpec((rows, width), lambda z: (0, 0))
    col = pl.BlockSpec((rows, hs), lambda z: (0, z))
    shape = jax.ShapeDtypeStruct
    return pl.pallas_call(
        functools.partial(ffn_forward_kernel, dims),
        out_shape=(
            shape((rows, nz * hs), F32),
            shape((rows, nz * hs), F32),
            shape((rows, nz * hs), BF),
            shape((rows, width), kind),
        ),
        grid=(nz,),
        in_specs=[full, wspec(0), wspec(1), wspec(2)],
        out_specs=[col, col, col, full],
        scratch_shapes=[pltpu.VMEM((rows, width), F32)],
        compiler_params=pltpu.CompilerParams(vmem_limit_bytes=56 * 2**20),
        cost_estimate=pl.CostEstimate(flops=12*10**9, bytes_accessed=8*10**6, transcendentals=0),
        name="feed_forward",
    )(hidden, weights, weights, weights)


def ffn_backward_kernel(dims, g_ref, wg_ref, wu_ref, wd_ref, slope_ref, act_ref, gg_ref, gu_ref, out_ref, acc):
    z = pl.program_id(0)
    grad_inner = dot(g_ref[...], whole_block(dims, wd_ref), 1, 0)
    gg = (grad_inner * slope_ref[...]).astype(BF)
    gu = (grad_inner * act_ref[...]).astype(BF)
    gg_ref[...] = gg
    gu_ref[...] = gu
    added = dot(gg, whole_block(dims, wg_ref), 1, 1) + dot(gu, whole_block(dims, wu_ref), 1, 1)
    add_up(z, added, acc, out_ref)


def ffn_backward(grad, weights, slope, act, dims, kind):
    rows, width = grad.shape
    nz, nb, _, nr, hs = weights.shape
    wspec = lambda m: pl.BlockSpec((1, nb, 1, nr, hs), lambda z: (z, 0, m, 0, 0))
    full = pl.BlockSpec((rows, width), lambda z: (0, 0))
    col = pl.BlockSpec((rows, hs), lambda z: (0, z))
    shape = jax.ShapeDtypeStruct
    return pl.pallas_call(
        functools.partial(ffn_backward_kernel, dims),
        out_shape=(
            shape((rows, nz * hs), BF),
            shape((rows, nz * hs), BF),
            shape((rows, width), kind),
        ),
        grid=(nz,),
        in_specs=[full, wspec(0), wspec(1), wspec(2), col, col],
        out_specs=[col, col, full],
        scratch_shapes=[pltpu.VMEM((rows, width), F32)],
        compiler_params=pltpu.CompilerParams(vmem_limit_bytes=56 * 2**20),
        cost_estimate=pl.CostEstimate(flops=12*10**9, bytes_accessed=8*10**6, transcendentals=0),
        name="feed_forward_back",
    )(grad, weights, weights, weights, slope, act)


def input_grad_kernel(dims, place, gq_ref, gkv_ref, w_ref, out_ref):
    nf, nx, nc = dims
    feat = w_ref.shape[2] // nx
    grads = jnp.concatenate([gq_ref[0], gkv_ref[0]], axis=0).astype(F32).T.astype(BF)
    weight = jnp.concatenate(
        [
            w_ref[0, f * nc + b, a * feat : (a + 1) * feat, :]
            for f in range(nf)
            for a in range(nx)
            for b in range(nc)
        ],
        axis=0,
    )
    added = dot(grads, weight, 1, 1)

    @pl.when(pl.program_id(0) == 0)
    def _():
        out_ref[...] = added

    @pl.when(pl.program_id(0) > 0)
    def _():
        out_ref[...] += added


def input_grad(gq, gkv, weights, place, dims):
    nz, q_cols, share = gq.shape
    nb, nr, cols = weights.shape[1:]
    width = nb * nr
    return pl.pallas_call(
        functools.partial(input_grad_kernel, dims),
        out_shape=jax.ShapeDtypeStruct((share, width), F32),
        grid_spec=pltpu.PrefetchScalarGridSpec(
            num_scalar_prefetch=1,
            grid=(nz,),
            in_specs=[
                pl.BlockSpec((1, q_cols, share), lambda k, place: (k, 0, 0)),
                pl.BlockSpec((1, gkv.shape[1], share), lambda k, place: (k, 0, 0)),
                pl.BlockSpec((1, nb, nr, cols), lambda k, place: (place[k], 0, 0, 0)),
            ],
            out_specs=pl.BlockSpec((share, width), lambda k, place: (0, 0)),
        ),
        compiler_params=pltpu.CompilerParams(vmem_limit_bytes=56 * 2**20),
        cost_estimate=pl.CostEstimate(flops=9*10**9, bytes_accessed=8*10**6, transcendentals=0),
        name="input_grad",
    )(place, gq, gkv, weights)


def weight_grad_kernel(dims, pieces, count, where, *refs):
    nf, nx, nc = dims
    lefts, rights = refs[:pieces], refs[pieces : pieces * (count + 1)]
    outs, (plain, flipped) = refs[pieces * (count + 1) : -2], refs[-2:]
    feat = plain.shape[0] // (nf * nx * nc)
    tokens = lefts[0].shape[0]

    @pl.when(pl.program_id(0) == 0)
    def _():
        for p, left in enumerate(lefts):
            plain[:, p * tokens : (p + 1) * tokens] = left[...].astype(F32).T.astype(BF)
        n = 0
        for dc in range(nc):
            for dy in range(nf):
                for a in range(nx):
                    row = ((where[0] ^ dy) * nx + a) * nc + (where[1] ^ dc)
                    flipped[n * feat : (n + 1) * feat, :] = plain[
                        pl.ds(pl.multiple_of(row * feat, feat), feat), :
                    ]
                    n += 1

    part = flipped.shape[0] // (nc * nf)
    for i in range(count):
        right = jnp.concatenate([rights[i * pieces + p][...] for p in range(pieces)], axis=0)
        done = dot(flipped[...], right, 1, 0).astype(BF)
        for b in range(nc):
            for f in range(nf):
                n = b * nf + f
                outs[i * nc + b][f, 0] = done[n * part : (n + 1) * part]


def weight_grad(lefts, rights, where, nz, dims):
    rows, width = lefts[0].shape
    nf, nx, nc = dims
    hs = rights[0][0].shape[1] // nz
    count, pieces = len(rights), len(lefts)
    shape = (nf, nz, width // (nf * nc), hs)
    return pl.pallas_call(
        functools.partial(weight_grad_kernel, dims, pieces, count),
        out_shape=(jax.ShapeDtypeStruct(shape, BF),) * (count * nc),
        grid_spec=pltpu.PrefetchScalarGridSpec(
            num_scalar_prefetch=1,
            grid=(nz,),
            in_specs=[pl.BlockSpec((rows, width), lambda z, w: (0, 0))] * pieces
            + [pl.BlockSpec((rows, hs), lambda z, w: (0, z))] * (count * pieces),
            out_specs=[pl.BlockSpec((nf, 1) + shape[2:], lambda z, w: (0, z, 0, 0))] * (count * nc),
            scratch_shapes=[pltpu.VMEM((width, rows * pieces), BF)] * 2,
        ),
        compiler_params=pltpu.CompilerParams(vmem_limit_bytes=56 * 2**20),
        cost_estimate=pl.CostEstimate(flops=10*10**9, bytes_accessed=8*10**6, transcendentals=0),
        name="weight_grad",
    )(where, *lefts, *[r for right in rights for r in right])


def on_device(
    tokens, teacher, segment_ids, positions, valid_mask, valid_count, gain_attn, w_query, w_key,
    w_value, w_out, gain_ffn, w_gate, w_up, w_down,
):
    nf, nx, nc, nz = (lax.axis_size(a) for a in AXES)
    y, x, c, z = (lax.axis_index(a) for a in AXES)
    place = x * nc + c
    rows, width = tokens.shape[1:]
    share = rows // nz
    feat = w_query.shape[0]
    q_cols, kv_cols = w_query.shape[1], w_key.shape[1]
    heads_k = kv_cols // HD
    hidden_dev = w_gate.shape[1]
    hs = hidden_dev // nx
    own_rows = lambda v: lax.dynamic_slice_in_dim(v, z * share, share, 0)
    att_scale = HD ** (-0.5)

    qkv_cols = q_cols + 2 * kv_cols
    gains = jnp.pad(jnp.stack([gain_attn, gain_ffn]), ((0, 14), (0, qkv_cols - feat)))
    in_shard = jnp.concatenate([jnp.concatenate([w_query, w_key, w_value], axis=1), gains], axis=0)
    rows_f = tokens[0].astype(F32)
    scale_a, normed_a = norm_parts(rows_f)
    out_shard = jnp.concatenate(everyone(w_out.T, "tp"), axis=1)
    (w_qkv, gain_rows), early, x_parts = gather_rows(in_shard, None, (scale_a, out_shard), feat)
    w_qkv = w_qkv.reshape(-1, qkv_cols)
    gain_rows = gain_rows[:, :2, :feat].astype(F32)
    gain_att, gain_mlp = (gain_rows[:, i].reshape(1, -1) for i in range(2))

    ffn_stack = after(jnp.stack([w_gate, w_up, w_down.T]), early)
    hidden_part = lambda k: lax.dynamic_slice_in_dim(ffn_stack, (x ^ k) * hs, hs, 2)
    pieces = [hidden_part(0)] + [swap(hidden_part(k), "cx", k) for k in range(1, nx)]
    swapped = pieces[1:]
    pieces[1:] = after(pieces[1:], w_qkv) if nx > 1 else []
    ffn_shard = jnp.stack(ordered(pieces, x), axis=1).reshape(3 * nx * feat, hs)
    ffn_weights = lax.all_gather(ffn_shard, ("tp", "fsdp", "cc"), axis=0, tiled=True)
    ffn_weights = ffn_weights.reshape(nz, nf * nc, 3, nx * feat, hs)

    half = HD // 2
    frequency = jnp.exp(
        jnp.arange(half).astype(F32) * (-2.0 * math.log(ROPE_BASE) / HD)
    )
    angles = frequency[:, None] * positions[0].astype(F32)[None]
    cos_table, sin_table = jnp.cos(angles)[None], jnp.sin(angles)[None]

    hidden_a = (normed_a * gain_att).astype(BF)
    kv_lin = dot(w_qkv[:, q_cols:], hidden_a, 0, 1)
    k_rot = turned(kv_lin[:kv_cols].reshape(heads_k, HD, rows), cos_table, sin_table)
    kv_own = jnp.concatenate([k_rot.reshape(kv_cols, rows), kv_lin[kv_cols:]], axis=0).astype(BF)
    q_lin = dot(w_qkv[:, :q_cols], hidden_a, 0, 1)
    q_rot = turned(q_lin.reshape(-1, HD, rows), cos_table, sin_table).reshape(q_cols, rows).astype(BF)
    kv_parts = everyone(kv_own.reshape(2, kv_cols, rows), "cx")

    seg_own = after(segment_ids[0][None], kv_own)
    seg_parts = everyone(seg_own, "cx")
    seg_near = jnp.concatenate(ordered(seg_parts, x), axis=0)
    seg_all = jnp.stack(ordered(everyone(seg_near, "cc"), c), axis=1).reshape(1, -1)
    doc_start = jnp.sum((seg_all < segment_ids[0][:, None]).astype(jnp.int32), axis=1)[None]
    query_place = place * rows + jnp.arange(rows, dtype=jnp.int32)[None]

    (out_weights,), out_near, out_parts = gather_rows(out_shard)
    out_weights = out_weights.reshape(width, -1)
    kv_parts[1:] = after(kv_parts[1:], q_rot, doc_start, out_parts) if nx > 1 else []
    q_rot = after(q_rot, out_near)
    kv_near = jnp.stack(kv_parts)
    kv_sources = everyone(kv_near, "cc")
    kv_place = jnp.stack(
        [(x ^ dx) * nc + (c ^ dc) for dc in range(nc) for dx in range(nx)]
    ).astype(jnp.int32)

    first_row = place * rows
    o_t, o_f, lse = attn_fwd(
        q_rot, kv_sources, kv_place, doc_start, query_place,
        make_bounds(doc_start, first_row, rows, FWD_TQ, FWD_TK), FWD_TQ, FWD_TK,
    )

    qkv_shard = jnp.concatenate(ordered([p[:feat] for p in x_parts], x), axis=0)
    qkv_weights = lax.all_gather(
        after(qkv_shard, o_t), ("tp", "fsdp", "cc"), axis=0, tiled=True
    ).reshape(nz, nf * nc, nx * feat, qkv_cols)

    chunk = lambda v, k: lax.dynamic_slice_in_dim(v, (z ^ k) * share, share, 1)
    att_t = jnp.concatenate(
        [chunk(o_t, 0)] + [swap(chunk(o_t, k), "tp", k) for k in range(1, nz)], axis=0
    )
    resid = own_rows(rows_f) + dot(att_t, out_weights, 0, 1)
    scale_f, normed_f = norm_parts(resid)
    hidden_own = (normed_f * gain_mlp).astype(BF)
    dims = (nf, nx, nc)
    hidden_parts = everyone(hidden_own, "cx")
    slopes, acts, inners, outs = zip(
        *(
            ffn_forward(h, ffn_weights, dims, F32 if k == 0 else BF)
            for k, h in enumerate(hidden_parts)
        )
    )

    def returned(parts, *others):
        total = parts[0]
        for k in range(1, nx):
            back = swap(parts[k], "cx", k)
            total = total + (after(back, *others) if others else back).astype(F32)
        return total

    result = resid + returned(outs)
    target = own_rows(teacher[0]).astype(F32)
    valid = own_rows(valid_mask[0].astype(F32)[:, None])
    error = result - target
    grad_out = valid * error
    loss_part = jnp.sum(grad_out * error)
    ffn_grads = everyone(grad_out.astype(BF), "cx")
    where = jnp.stack([y, c]).astype(jnp.int32)
    part_down = weight_grad(ffn_grads, [inners], where, nz, dims)
    mixed = lax.all_gather(result.astype(BF), "tp", axis=0, tiled=True)

    def to_rows(parts):
        others = [swap(parts[k], "cc", k) for k in range(1, nc)]

        def over_cores(f):
            total = parts[0][f].astype(F32)
            for other in others:
                total = total + other[f].astype(F32)
            return total

        return over_cores, [over_cores(k).astype(BF) for k in range(1, nf)]

    def scattered(over_cores, sends, hold):
        total = over_cores(0)
        for k in range(1, nf):
            total = total + after(swap(sends[k - 1], "fsdp", k), hold).astype(F32)
        total = total.astype(BF)
        return total, spread(total)

    def spread(total):
        done = lax.psum_scatter(
            total.reshape(nz * nx * feat, hs), "tp", scatter_dimension=0, tiled=True
        ).reshape(nx, feat, hs)
        piece = lambda k: lax.dynamic_index_in_dim(done, x ^ k, 0, keepdims=False)
        pieces = [piece(0)] + [swap(piece(k), "cx", k) for k in range(1, nx)]
        return jnp.concatenate(ordered(pieces, x), axis=1).astype(F32)

    down_own, down_sends = to_rows(part_down)
    grad_gates, grad_ups, ffn_backs = zip(
        *(
            ffn_backward(g, ffn_weights, slopes[k], acts[k], dims, F32 if k == 0 else BF)
            for k, g in enumerate(ffn_grads)
        )
    )
    part_gate_up = weight_grad(hidden_parts, [grad_gates, grad_ups], where, nz, dims)
    grad_hidden_f = returned(ffn_backs, part_down)
    part_gain_mlp = jnp.sum(grad_hidden_f * normed_f, axis=0)
    grad_mid = grad_out + norm_back(grad_hidden_f, normed_f, scale_f, gain_mlp)
    grad_attn = grad_mid.astype(BF)
    g_att = dot(out_weights, grad_attn, 0, 1).astype(BF).reshape(nz, q_cols, share)
    g_parts = [g_att[0]] + [swap(g_att[k], "tp", k) for k in range(1, nz)]
    grad_heads = jnp.concatenate(ordered(after(g_parts, part_gate_up, down_sends), z), axis=1)

    bounds = make_bounds(doc_start, first_row, rows, BWD_TQ, BWD_TK)
    dqs, kv_grads = [], []
    for head in range(heads_k):
        dq, *dkv = attn_bwd(
            q_rot, kv_sources, kv_place, doc_start, query_place, bounds, grad_heads, o_f, lse,
            BWD_TQ, BWD_TK, head,
        )
        dkv_others = [swap(dkv[k], "cc", k) for k in range(1, nc)]

        def kv_over_cores(k):
            total = dkv[0][k].astype(F32)
            for other in dkv_others:
                total = total + other[k].astype(F32)
            return total

        sends = [kv_over_cores(k).astype(BF) for k in range(1, nx)]
        if head == 0:
            down_total, shard_down_t = scattered(down_own, down_sends, dq)
            gate_own, gate_sends = to_rows(part_gate_up[:nc])
            up_own, up_sends = to_rows(part_gate_up[nc:])
            if heads_k > 1:
                grad_heads = after(grad_heads, sends, down_total, gate_sends, up_sends)
        kv_grad = kv_over_cores(0)
        for k in range(1, nx):
            kv_grad = kv_grad + swap(sends[k - 1], "cx", k).astype(F32)
        dqs.append(dq)
        kv_grads.append(kv_grad)
    gq = jnp.concatenate([turned(d.reshape(-1, HD, rows) * att_scale, cos_table, -sin_table) for d in dqs])
    gq = gq.reshape(q_cols, rows).astype(BF)
    to_owners = lambda v: jnp.stack(
        [chunk(v, 0)] + [swap(chunk(v, k), "tp", k) for k in range(1, nz)]
    )
    gq_all = to_owners(gq)
    kv_grad = jnp.stack(kv_grads, axis=1)
    gk = turned(kv_grad[0] * att_scale, cos_table, -sin_table)
    gkv = jnp.concatenate([gk, kv_grad[1]], axis=0).reshape(2 * kv_cols, rows).astype(BF)
    gkv_all = to_owners(gkv)
    grad_hidden_a = input_grad(
        gq_all, gkv_all, qkv_weights, jnp.stack([z ^ k for k in range(nz)]).astype(jnp.int32), dims
    )
    gate_total, shard_gate = scattered(gate_own, gate_sends, gkv)
    up_total, shard_up = scattered(up_own, up_sends, gkv)
    part_qkv = dot(hidden_a, jnp.concatenate([gq, gkv], axis=0), 0, 1).astype(BF)
    part_out = dot(after(grad_attn, gkv), att_t, 0, 1).astype(BF)
    normed_share = own_rows(normed_a)
    part_gain_att = jnp.sum(grad_hidden_a * normed_share, axis=0)
    grad_share = grad_mid + norm_back(grad_hidden_a, normed_share, own_rows(scale_a), gain_att)
    grad_tokens = lax.all_gather(grad_share.astype(BF), "tp", axis=0, tiled=True)

    small = jnp.stack([part_gain_att, part_gain_mlp, jnp.broadcast_to(loss_part, (width,))])
    for axis in AXES:
        step = 1
        while step < lax.axis_size(axis):
            small = small + swap(small, axis, step)
            step *= 2
    small_own = lax.dynamic_slice_in_dim(small[:2], ((y * nx + x) * nc + c) * feat, feat, 1)
    loss = small[2, 0] / (valid_count.astype(F32) * width)

    shard_qkv = scatter_rows(part_qkv)
    shard_out_t = scatter_rows(part_out)
    shard_out_t = summed(
        shard_out_t.astype(BF).reshape(feat, nz, q_cols), 1, "tp", 0
    )
    grad_tokens = after(
        grad_tokens, small_own, shard_qkv, shard_out_t, shard_gate, shard_up, shard_down_t
    ).astype(F32)
    return (
        mixed[None],
        loss,
        grad_tokens[None],
        small_own[0],
        shard_qkv[:, :q_cols],
        shard_qkv[:, q_cols : q_cols + kv_cols],
        shard_qkv[:, q_cols + kv_cols :],
        shard_out_t.T,
        small_own[1],
        shard_gate,
        shard_up,
        shard_down_t.T,
    )


FWD_TQ, FWD_TK = 256, 1024
BWD_TQ, BWD_TK = 256, 512


def solution(mesh):
    nf, nctx, nz = (mesh.shape[a] for a in ("fsdp", "ctx", "tp"))
    nc = 2 if nctx % 2 == 0 else 1
    fine = Mesh(mesh.devices.reshape(nf, nctx // nc, nc, nz), AXES)
    ctx = ("cx", "cc")
    rows = ("fsdp", "cx", "cc")
    return jax.shard_map(
        on_device,
        mesh=fine,
        in_specs=(
            P("fsdp", ctx, None),
            P("fsdp", ctx, None),
            P("fsdp", ctx),
            P("fsdp", ctx),
            P("fsdp", ctx),
            P(),
            P(rows),
            P(rows, "tp"),
            P(rows, "tp"),
            P(rows, "tp"),
            P("tp", rows),
            P(rows),
            P(rows, "tp"),
            P(rows, "tp"),
            P("tp", rows),
        ),
        out_specs=(
            P("fsdp", ctx, None),
            P(),
            P("fsdp", ctx, None),
            P(rows),
            P(rows, "tp"),
            P(rows, "tp"),
            P(rows, "tp"),
            P("tp", rows),
            P(rows),
            P(rows, "tp"),
            P(rows, "tp"),
            P("tp", rows),
        ),
        check_vma=False,
    )
```

```python
import functools
import math

import jax
import jax.numpy as jnp
from jax import lax
from jax.experimental import pallas as pl
from jax.experimental.pallas import tpu as pltpu
from jax.sharding import Mesh
from jax.sharding import PartitionSpec as P

HD=96
NO_COST = pl.CostEstimate(flops=0, bytes_accessed=0, transcendentals=0)


def about(us):
    return pl.CostEstimate(flops=us*10**9, bytes_accessed=10**6, transcendentals=0)
NEG=-1e30
F32=jnp.float32; BF=jnp.bfloat16
def dot(a,b,ca,cb):
    return lax.dot_general(a,b,(((ca,),(cb,)),((),())),preferred_element_type=F32)

def load_blocks(place, sources, keys_t, keys, values_t, values):
    n = 0
    for source in sources:
        width = source.shape[3]
        for b in range(source.shape[0]):
            at = pl.ds(pl.multiple_of(place[n]*width, width), width)
            n += 1
            if keys_t is not None:
                keys_t[:, at] = source[b, 0]
            keys[at, :] = source[b, 0].astype(F32).T.astype(BF)
            if values_t is not None:
                values_t[:, at] = source[b, 1]
            if values is not None:
                values[at, :] = source[b, 1].astype(F32).T.astype(BF)

def fwd_kernel(scale2, tq, tk, group, count, bounds, place, q_ref, *refs):
    sources, (st_ref, qp_ref, o_ref, of_ref, lse_ref, ks, v_ref, m_s, l_s, acc) = refs[:count], refs[count:]
    i = pl.program_id(1)
    @pl.when(i == 0)
    def _():
        load_blocks(place, sources, None, ks, v_ref, None)
    q2 = jnp.concatenate([q_ref[h*HD:(h+1)*HD, :] for h in range(group)], axis=1)
    st = jnp.concatenate([st_ref[...]]*group, axis=1)
    qp = jnp.concatenate([qp_ref[...]]*group, axis=1)
    m_s[...] = jnp.full_like(m_s, NEG)
    l_s[...] = jnp.zeros_like(l_s)
    acc[...] = jnp.zeros_like(acc)
    def step(masked, j, _):
        off = pl.multiple_of(j*tk, tk)
        s = dot(ks[pl.ds(off, tk), :], q2, 1, 0)
        if masked:
            kid = off + lax.broadcasted_iota(jnp.int32, s.shape, 0)
            s = jnp.where((kid >= st) & (kid <= qp), s, NEG)
        m_old = m_s[...]
        m_new = jnp.maximum(m_old, jnp.max(s, axis=0, keepdims=True))
        p = jnp.exp2((s - m_new)*scale2)
        al = jnp.exp2((m_old - m_new)*scale2)
        l_s[...] = l_s[...]*al + jnp.sum(p, axis=0, keepdims=True)
        m_s[...] = m_new
        acc[...] = acc[...]*al + dot(v_ref[:, pl.ds(off, tk)], p.astype(BF), 1, 0)
        return 0
    lo, a, b, hi = bounds[i,0], bounds[i,1], bounds[i,2], bounds[i,3]
    lax.fori_loop(lo, a, functools.partial(step, True), 0)
    lax.fori_loop(a, b, functools.partial(step, False), 0)
    lax.fori_loop(b, hi, functools.partial(step, True), 0)
    o = acc[...]/l_s[...]
    lse = m_s[...]*scale2 + jnp.log2(l_s[...])
    for h in range(group):
        oh = o[:, h*tq:(h+1)*tq]
        of_ref[h*HD:(h+1)*HD, :] = oh
        o_ref[h*HD:(h+1)*HD, :] = oh.astype(BF)
        lse_ref[0, h:h+1, :] = lse[:, h*tq:(h+1)*tq]

def kv_spec(source):
    return pl.BlockSpec((source.shape[0], 2, HD, source.shape[3]), lambda g,i,*_:(0,0,g,0))

def attn_fwd(qT, kv_sources, place, start, qpos, bounds, tq=256, tk=512):
    T = qT.shape[1]; kv = kv_sources[0].shape[2]//HD; group = qT.shape[0]//HD//kv
    N = sum(s.shape[0] for s in kv_sources)*T
    scale2 = HD**-0.5*math.log2(math.e)
    qs = pl.BlockSpec((group*HD, tq), lambda g,i,*_:(g,i))
    row = pl.BlockSpec((1, tq), lambda g,i,*_:(0,i))
    return pl.pallas_call(
        functools.partial(fwd_kernel, scale2, tq, tk, group, len(kv_sources)),
        out_shape=(jax.ShapeDtypeStruct(qT.shape, BF), jax.ShapeDtypeStruct(qT.shape, F32), jax.ShapeDtypeStruct((kv, group, T), F32)),
        grid_spec=pltpu.PrefetchScalarGridSpec(num_scalar_prefetch=2, grid=(kv, T//tq),
            in_specs=[qs] + [kv_spec(s) for s in kv_sources] + [row, row],
            out_specs=[qs, qs, pl.BlockSpec((1, group, tq), lambda g,i,*_:(g,0,i))],
            scratch_shapes=[pltpu.VMEM((N,HD),BF), pltpu.VMEM((HD,N),BF), pltpu.VMEM((1,group*tq),F32), pltpu.VMEM((1,group*tq),F32), pltpu.VMEM((HD,group*tq),F32)]),
        compiler_params=pltpu.CompilerParams(vmem_limit_bytes=48*2**20),
        cost_estimate=about(12),
        name="attend",
    )(bounds, place, qT, *kv_sources, start, qpos)

def bwd_kernel(scale2, tq, tk, group, count, bounds, place, q_ref, *refs):
    sources, (st_ref, qp_ref, g_ref, of_ref, lse_ref, dq_ref) = refs[:count], refs[count:count+6]
    dkv_refs, (k_ref, ks, vs, dks, dvs, dqs) = refs[count+6:2*count+6], refs[2*count+6:]
    i = pl.program_id(1)
    @pl.when(i == 0)
    def _():
        load_blocks(place, sources, k_ref, ks, None, vs)
        dks[...] = jnp.zeros_like(dks)
        dvs[...] = jnp.zeros_like(dvs)
    cat = lambda f: jnp.concatenate([f(h) for h in range(group)], axis=1)
    q2 = cat(lambda h: q_ref[h*HD:(h+1)*HD, :])
    g2 = cat(lambda h: g_ref[h*HD:(h+1)*HD, :])
    lse = cat(lambda h: lse_ref[0, h:h+1, :])
    delta = cat(lambda h: jnp.sum(g_ref[h*HD:(h+1)*HD, :].astype(F32)*of_ref[h*HD:(h+1)*HD, :], axis=0, keepdims=True))
    st = cat(lambda h: st_ref[...])
    qp = cat(lambda h: qp_ref[...])
    dqs[...] = jnp.zeros_like(dqs)
    def step(masked, j, _):
        off = pl.multiple_of(j*tk, tk)
        s = dot(ks[pl.ds(off, tk), :], q2, 1, 0)
        if masked:
            kid = off + lax.broadcasted_iota(jnp.int32, s.shape, 0)
            s = jnp.where((kid >= st) & (kid <= qp), s, NEG)
        p = jnp.exp2(s*scale2 - lse)
        dp = dot(vs[pl.ds(off, tk), :], g2, 1, 0)
        ds = (p*(dp - delta)).astype(BF)
        dvs[:, pl.ds(off, tk)] += dot(g2, p.astype(BF), 1, 1)
        dks[:, pl.ds(off, tk)] += dot(q2, ds, 1, 1)
        dqs[...] += dot(k_ref[:, pl.ds(off, tk)], ds, 1, 0)
        return 0
    lo, a, b, hi = bounds[i,0], bounds[i,1], bounds[i,2], bounds[i,3]
    lax.fori_loop(lo, a, functools.partial(step, True), 0)
    lax.fori_loop(a, b, functools.partial(step, False), 0)
    lax.fori_loop(b, hi, functools.partial(step, True), 0)
    for h in range(group):
        dq_ref[h*HD:(h+1)*HD, :] = dqs[:, h*tq:(h+1)*tq]
    @pl.when(i == pl.num_programs(1)-1)
    def _():
        n = 0
        for dkv_ref in dkv_refs:
            width = dkv_ref.shape[3]
            for b in range(dkv_ref.shape[0]):
                at = pl.ds(pl.multiple_of(place[n]*width, width), width)
                n += 1
                dkv_ref[b, 0] = dks[:, at].astype(BF)
                dkv_ref[b, 1] = dvs[:, at].astype(BF)

def attn_bwd(qT, kv_sources, place, start, qpos, bounds, gT, of, lse, tq, tk, head):
    T = qT.shape[1]; kv = kv_sources[0].shape[2]//HD; group = qT.shape[0]//HD//kv
    N = sum(s.shape[0] for s in kv_sources)*T
    scale2 = HD**-0.5*math.log2(math.e)
    qs = pl.BlockSpec((group*HD, tq), lambda g,i,*_:(head,i))
    row = pl.BlockSpec((1, tq), lambda g,i,*_:(0,i))
    kv_in = [pl.BlockSpec((s.shape[0], 2, HD, T), lambda g,i,*_:(0,0,head,0)) for s in kv_sources]
    kv_out = [pl.BlockSpec((s.shape[0], 2, HD, T), lambda g,i,*_:(0,0,0,0)) for s in kv_sources]
    return pl.pallas_call(
        functools.partial(bwd_kernel, scale2, tq, tk, group, len(kv_sources)),
        out_shape=[jax.ShapeDtypeStruct((group*HD, T), F32)] + [jax.ShapeDtypeStruct((s.shape[0], 2, HD, T), BF) for s in kv_sources],
        grid_spec=pltpu.PrefetchScalarGridSpec(num_scalar_prefetch=2, grid=(1, T//tq),
            in_specs=[qs] + kv_in + [row, row, qs, qs, pl.BlockSpec((1, group, tq), lambda g,i,*_:(head,0,i))],
            out_specs=[pl.BlockSpec((group*HD, tq), lambda g,i,*_:(0,i))] + kv_out,
            scratch_shapes=[pltpu.VMEM((HD,N),BF), pltpu.VMEM((N,HD),BF), pltpu.VMEM((N,HD),BF), pltpu.VMEM((HD,N),F32), pltpu.VMEM((HD,N),F32), pltpu.VMEM((HD,group*tq),F32)]),
        compiler_params=pltpu.CompilerParams(vmem_limit_bytes=56*2**20),
        cost_estimate=about(12),
        name="attend_back",
    )(bounds, place, qT, *kv_sources, start, qpos, gT, of, lse)

def make_bounds(start, q_first, T, tq, tk):
    s = start.reshape(-1, tq)
    first = q_first + jnp.arange(T//tq, dtype=jnp.int32)*tq
    lo = s[:,0]//tk
    hi = (first + tq - 1)//tk + 1
    a = jnp.minimum((s[:,-1] + tk - 1)//tk, hi)
    b = jnp.maximum(first//tk, a)
    return jnp.stack([lo,a,b,hi],axis=1).astype(jnp.int32)

EPSILON = 1e-05
ROPE_BASE = 100000.0
AXES = ("fsdp", "cx", "cc", "tp")


def swap(values, axis, step=1):
    size = lax.axis_size(axis)
    return lax.ppermute(values, axis, [(i, i ^ step) for i in range(size)])


def after_kernel(*refs):
    pass


def after(values, *others):
    values, tree = jax.tree.flatten(values)
    others = jax.tree.leaves(others)
    done = pl.pallas_call(
        after_kernel,
        out_shape=[jax.ShapeDtypeStruct(v.shape, v.dtype) for v in values],
        in_specs=[pl.BlockSpec(memory_space=pl.ANY)] * (len(values) + len(others)),
        out_specs=[pl.BlockSpec(memory_space=pl.ANY)] * len(values),
        input_output_aliases={i: i for i in range(len(values))},
        cost_estimate=NO_COST,
        name="after",
    )(*values, *others)
    return jax.tree.unflatten(tree, list(done))


def ordered(parts, index):
    if len(parts) == 1:
        return list(parts)
    if len(parts) == 2:
        first = index == 0
        return [jnp.where(first, parts[0], parts[1]), jnp.where(first, parts[1], parts[0])]
    stacked = jnp.stack(parts)
    return [
        lax.dynamic_index_in_dim(stacked, jnp.bitwise_xor(index, a), 0, keepdims=False)
        for a in range(len(parts))
    ]


def everyone(values, axis):
    return [values] + [swap(values, axis, k) for k in range(1, lax.axis_size(axis))]


def place_kernel(plan, count, place, *refs):
    sources, outs, sems = refs[:count], refs[count:-1], refs[-1]
    copies = [
        pltpu.make_async_copy(
            sources[source].at[pl.ds(first, n)], outs[out].at[place[spot], pl.ds(row, n)], sems.at[i]
        )
        for i, (source, first, n, out, spot, row) in enumerate(plan)
    ]
    for copy in copies:
        copy.start()
    for copy in copies:
        copy.wait()


def put_blocks(pieces, place, rows, cut=None):
    width, kind = pieces[0][0].shape[1], pieces[0][0].dtype
    cuts = [0, rows] if cut is None else [0, cut, rows]
    sources, plan = [], []
    for array, first, n, spot, row in pieces:
        known = [i for i, s in enumerate(sources) if s is array]
        if not known:
            known = [len(sources)]
            sources.append(array)
        for out, (low, high) in enumerate(zip(cuts[:-1], cuts[1:])):
            a, b = max(row, low), min(row + n, high)
            if a < b:
                plan.append((known[0], first + a - row, b - a, out, spot, a - low))
    return pl.pallas_call(
        functools.partial(place_kernel, plan, len(sources)),
        out_shape=[
            jax.ShapeDtypeStruct((len(place), b - a, width), kind) for a, b in zip(cuts[:-1], cuts[1:])
        ],
        in_specs=[pl.BlockSpec(memory_space=pltpu.SMEM)]
        + [pl.BlockSpec(memory_space=pltpu.VMEM)] * len(sources),
        out_specs=[pl.BlockSpec(memory_space=pl.ANY)] * (len(cuts) - 1),
        scratch_shapes=[pltpu.SemaphoreType.DMA((len(plan),))],
        compiler_params=pltpu.CompilerParams(vmem_limit_bytes=32 * 2**20),
        cost_estimate=about(2),
        name="put_blocks",
    )(jnp.stack(place).astype(jnp.int32), *sources)


def gather_rows(shard, hold_near=None, hold_core=None, cut=None, from_y=None, hold_x=None):
    rows, width = shard.shape
    nf, nx, nc = (lax.axis_size(a) for a in ("fsdp", "cx", "cc"))
    y, x, c = (lax.axis_index(a) for a in ("fsdp", "cx", "cc"))
    if nf == 2 and nx == 2:
        half = rows // 2 // 16 * 16
        from_x = swap(shard if hold_x is None else after(shard, hold_x), "cx")
        if from_y is None:
            from_y = swap(shard, "fsdp")
        top = swap(from_y[:half], "cx")
        low = swap(from_x[half:], "fsdp")
        x_parts = [shard, from_x]
        came = [from_x, from_y, top, low]
        if hold_near is not None:
            top, low = after((top, low), hold_near)
        own = [
            (shard, 0, rows, 0, 0),
            (from_x, 0, rows, 1, 0),
            (from_y, 0, rows, 2, 0),
            (top, 0, half, 3, 0),
            (low, 0, rows - half, 3, half),
        ]
    else:
        x_parts = everyone(shard, "cx")
        near = jnp.concatenate(x_parts, axis=0)
        near = jnp.concatenate(everyone(near, "fsdp"), axis=0)
        came = [near]
        own = [(near, i * rows, rows, i, 0) for i in range(nf * nx)]
    pieces = list(own)
    for k in range(1, nc):
        given = {}
        for array, first, n, spot, row in own:
            if id(array) not in given:
                given[id(array)] = swap(array, "cc", k)
                last = id(array)
        if hold_core is not None:
            given[last] = after(given[last], hold_core)
        pieces += [(given[id(a)], first, n, spot + k * nf * nx, row) for a, first, n, spot, row in own]
    place = [
        ((y ^ dy) * nx + (x ^ dx)) * nc + (c ^ dc)
        for dc in range(nc)
        for dy in range(nf)
        for dx in range(nx)
    ]
    return put_blocks(pieces, place, rows, cut), x_parts, came


def scatter_rows(part):
    nf, nx, nc = (lax.axis_size(a) for a in ("fsdp", "cx", "cc"))
    y, x, c = (lax.axis_index(a) for a in ("fsdp", "cx", "cc"))
    width = part.shape[1]
    total = part.reshape(nf, nx, nc, -1, width)
    on_chip = summed(total, 2, "cc", c).astype(jnp.bfloat16)
    on_y = summed(on_chip, 0, "fsdp", y).astype(jnp.bfloat16)
    total = summed(on_y, 0, "cx", x)
    return total, on_y


def summed(part, dim, axis, index):
    take = lambda k: lax.dynamic_index_in_dim(part, index ^ k, dim, keepdims=False)
    total = take(0).astype(jnp.float32)
    for k in range(1, lax.axis_size(axis)):
        total = total + swap(take(k), axis, k).astype(jnp.float32)
    return total


def norm_parts(values):
    factor = lax.rsqrt(jnp.mean(values * values, axis=-1, keepdims=True) + EPSILON)
    return (factor, values * factor)


def norm_back(grad_normed_in, normed, factor, gain_vec):
    grad_normed = grad_normed_in * gain_vec
    return factor * (grad_normed - normed * jnp.mean(grad_normed * normed, axis=-1, keepdims=True))


def turned(values, cos_table, sin_table):
    half = values.shape[1] // 2
    low, high = values[:, :half], values[:, half:]
    return jnp.concatenate(
        [low * cos_table - high * sin_table, high * cos_table + low * sin_table], axis=1
    )


def whole_block(dims, ref):
    nf, nx, nc = dims
    feat = ref.shape[3] // nx
    return jnp.concatenate(
        [
            ref[0, f * nc + b, 0, a * feat : (a + 1) * feat, :]
            for f in range(nf)
            for a in range(nx)
            for b in range(nc)
        ],
        axis=0,
    )


def ffn_forward_kernel(dims, h_ref, wg_ref, wu_ref, wd_ref, slope_ref, act_ref, inner_ref, out_ref, acc):
    z = pl.program_id(0)
    hidden = h_ref[...]
    gate = dot(hidden, whole_block(dims, wg_ref), 1, 0)
    up = dot(hidden, whole_block(dims, wu_ref), 1, 0)
    sig = jax.nn.sigmoid(gate)
    act = gate * sig
    slope_ref[...] = up * (sig * (1.0 + gate * (1.0 - sig)))
    act_ref[...] = act
    inner = (act * up).astype(BF)
    inner_ref[...] = inner
    add_up(z, dot(inner, whole_block(dims, wd_ref), 1, 1), acc, out_ref)


def add_up(z, added, acc, out_ref):
    @pl.when(z == 0)
    def _():
        acc[...] = added

    @pl.when(z > 0)
    def _():
        acc[...] += added

    @pl.when(z == pl.num_programs(0) - 1)
    def _():
        out_ref[...] = acc[...].astype(out_ref.dtype)


def ffn_forward(hidden, weights, dims, kind):
    rows, width = hidden.shape
    nz, nb, _, nr, hs = weights.shape
    wspec = lambda m: pl.BlockSpec((1, nb, 1, nr, hs), lambda z: (z, 0, m, 0, 0))
    full = pl.BlockSpec((rows, width), lambda z: (0, 0))
    col = pl.BlockSpec((rows, hs), lambda z: (0, z))
    shape = jax.ShapeDtypeStruct
    return pl.pallas_call(
        functools.partial(ffn_forward_kernel, dims),
        out_shape=(
            shape((rows, nz * hs), F32),
            shape((rows, nz * hs), F32),
            shape((rows, nz * hs), BF),
            shape((rows, width), kind),
        ),
        grid=(nz,),
        in_specs=[full, wspec(0), wspec(1), wspec(2)],
        out_specs=[col, col, col, full],
        scratch_shapes=[pltpu.VMEM((rows, width), F32)],
        compiler_params=pltpu.CompilerParams(vmem_limit_bytes=56 * 2**20),
        cost_estimate=about(6),
        name="feed_forward",
    )(hidden, weights, weights, weights)


def ffn_backward_kernel(dims, g_ref, wg_ref, wu_ref, wd_ref, slope_ref, act_ref, gg_ref, gu_ref, out_ref, acc):
    z = pl.program_id(0)
    grad_inner = dot(g_ref[...], whole_block(dims, wd_ref), 1, 0)
    gg = (grad_inner * slope_ref[...]).astype(BF)
    gu = (grad_inner * act_ref[...]).astype(BF)
    gg_ref[...] = gg
    gu_ref[...] = gu
    added = dot(gg, whole_block(dims, wg_ref), 1, 1) + dot(gu, whole_block(dims, wu_ref), 1, 1)
    add_up(z, added, acc, out_ref)


def ffn_backward(grad, weights, slope, act, dims, kind):
    rows, width = grad.shape
    nz, nb, _, nr, hs = weights.shape
    wspec = lambda m: pl.BlockSpec((1, nb, 1, nr, hs), lambda z: (z, 0, m, 0, 0))
    full = pl.BlockSpec((rows, width), lambda z: (0, 0))
    col = pl.BlockSpec((rows, hs), lambda z: (0, z))
    shape = jax.ShapeDtypeStruct
    return pl.pallas_call(
        functools.partial(ffn_backward_kernel, dims),
        out_shape=(
            shape((rows, nz * hs), BF),
            shape((rows, nz * hs), BF),
            shape((rows, width), kind),
        ),
        grid=(nz,),
        in_specs=[full, wspec(0), wspec(1), wspec(2), col, col],
        out_specs=[col, col, full],
        scratch_shapes=[pltpu.VMEM((rows, width), F32)],
        compiler_params=pltpu.CompilerParams(vmem_limit_bytes=56 * 2**20),
        cost_estimate=about(6),
        name="feed_forward_back",
    )(grad, weights, weights, weights, slope, act)


def weight_grad_kernel(dims, pieces, count, where, *refs):
    nf, nx, nc = dims
    lefts, rights = refs[:pieces], refs[pieces : pieces * (count + 1)]
    outs, (plain, flipped) = refs[pieces * (count + 1) : -2], refs[-2:]
    feat = plain.shape[0] // (nf * nx * nc)
    tokens = lefts[0].shape[0]

    @pl.when(pl.program_id(0) == 0)
    def _():
        for p, left in enumerate(lefts):
            plain[:, p * tokens : (p + 1) * tokens] = left[...].astype(F32).T.astype(BF)
        n = 0
        for dc in range(nc):
            for dy in range(nf):
                for a in range(nx):
                    row = ((where[0] ^ dy) * nx + a) * nc + (where[1] ^ dc)
                    flipped[n * feat : (n + 1) * feat, :] = plain[
                        pl.ds(pl.multiple_of(row * feat, feat), feat), :
                    ]
                    n += 1

    part = flipped.shape[0] // (nc * nf)
    for i in range(count):
        right = jnp.concatenate([rights[i * pieces + p][...] for p in range(pieces)], axis=0)
        done = dot(flipped[...], right, 1, 0).astype(BF)
        for b in range(nc):
            for f in range(nf):
                n = b * nf + f
                outs[i * nc + b][f, 0] = done[n * part : (n + 1) * part]


def weight_grad(lefts, rights, where, nz, dims):
    rows, width = lefts[0].shape
    nf, nx, nc = dims
    hs = rights[0][0].shape[1] // nz
    count, pieces = len(rights), len(lefts)
    shape = (nf, nz, width // (nf * nc), hs)
    return pl.pallas_call(
        functools.partial(weight_grad_kernel, dims, pieces, count),
        out_shape=(jax.ShapeDtypeStruct(shape, BF),) * (count * nc),
        grid_spec=pltpu.PrefetchScalarGridSpec(
            num_scalar_prefetch=1,
            grid=(nz,),
            in_specs=[pl.BlockSpec((rows, width), lambda z, w: (0, 0))] * pieces
            + [pl.BlockSpec((rows, hs), lambda z, w: (0, z))] * (count * pieces),
            out_specs=[pl.BlockSpec((nf, 1) + shape[2:], lambda z, w: (0, z, 0, 0))] * (count * nc),
            scratch_shapes=[pltpu.VMEM((width, rows * pieces), BF)] * 2,
        ),
        compiler_params=pltpu.CompilerParams(vmem_limit_bytes=56 * 2**20),
        cost_estimate=about(5),
        name="weight_grad",
    )(where, *lefts, *[r for right in rights for r in right])


def on_device(
    tokens, teacher, segment_ids, positions, valid_mask, valid_count, gain_attn, w_query, w_key,
    w_value, w_out, gain_ffn, w_gate, w_up, w_down,
):
    nf, nx, nc, nz = (lax.axis_size(a) for a in AXES)
    y, x, c, z = (lax.axis_index(a) for a in AXES)
    place = x * nc + c
    rows, width = tokens.shape[1:]
    share = rows // nz
    feat = w_query.shape[0]
    q_cols, kv_cols = w_query.shape[1], w_key.shape[1]
    heads_k = kv_cols // HD
    hidden_dev = w_gate.shape[1]
    hs = hidden_dev // nx
    own_rows = lambda v: lax.dynamic_slice_in_dim(v, z * share, share, 0)
    att_scale = HD ** (-0.5)

    qkv_cols = q_cols + 2 * kv_cols
    gains = jnp.pad(jnp.stack([gain_attn, gain_ffn]), ((0, 14), (0, qkv_cols - feat)))
    in_shard = jnp.concatenate([jnp.concatenate([w_query, w_key, w_value], axis=1), gains], axis=0)
    scale_a, normed_a = norm_parts(tokens[0].astype(F32))
    out_parts = everyone(w_out.T, "tp")
    out_shard = jnp.concatenate(out_parts, axis=1)
    out_y = swap(out_shard, "fsdp") if nf == 2 else out_shard
    (w_qkv, gain_rows), x_parts, came = gather_rows(in_shard, out_parts[1:] or None, (scale_a, out_y), feat)
    w_qkv = w_qkv.reshape(-1, qkv_cols)
    gain_rows = gain_rows[:, :2, :feat].astype(F32)
    gain_att, gain_mlp = (gain_rows[:, i].reshape(1, -1) for i in range(2))

    ffn_stack = after(jnp.stack([w_gate, w_up, w_down.T]), came[:2])
    hidden_part = lambda k: lax.dynamic_slice_in_dim(ffn_stack, (x ^ k) * hs, hs, 2)
    pieces = [hidden_part(0)] + [swap(hidden_part(k), "cx", k) for k in range(1, nx)]
    swapped = pieces[1:]
    pieces[1:] = after(pieces[1:], w_qkv) if nx > 1 else []
    ffn_shard = jnp.stack(ordered(pieces, x), axis=1).reshape(3 * nx * feat, hs)
    ffn_weights = lax.all_gather(ffn_shard, ("tp", "fsdp", "cc"), axis=0, tiled=True)
    ffn_weights = ffn_weights.reshape(nz, nf * nc, 3, nx * feat, hs)

    half = HD // 2
    frequency = jnp.exp(
        jnp.arange(half).astype(F32) * (-2.0 * math.log(ROPE_BASE) / HD)
    )
    angles = frequency[:, None] * positions[0].astype(F32)[None]
    cos_table, sin_table = jnp.cos(angles)[None], jnp.sin(angles)[None]

    hidden_a = (normed_a * gain_att).astype(BF)
    kv_lin = dot(w_qkv[:, q_cols:], hidden_a, 0, 1)
    k_rot = turned(kv_lin[:kv_cols].reshape(heads_k, HD, rows), cos_table, sin_table)
    kv_own = jnp.concatenate([k_rot.reshape(kv_cols, rows), kv_lin[kv_cols:]], axis=0).astype(BF)
    q_lin = dot(w_qkv[:, :q_cols], hidden_a, 0, 1)
    q_rot = turned(q_lin.reshape(-1, HD, rows), cos_table, sin_table).reshape(q_cols, rows).astype(BF)
    (out_weights,), out_x, out_came = gather_rows(out_shard, from_y=out_y, hold_x=came)
    out_weights = out_weights.reshape(width, -1)
    kv_parts = everyone(kv_own.reshape(2, kv_cols, rows), "cx")

    seg_own = after(segment_ids[0][None], kv_own)
    seg_parts = everyone(seg_own, "cx")
    seg_near = jnp.concatenate(ordered(seg_parts, x), axis=0)
    seg_all = jnp.stack(ordered(everyone(seg_near, "cc"), c), axis=1).reshape(1, -1)
    doc_start = jnp.sum((seg_all < segment_ids[0][:, None]).astype(jnp.int32), axis=1)[None]
    query_place = place * rows + jnp.arange(rows, dtype=jnp.int32)[None]

    q_rot = after(q_rot, out_weights)
    if nx > 1:
        kv_parts[1:] = after(kv_parts[1:], q_rot, doc_start)
    kv_near = jnp.stack(kv_parts)
    kv_sources = everyone(kv_near, "cc")
    kv_place = jnp.stack(
        [(x ^ dx) * nc + (c ^ dc) for dc in range(nc) for dx in range(nx)]
    ).astype(jnp.int32)

    first_row = place * rows
    o_t, o_f, lse = attn_fwd(
        q_rot, kv_sources, kv_place, doc_start, query_place,
        make_bounds(doc_start, first_row, rows, FWD_TQ, FWD_TK), FWD_TQ, FWD_TK,
    )

    chunk = lambda v, k: lax.dynamic_slice_in_dim(v, (z ^ k) * share, share, 1)
    att_t = jnp.concatenate(
        [chunk(o_t, 0)] + [swap(chunk(o_t, k), "tp", k) for k in range(1, nz)], axis=0
    )
    rows_own = own_rows(tokens[0]).astype(F32)
    resid = rows_own + dot(att_t, out_weights, 0, 1)
    scale_f, normed_f = norm_parts(resid)
    hidden_own = (normed_f * gain_mlp).astype(BF)
    dims = (nf, nx, nc)
    hidden_parts = everyone(hidden_own, "cx")
    done = []
    for k, h in enumerate(hidden_parts):
        hidden_parts[k] = after(h, done[-1]) if k else h
        done.append(ffn_forward(hidden_parts[k], ffn_weights, dims, BF if k else F32))
    slopes, acts, inners, outs = zip(*done)

    def returned(parts, *others):
        total = parts[0]
        for k in range(1, nx):
            back = swap(parts[k], "cx", k)
            total = total + (after(back, *others) if others else back).astype(F32)
        return total

    result = resid + returned(outs)
    target = own_rows(teacher[0]).astype(F32)
    valid = own_rows(valid_mask[0].astype(F32)[:, None])
    error = result - target
    grad_out = valid * error
    loss_part = jnp.sum(grad_out * error)
    grad_out_low, result_low = after((grad_out.astype(BF), result.astype(BF)), loss_part[None])
    ffn_grads = everyone(grad_out_low, "cx")
    where = jnp.stack([y, c]).astype(jnp.int32)
    mixed = lax.all_gather(result_low, "tp", axis=0, tiled=True)

    def to_rows(parts):
        others = [swap(parts[k], "cc", k) for k in range(1, nc)]

        def over_cores(f):
            total = parts[0][f].astype(F32)
            for other in others:
                total = total + other[f].astype(F32)
            return total

        sends = [over_cores(k).astype(BF) for k in range(1, nf)]
        return over_cores, sends, [swap(sends[k - 1], "fsdp", k) for k in range(1, nf)]

    def scattered(over_cores, given, hold):
        total = over_cores(0)
        for k in range(1, nf):
            total = total + after(given[k - 1], hold).astype(F32)
        total = total.astype(BF)
        return (total,) + spread(total)

    def spread(total):
        done = lax.psum_scatter(
            total.reshape(nz * nx * feat, hs), "tp", scatter_dimension=0, tiled=True
        ).reshape(nx, feat, hs)
        piece = lambda k: lax.dynamic_index_in_dim(done, x ^ k, 0, keepdims=False)
        pieces = [piece(0)] + [swap(piece(k), "cx", k) for k in range(1, nx)]
        return done, jnp.concatenate(ordered(pieces, x), axis=1).astype(F32)

    done = []
    for k, g in enumerate(ffn_grads):
        ffn_grads[k] = after(g, done[-1]) if k else g
        done.append(ffn_backward(ffn_grads[k], ffn_weights, slopes[k], acts[k], dims, BF if k else F32))
    grad_gates, grad_ups, ffn_backs = zip(*done)
    inners = (after(inners[0], ffn_backs[-1]),) + inners[1:]
    part_down = weight_grad(ffn_grads, [inners], where, nz, dims)
    grad_gates = (after(grad_gates[0], part_down),) + grad_gates[1:]
    part_gate_up = weight_grad(hidden_parts, [grad_gates, grad_ups], where, nz, dims)
    down_own, down_sends, down_given = to_rows(part_down)
    grad_hidden_f = returned(ffn_backs, down_sends, part_gate_up)
    part_gain_mlp = jnp.sum(grad_hidden_f * normed_f, axis=0)
    grad_mid = grad_out + norm_back(grad_hidden_f, normed_f, scale_f, gain_mlp)
    grad_attn = after(grad_mid.astype(BF), mixed)
    g_att = dot(out_weights, grad_attn, 0, 1).astype(BF).reshape(nz, q_cols, share)
    g_parts = [g_att[0]] + [swap(g_att[k], "tp", k) for k in range(1, nz)]
    down_total, down_done, shard_down_t = scattered(down_own, down_given, g_parts[1:])
    gate_own, gate_sends, gate_given = to_rows(part_gate_up[:nc])
    up_own, up_sends, up_given = to_rows(part_gate_up[nc:])
    grad_heads = jnp.concatenate(ordered(after(g_parts, down_total, gate_sends), z), axis=1)

    bounds = make_bounds(doc_start, first_row, rows, BWD_TQ, BWD_TK)
    dqs, kv_sends, kv_grads = [], [], []
    for head in range(heads_k):
        dq, *dkv = attn_bwd(
            q_rot, kv_sources, kv_place, doc_start, query_place, bounds, grad_heads, o_f, lse,
            BWD_TQ, BWD_TK, head,
        )
        if head == heads_k - 1 and head:
            dkv[-1] = after(dkv[-1], gate_done)
        dkv_others = [swap(dkv[k], "cc", k) for k in range(1, nc)]

        def kv_over_cores(k):
            total = dkv[0][k].astype(F32)
            for other in dkv_others:
                total = total + other[k].astype(F32)
            return total

        sends = [kv_over_cores(k).astype(BF) for k in range(1, nx)]
        if head == 0 and heads_k > 1:
            gate_total, gate_done, shard_gate = scattered(gate_own, gate_given, sends)
            grad_heads = after(grad_heads, sends, gate_total, up_sends, down_done)
        if head == heads_k - 1 and sends:
            sends = after(sends, up_given)
        dqs.append(dq)
        kv_sends.append((kv_over_cores(0), [swap(sends[k - 1], "cx", k) for k in range(1, nx)]))
    if heads_k == 1:
        gate_total, gate_done, shard_gate = scattered(gate_own, gate_given, sends)
    gq = jnp.concatenate([turned(d.reshape(-1, HD, rows) * att_scale, cos_table, -sin_table) for d in dqs])
    gq = gq.reshape(q_cols, rows).astype(BF)
    up_total, up_done, shard_up = scattered(up_own, up_given, sends)
    for kv_grad, others in kv_sends:
        for other in others:
            kv_grad = kv_grad + after(other, up_total).astype(F32)
        kv_grads.append(kv_grad)
    kv_grad = jnp.stack(kv_grads, axis=1)
    gk = turned(kv_grad[0] * att_scale, cos_table, -sin_table)
    gkv = jnp.concatenate([gk, kv_grad[1]], axis=0).reshape(2 * kv_cols, rows).astype(BF)
    grad_qkv = jnp.concatenate([gq, gkv], axis=0)
    part_h1 = dot(grad_qkv, w_qkv, 0, 1).astype(BF)
    part_h1 = after(part_h1, up_done)
    grad_hidden_a = lax.psum_scatter(part_h1, "tp", scatter_dimension=0, tiled=True)
    part_out = dot(after(grad_attn, sends), att_t, 0, 1).astype(BF)
    part_qkv = dot(after(hidden_a, part_h1), grad_qkv, 0, 1).astype(BF)
    shard_out_t, out_y = scatter_rows(part_out)
    shard_qkv, qkv_y = scatter_rows(part_qkv)
    shard_out_t = summed(
        shard_out_t.astype(BF).reshape(feat, nz, q_cols), 1, "tp", 0
    )
    grad_hidden_a = after(grad_hidden_a, out_y, qkv_y).astype(F32)
    scale_share = own_rows(scale_a)
    normed_share = rows_own * scale_share
    part_gain_att = jnp.sum(grad_hidden_a * normed_share, axis=0)
    grad_share = grad_mid + norm_back(grad_hidden_a, normed_share, scale_share, gain_att)
    grad_share = grad_share.astype(BF)
    grad_tokens = lax.all_gather(grad_share, "tp", axis=0, tiled=True)

    small = jnp.stack([part_gain_att, part_gain_mlp, jnp.broadcast_to(loss_part, (width,))])
    small = after(small, grad_share)
    for axis in AXES:
        step = 1
        while step < lax.axis_size(axis):
            small = small + swap(small, axis, step)
            step *= 2
    small_own = lax.dynamic_slice_in_dim(small[:2], ((y * nx + x) * nc + c) * feat, feat, 1)
    loss = small[2, 0] / (valid_count.astype(F32) * width)

    grad_tokens = after(
        grad_tokens, small_own, shard_qkv, shard_out_t, shard_gate, shard_up, shard_down_t
    ).astype(F32)
    return (
        mixed[None],
        loss,
        grad_tokens[None],
        small_own[0],
        shard_qkv[:, :q_cols],
        shard_qkv[:, q_cols : q_cols + kv_cols],
        shard_qkv[:, q_cols + kv_cols :],
        shard_out_t.T,
        small_own[1],
        shard_gate,
        shard_up,
        shard_down_t.T,
    )


FWD_TQ, FWD_TK = 256, 1024
BWD_TQ, BWD_TK = 256, 512


def solution(mesh):
    nf, nctx, nz = (mesh.shape[a] for a in ("fsdp", "ctx", "tp"))
    nc = 2 if nctx % 2 == 0 else 1
    fine = Mesh(mesh.devices.reshape(nf, nctx // nc, nc, nz), AXES)
    ctx = ("cx", "cc")
    rows = ("fsdp", "cx", "cc")
    return jax.shard_map(
        on_device,
        mesh=fine,
        in_specs=(
            P("fsdp", ctx, None),
            P("fsdp", ctx, None),
            P("fsdp", ctx),
            P("fsdp", ctx),
            P("fsdp", ctx),
            P(),
            P(rows),
            P(rows, "tp"),
            P(rows, "tp"),
            P(rows, "tp"),
            P("tp", rows),
            P(rows),
            P(rows, "tp"),
            P(rows, "tp"),
            P("tp", rows),
        ),
        out_specs=(
            P("fsdp", ctx, None),
            P(),
            P("fsdp", ctx, None),
            P(rows),
            P(rows, "tp"),
            P(rows, "tp"),
            P(rows, "tp"),
            P("tp", rows),
            P(rows),
            P(rows, "tp"),
            P(rows, "tp"),
            P("tp", rows),
        ),
        check_vma=False,
    )
```

```python
import functools
import math

import jax
import jax.numpy as jnp
from jax import lax
from jax.experimental import pallas as pl
from jax.experimental.pallas import tpu as pltpu
from jax.sharding import Mesh
from jax.sharding import PartitionSpec as P

HD=96
NO_COST = pl.CostEstimate(flops=0, bytes_accessed=0, transcendentals=0)


def about(us):
    return pl.CostEstimate(flops=us*10**9, bytes_accessed=10**6, transcendentals=0)
NEG=-1e30
F32=jnp.float32; BF=jnp.bfloat16
def dot(a,b,ca,cb):
    return lax.dot_general(a,b,(((ca,),(cb,)),((),())),preferred_element_type=F32)

def load_blocks(place, sources, keys_t, keys, values_t, values):
    n = 0
    for source in sources:
        width = source.shape[3]
        for b in range(source.shape[0]):
            at = pl.ds(pl.multiple_of(place[n]*width, width), width)
            n += 1
            if keys_t is not None:
                keys_t[:, at] = source[b, 0]
            keys[at, :] = source[b, 0].astype(F32).T.astype(BF)
            if values_t is not None:
                values_t[:, at] = source[b, 1]
            if values is not None:
                values[at, :] = source[b, 1].astype(F32).T.astype(BF)

def fwd_kernel(scale2, tq, tk, group, count, bounds, place, q_ref, *refs):
    sources, (st_ref, qp_ref, o_ref, of_ref, lse_ref, ks, v_ref, m_s, l_s, acc) = refs[:count], refs[count:]
    i = pl.program_id(1)
    @pl.when(i == 0)
    def _():
        load_blocks(place, sources, None, ks, v_ref, None)
    q2 = jnp.concatenate([q_ref[h*HD:(h+1)*HD, :] for h in range(group)], axis=1)
    st = jnp.concatenate([st_ref[...]]*group, axis=1)
    qp = jnp.concatenate([qp_ref[...]]*group, axis=1)
    m_s[...] = jnp.full_like(m_s, NEG)
    l_s[...] = jnp.zeros_like(l_s)
    acc[...] = jnp.zeros_like(acc)
    def step(masked, j, _):
        off = pl.multiple_of(j*tk, tk)
        s = dot(ks[pl.ds(off, tk), :], q2, 1, 0)
        if masked:
            kid = off + lax.broadcasted_iota(jnp.int32, s.shape, 0)
            s = jnp.where((kid >= st) & (kid <= qp), s, NEG)
        m_old = m_s[...]
        m_new = jnp.maximum(m_old, jnp.max(s, axis=0, keepdims=True))
        p = jnp.exp2((s - m_new)*scale2)
        al = jnp.exp2((m_old - m_new)*scale2)
        l_s[...] = l_s[...]*al + jnp.sum(p, axis=0, keepdims=True)
        m_s[...] = m_new
        acc[...] = acc[...]*al + dot(v_ref[:, pl.ds(off, tk)], p.astype(BF), 1, 0)
        return 0
    lo, a, b, hi = bounds[i,0], bounds[i,1], bounds[i,2], bounds[i,3]
    lax.fori_loop(lo, a, functools.partial(step, True), 0)
    lax.fori_loop(a, b, functools.partial(step, False), 0)
    lax.fori_loop(b, hi, functools.partial(step, True), 0)
    o = acc[...]/l_s[...]
    lse = m_s[...]*scale2 + jnp.log2(l_s[...])
    for h in range(group):
        oh = o[:, h*tq:(h+1)*tq]
        of_ref[h*HD:(h+1)*HD, :] = oh
        o_ref[h*HD:(h+1)*HD, :] = oh.astype(BF)
        lse_ref[0, h:h+1, :] = lse[:, h*tq:(h+1)*tq]

def kv_spec(source):
    return pl.BlockSpec((source.shape[0], 2, HD, source.shape[3]), lambda g,i,*_:(0,0,g,0))

def attn_fwd(qT, kv_sources, place, start, qpos, bounds, tq=256, tk=512):
    T = qT.shape[1]; kv = kv_sources[0].shape[2]//HD; group = qT.shape[0]//HD//kv
    N = sum(s.shape[0] for s in kv_sources)*T
    scale2 = HD**-0.5*math.log2(math.e)
    qs = pl.BlockSpec((group*HD, tq), lambda g,i,*_:(g,i))
    row = pl.BlockSpec((1, tq), lambda g,i,*_:(0,i))
    return pl.pallas_call(
        functools.partial(fwd_kernel, scale2, tq, tk, group, len(kv_sources)),
        out_shape=(jax.ShapeDtypeStruct(qT.shape, BF), jax.ShapeDtypeStruct(qT.shape, F32), jax.ShapeDtypeStruct((kv, group, T), F32)),
        grid_spec=pltpu.PrefetchScalarGridSpec(num_scalar_prefetch=2, grid=(kv, T//tq),
            in_specs=[qs] + [kv_spec(s) for s in kv_sources] + [row, row],
            out_specs=[qs, qs, pl.BlockSpec((1, group, tq), lambda g,i,*_:(g,0,i))],
            scratch_shapes=[pltpu.VMEM((N,HD),BF), pltpu.VMEM((HD,N),BF), pltpu.VMEM((1,group*tq),F32), pltpu.VMEM((1,group*tq),F32), pltpu.VMEM((HD,group*tq),F32)]),
        compiler_params=pltpu.CompilerParams(vmem_limit_bytes=48*2**20),
        cost_estimate=about(12),
        name="attend",
    )(bounds, place, qT, *kv_sources, start, qpos)

def bwd_kernel(scale2, tq, tk, group, count, bounds, place, q_ref, *refs):
    sources, (st_ref, qp_ref, g_ref, of_ref, lse_ref, dq_ref) = refs[:count], refs[count:count+6]
    dkv_refs, (k_ref, ks, vs, dks, dvs, dqs) = refs[count+6:2*count+6], refs[2*count+6:]
    i = pl.program_id(1)
    @pl.when(i == 0)
    def _():
        load_blocks(place, sources, k_ref, ks, None, vs)
        dks[...] = jnp.zeros_like(dks)
        dvs[...] = jnp.zeros_like(dvs)
    cat = lambda f: jnp.concatenate([f(h) for h in range(group)], axis=1)
    q2 = cat(lambda h: q_ref[h*HD:(h+1)*HD, :])
    g2 = cat(lambda h: g_ref[h*HD:(h+1)*HD, :])
    lse = cat(lambda h: lse_ref[0, h:h+1, :])
    delta = cat(lambda h: jnp.sum(g_ref[h*HD:(h+1)*HD, :].astype(F32)*of_ref[h*HD:(h+1)*HD, :], axis=0, keepdims=True))
    st = cat(lambda h: st_ref[...])
    qp = cat(lambda h: qp_ref[...])
    dqs[...] = jnp.zeros_like(dqs)
    def step(masked, j, _):
        off = pl.multiple_of(j*tk, tk)
        s = dot(ks[pl.ds(off, tk), :], q2, 1, 0)
        if masked:
            kid = off + lax.broadcasted_iota(jnp.int32, s.shape, 0)
            s = jnp.where((kid >= st) & (kid <= qp), s, NEG)
        p = jnp.exp2(s*scale2 - lse)
        dp = dot(vs[pl.ds(off, tk), :], g2, 1, 0)
        ds = (p*(dp - delta)).astype(BF)
        dvs[:, pl.ds(off, tk)] += dot(g2, p.astype(BF), 1, 1)
        dks[:, pl.ds(off, tk)] += dot(q2, ds, 1, 1)
        dqs[...] += dot(k_ref[:, pl.ds(off, tk)], ds, 1, 0)
        return 0
    lo, a, b, hi = bounds[i,0], bounds[i,1], bounds[i,2], bounds[i,3]
    lax.fori_loop(lo, a, functools.partial(step, True), 0)
    lax.fori_loop(a, b, functools.partial(step, False), 0)
    lax.fori_loop(b, hi, functools.partial(step, True), 0)
    for h in range(group):
        dq_ref[h*HD:(h+1)*HD, :] = dqs[:, h*tq:(h+1)*tq]
    @pl.when(i == pl.num_programs(1)-1)
    def _():
        n = 0
        for dkv_ref in dkv_refs:
            width = dkv_ref.shape[3]
            for b in range(dkv_ref.shape[0]):
                at = pl.ds(pl.multiple_of(place[n]*width, width), width)
                n += 1
                dkv_ref[b, 0] = dks[:, at].astype(BF)
                dkv_ref[b, 1] = dvs[:, at].astype(BF)

def attn_bwd(qT, kv_sources, place, start, qpos, bounds, gT, of, lse, tq, tk, head):
    T = qT.shape[1]; kv = kv_sources[0].shape[2]//HD; group = qT.shape[0]//HD//kv
    N = sum(s.shape[0] for s in kv_sources)*T
    scale2 = HD**-0.5*math.log2(math.e)
    qs = pl.BlockSpec((group*HD, tq), lambda g,i,*_:(head,i))
    row = pl.BlockSpec((1, tq), lambda g,i,*_:(0,i))
    kv_in = [pl.BlockSpec((s.shape[0], 2, HD, T), lambda g,i,*_:(0,0,head,0)) for s in kv_sources]
    kv_out = [pl.BlockSpec((s.shape[0], 2, HD, T), lambda g,i,*_:(0,0,0,0)) for s in kv_sources]
    return pl.pallas_call(
        functools.partial(bwd_kernel, scale2, tq, tk, group, len(kv_sources)),
        out_shape=[jax.ShapeDtypeStruct((group*HD, T), F32)] + [jax.ShapeDtypeStruct((s.shape[0], 2, HD, T), BF) for s in kv_sources],
        grid_spec=pltpu.PrefetchScalarGridSpec(num_scalar_prefetch=2, grid=(1, T//tq),
            in_specs=[qs] + kv_in + [row, row, qs, qs, pl.BlockSpec((1, group, tq), lambda g,i,*_:(head,0,i))],
            out_specs=[pl.BlockSpec((group*HD, tq), lambda g,i,*_:(0,i))] + kv_out,
            scratch_shapes=[pltpu.VMEM((HD,N),BF), pltpu.VMEM((N,HD),BF), pltpu.VMEM((N,HD),BF), pltpu.VMEM((HD,N),F32), pltpu.VMEM((HD,N),F32), pltpu.VMEM((HD,group*tq),F32)]),
        compiler_params=pltpu.CompilerParams(vmem_limit_bytes=56*2**20),
        cost_estimate=about(12),
        name="attend_back",
    )(bounds, place, qT, *kv_sources, start, qpos, gT, of, lse)

def make_bounds(start, q_first, T, tq, tk):
    s = start.reshape(-1, tq)
    first = q_first + jnp.arange(T//tq, dtype=jnp.int32)*tq
    lo = s[:,0]//tk
    hi = (first + tq - 1)//tk + 1
    a = jnp.minimum((s[:,-1] + tk - 1)//tk, hi)
    b = jnp.maximum(first//tk, a)
    return jnp.stack([lo,a,b,hi],axis=1).astype(jnp.int32)

EPSILON = 1e-05
ROPE_BASE = 100000.0
AXES = ("fsdp", "cx", "cc", "tp")


def swap(values, axis, step=1):
    size = lax.axis_size(axis)
    return lax.ppermute(values, axis, [(i, i ^ step) for i in range(size)])


def after_kernel(*refs):
    pass


def after(values, *others):
    values, tree = jax.tree.flatten(values)
    others = jax.tree.leaves(others)
    done = pl.pallas_call(
        after_kernel,
        out_shape=[jax.ShapeDtypeStruct(v.shape, v.dtype) for v in values],
        in_specs=[pl.BlockSpec(memory_space=pl.ANY)] * (len(values) + len(others)),
        out_specs=[pl.BlockSpec(memory_space=pl.ANY)] * len(values),
        input_output_aliases={i: i for i in range(len(values))},
        cost_estimate=NO_COST,
        name="after",
    )(*values, *others)
    return jax.tree.unflatten(tree, list(done))


def ordered(parts, index):
    if len(parts) == 1:
        return list(parts)
    if len(parts) == 2:
        first = index == 0
        return [jnp.where(first, parts[0], parts[1]), jnp.where(first, parts[1], parts[0])]
    stacked = jnp.stack(parts)
    return [
        lax.dynamic_index_in_dim(stacked, jnp.bitwise_xor(index, a), 0, keepdims=False)
        for a in range(len(parts))
    ]


def everyone(values, axis):
    return [values] + [swap(values, axis, k) for k in range(1, lax.axis_size(axis))]


def place_kernel(plan, count, place, *refs):
    sources, outs, sems = refs[:count], refs[count:-1], refs[-1]
    copies = [
        pltpu.make_async_copy(
            sources[source].at[pl.ds(first, n)], outs[out].at[place[spot], pl.ds(row, n)], sems.at[i]
        )
        for i, (source, first, n, out, spot, row) in enumerate(plan)
    ]
    for copy in copies:
        copy.start()
    for copy in copies:
        copy.wait()


def put_blocks(pieces, place, rows, cut=None):
    width, kind = pieces[0][0].shape[1], pieces[0][0].dtype
    cuts = [0, rows] if cut is None else [0, cut, rows]
    sources, plan = [], []
    for array, first, n, spot, row in pieces:
        known = [i for i, s in enumerate(sources) if s is array]
        if not known:
            known = [len(sources)]
            sources.append(array)
        for out, (low, high) in enumerate(zip(cuts[:-1], cuts[1:])):
            a, b = max(row, low), min(row + n, high)
            if a < b:
                plan.append((known[0], first + a - row, b - a, out, spot, a - low))
    return pl.pallas_call(
        functools.partial(place_kernel, plan, len(sources)),
        out_shape=[
            jax.ShapeDtypeStruct((len(place), b - a, width), kind) for a, b in zip(cuts[:-1], cuts[1:])
        ],
        in_specs=[pl.BlockSpec(memory_space=pltpu.SMEM)]
        + [pl.BlockSpec(memory_space=pltpu.VMEM)] * len(sources),
        out_specs=[pl.BlockSpec(memory_space=pl.ANY)] * (len(cuts) - 1),
        scratch_shapes=[pltpu.SemaphoreType.DMA((len(plan),))],
        compiler_params=pltpu.CompilerParams(vmem_limit_bytes=32 * 2**20),
        cost_estimate=about(2),
        name="put_blocks",
    )(jnp.stack(place).astype(jnp.int32), *sources)


def gather_rows(shard, hold_near=None, hold_core=None, cut=None, from_y=None, hold_x=None):
    rows, width = shard.shape
    nf, nx, nc = (lax.axis_size(a) for a in ("fsdp", "cx", "cc"))
    y, x, c = (lax.axis_index(a) for a in ("fsdp", "cx", "cc"))
    if nf == 2 and nx == 2:
        half = rows // 2 // 16 * 16
        from_x = swap(shard if hold_x is None else after(shard, hold_x), "cx")
        if from_y is None:
            from_y = swap(shard, "fsdp")
        top = swap(from_y[:half], "cx")
        low = swap(from_x[half:], "fsdp")
        x_parts = [shard, from_x]
        came = [from_x, from_y, top, low]
        if hold_near is not None:
            top, low = after((top, low), hold_near)
        own = [
            (shard, 0, rows, 0, 0),
            (from_x, 0, rows, 1, 0),
            (from_y, 0, rows, 2, 0),
            (top, 0, half, 3, 0),
            (low, 0, rows - half, 3, half),
        ]
    else:
        x_parts = everyone(shard, "cx")
        near = jnp.concatenate(x_parts, axis=0)
        near = jnp.concatenate(everyone(near, "fsdp"), axis=0)
        came = [near]
        own = [(near, i * rows, rows, i, 0) for i in range(nf * nx)]
    pieces = list(own)
    for k in range(1, nc):
        given = {}
        for array, first, n, spot, row in own:
            if id(array) not in given:
                given[id(array)] = swap(array, "cc", k)
                last = id(array)
        if hold_core is not None:
            given[last] = after(given[last], hold_core)
        pieces += [(given[id(a)], first, n, spot + k * nf * nx, row) for a, first, n, spot, row in own]
    place = [
        ((y ^ dy) * nx + (x ^ dx)) * nc + (c ^ dc)
        for dc in range(nc)
        for dy in range(nf)
        for dx in range(nx)
    ]
    return put_blocks(pieces, place, rows, cut), x_parts, came


def scatter_rows(part):
    nf, nx, nc = (lax.axis_size(a) for a in ("fsdp", "cx", "cc"))
    y, x, c = (lax.axis_index(a) for a in ("fsdp", "cx", "cc"))
    width = part.shape[1]
    total = part.reshape(nf, nx, nc, -1, width)
    on_chip = summed(total, 2, "cc", c).astype(jnp.bfloat16)
    on_y = summed(on_chip, 0, "fsdp", y).astype(jnp.bfloat16)
    total = summed(on_y, 0, "cx", x)
    return total, on_y


def summed(part, dim, axis, index):
    take = lambda k: lax.dynamic_index_in_dim(part, index ^ k, dim, keepdims=False)
    total = take(0).astype(jnp.float32)
    for k in range(1, lax.axis_size(axis)):
        total = total + swap(take(k), axis, k).astype(jnp.float32)
    return total


def norm_parts(values):
    factor = lax.rsqrt(jnp.mean(values * values, axis=-1, keepdims=True) + EPSILON)
    return (factor, values * factor)


def norm_back(grad_normed_in, normed, factor, gain_vec):
    grad_normed = grad_normed_in * gain_vec
    return factor * (grad_normed - normed * jnp.mean(grad_normed * normed, axis=-1, keepdims=True))


def turned(values, cos_table, sin_table):
    half = values.shape[1] // 2
    low, high = values[:, :half], values[:, half:]
    return jnp.concatenate(
        [low * cos_table - high * sin_table, high * cos_table + low * sin_table], axis=1
    )


def whole_block(dims, ref):
    nf, nx, nc = dims
    feat = ref.shape[3] // nx
    return jnp.concatenate(
        [
            ref[0, f * nc + b, 0, a * feat : (a + 1) * feat, :]
            for f in range(nf)
            for a in range(nx)
            for b in range(nc)
        ],
        axis=0,
    )


def ffn_forward_kernel(dims, h_ref, wg_ref, wu_ref, wd_ref, slope_ref, act_ref, inner_ref, out_ref, acc):
    z = pl.program_id(0)
    hidden = h_ref[...]
    gate = dot(hidden, whole_block(dims, wg_ref), 1, 0)
    up = dot(hidden, whole_block(dims, wu_ref), 1, 0)
    sig = jax.nn.sigmoid(gate)
    act = gate * sig
    slope_ref[...] = up * (sig * (1.0 + gate * (1.0 - sig)))
    act_ref[...] = act
    inner = (act * up).astype(BF)
    inner_ref[...] = inner
    add_up(z, dot(inner, whole_block(dims, wd_ref), 1, 1), acc, out_ref)


def add_up(z, added, acc, out_ref):
    @pl.when(z == 0)
    def _():
        acc[...] = added

    @pl.when(z > 0)
    def _():
        acc[...] += added

    @pl.when(z == pl.num_programs(0) - 1)
    def _():
        out_ref[...] = acc[...].astype(out_ref.dtype)


def ffn_forward(hidden, weights, dims, kind):
    rows, width = hidden.shape
    nz, nb, _, nr, hs = weights.shape
    wspec = lambda m: pl.BlockSpec((1, nb, 1, nr, hs), lambda z: (z, 0, m, 0, 0))
    full = pl.BlockSpec((rows, width), lambda z: (0, 0))
    col = pl.BlockSpec((rows, hs), lambda z: (0, z))
    shape = jax.ShapeDtypeStruct
    return pl.pallas_call(
        functools.partial(ffn_forward_kernel, dims),
        out_shape=(
            shape((rows, nz * hs), F32),
            shape((rows, nz * hs), F32),
            shape((rows, nz * hs), BF),
            shape((rows, width), kind),
        ),
        grid=(nz,),
        in_specs=[full, wspec(0), wspec(1), wspec(2)],
        out_specs=[col, col, col, full],
        scratch_shapes=[pltpu.VMEM((rows, width), F32)],
        compiler_params=pltpu.CompilerParams(vmem_limit_bytes=56 * 2**20),
        cost_estimate=about(6),
        name="feed_forward",
    )(hidden, weights, weights, weights)


def ffn_backward_kernel(dims, g_ref, wg_ref, wu_ref, wd_ref, slope_ref, act_ref, gg_ref, gu_ref, out_ref, acc):
    z = pl.program_id(0)
    grad_inner = dot(g_ref[...], whole_block(dims, wd_ref), 1, 0)
    gg = (grad_inner * slope_ref[...]).astype(BF)
    gu = (grad_inner * act_ref[...]).astype(BF)
    gg_ref[...] = gg
    gu_ref[...] = gu
    added = dot(gg, whole_block(dims, wg_ref), 1, 1) + dot(gu, whole_block(dims, wu_ref), 1, 1)
    add_up(z, added, acc, out_ref)


def ffn_backward(grad, weights, slope, act, dims, kind):
    rows, width = grad.shape
    nz, nb, _, nr, hs = weights.shape
    wspec = lambda m: pl.BlockSpec((1, nb, 1, nr, hs), lambda z: (z, 0, m, 0, 0))
    full = pl.BlockSpec((rows, width), lambda z: (0, 0))
    col = pl.BlockSpec((rows, hs), lambda z: (0, z))
    shape = jax.ShapeDtypeStruct
    return pl.pallas_call(
        functools.partial(ffn_backward_kernel, dims),
        out_shape=(
            shape((rows, nz * hs), BF),
            shape((rows, nz * hs), BF),
            shape((rows, width), kind),
        ),
        grid=(nz,),
        in_specs=[full, wspec(0), wspec(1), wspec(2), col, col],
        out_specs=[col, col, full],
        scratch_shapes=[pltpu.VMEM((rows, width), F32)],
        compiler_params=pltpu.CompilerParams(vmem_limit_bytes=56 * 2**20),
        cost_estimate=about(6),
        name="feed_forward_back",
    )(grad, weights, weights, weights, slope, act)


def weight_grad_kernel(dims, pieces, count, where, *refs):
    nf, nx, nc = dims
    lefts, rights = refs[:pieces], refs[pieces : pieces * (count + 1)]
    outs, (plain, flipped) = refs[pieces * (count + 1) : -2], refs[-2:]
    feat = plain.shape[0] // (nf * nx * nc)
    tokens = lefts[0].shape[0]

    @pl.when(pl.program_id(0) == 0)
    def _():
        for p, left in enumerate(lefts):
            plain[:, p * tokens : (p + 1) * tokens] = left[...].astype(F32).T.astype(BF)
        n = 0
        for dy in range(nf):
            for a in range(nx):
                row = ((where[0] ^ dy) * nx + a) * nc + where[1]
                flipped[n * feat : (n + 1) * feat, :] = plain[
                    pl.ds(pl.multiple_of(row * feat, feat), feat), :
                ]
                n += 1

    for i in range(count):
        right = jnp.concatenate([rights[i * pieces + p][...] for p in range(pieces)], axis=0)
        done = dot(flipped[...], right, 1, 0).astype(BF)
        for f in range(nf):
            outs[i * nf + f][0] = done[f * nx * feat : (f + 1) * nx * feat]


def weight_grad(lefts, rights, where, nz, dims):
    rows, width = lefts[0].shape
    nf, nx, nc = dims
    hs = rights[0][0].shape[1] // nz
    count, pieces = len(rights), len(lefts)
    shape = (nz, width // (nf * nc), hs)
    return pl.pallas_call(
        functools.partial(weight_grad_kernel, dims, pieces, count),
        out_shape=(jax.ShapeDtypeStruct(shape, BF),) * (count * nf),
        grid_spec=pltpu.PrefetchScalarGridSpec(
            num_scalar_prefetch=1,
            grid=(nz,),
            in_specs=[pl.BlockSpec((rows, width), lambda z, w: (0, 0))] * pieces
            + [pl.BlockSpec((rows, hs), lambda z, w: (0, z))] * (count * pieces),
            out_specs=[pl.BlockSpec((1,) + shape[1:], lambda z, w: (z, 0, 0))] * (count * nf),
            scratch_shapes=[
                pltpu.VMEM((width, rows * pieces), BF),
                pltpu.VMEM((width // nc, rows * pieces), BF),
            ],
        ),
        compiler_params=pltpu.CompilerParams(vmem_limit_bytes=56 * 2**20),
        cost_estimate=about(5),
        name="weight_grad",
    )(where, *lefts, *[r for right in rights for r in right])


def on_device(
    tokens, teacher, segment_ids, positions, valid_mask, valid_count, gain_attn, w_query, w_key,
    w_value, w_out, gain_ffn, w_gate, w_up, w_down,
):
    nf, nx, nc, nz = (lax.axis_size(a) for a in AXES)
    y, x, c, z = (lax.axis_index(a) for a in AXES)
    place = x * nc + c
    rows, width = tokens.shape[1:]
    share = rows // nz
    feat = w_query.shape[0]
    q_cols, kv_cols = w_query.shape[1], w_key.shape[1]
    heads_k = kv_cols // HD
    hidden_dev = w_gate.shape[1]
    hs = hidden_dev // nx
    own_rows = lambda v: lax.dynamic_slice_in_dim(v, z * share, share, 0)
    att_scale = HD ** (-0.5)

    qkv_cols = q_cols + 2 * kv_cols
    gains = jnp.pad(jnp.stack([gain_attn, gain_ffn]), ((0, 14), (0, qkv_cols - feat)))
    in_shard = jnp.concatenate([jnp.concatenate([w_query, w_key, w_value], axis=1), gains], axis=0)
    scale_a, normed_a = norm_parts(tokens[0].astype(F32))
    out_parts = everyone(w_out.T, "tp")
    out_shard = jnp.concatenate(out_parts, axis=1)
    out_y = swap(out_shard, "fsdp") if nf == 2 else out_shard
    (w_qkv, gain_rows), x_parts, came = gather_rows(in_shard, out_parts[1:] or None, (scale_a, out_y), feat)
    w_qkv = w_qkv.reshape(-1, qkv_cols)
    gain_rows = gain_rows[:, :2, :feat].astype(F32)
    gain_att, gain_mlp = (gain_rows[:, i].reshape(1, -1) for i in range(2))

    ffn_stack = after(jnp.stack([w_gate, w_up, w_down.T]), came[:2])
    hidden_part = lambda k: lax.dynamic_slice_in_dim(ffn_stack, (x ^ k) * hs, hs, 2)
    pieces = [hidden_part(0)] + [swap(hidden_part(k), "cx", k) for k in range(1, nx)]
    swapped = pieces[1:]
    pieces[1:] = after(pieces[1:], w_qkv) if nx > 1 else []
    ffn_shard = jnp.stack(ordered(pieces, x), axis=1).reshape(3 * nx * feat, hs)
    ffn_weights = lax.all_gather(ffn_shard, ("tp", "fsdp", "cc"), axis=0, tiled=True)
    ffn_weights = ffn_weights.reshape(nz, nf * nc, 3, nx * feat, hs)

    half = HD // 2
    frequency = jnp.exp(
        jnp.arange(half).astype(F32) * (-2.0 * math.log(ROPE_BASE) / HD)
    )
    angles = frequency[:, None] * positions[0].astype(F32)[None]
    cos_table, sin_table = jnp.cos(angles)[None], jnp.sin(angles)[None]

    hidden_a = (normed_a * gain_att).astype(BF)
    kv_lin = dot(w_qkv[:, q_cols:], hidden_a, 0, 1)
    k_rot = turned(kv_lin[:kv_cols].reshape(heads_k, HD, rows), cos_table, sin_table)
    kv_own = jnp.concatenate([k_rot.reshape(kv_cols, rows), kv_lin[kv_cols:]], axis=0).astype(BF)
    q_lin = dot(w_qkv[:, :q_cols], hidden_a, 0, 1)
    q_rot = turned(q_lin.reshape(-1, HD, rows), cos_table, sin_table).reshape(q_cols, rows).astype(BF)
    (out_weights,), out_x, out_came = gather_rows(out_shard, from_y=out_y, hold_x=came)
    out_weights = out_weights.reshape(width, -1)
    kv_parts = everyone(kv_own.reshape(2, kv_cols, rows), "cx")

    seg_own = after(segment_ids[0][None], kv_own)
    seg_parts = everyone(seg_own, "cx")
    seg_near = jnp.concatenate(ordered(seg_parts, x), axis=0)
    seg_all = jnp.stack(ordered(everyone(seg_near, "cc"), c), axis=1).reshape(1, -1)
    doc_start = jnp.sum((seg_all < segment_ids[0][:, None]).astype(jnp.int32), axis=1)[None]
    query_place = place * rows + jnp.arange(rows, dtype=jnp.int32)[None]

    q_rot = after(q_rot, out_weights)
    if nx > 1:
        kv_parts[1:] = after(kv_parts[1:], q_rot, doc_start)
    kv_near = jnp.stack(kv_parts)
    kv_sources = everyone(kv_near, "cc")
    kv_place = jnp.stack(
        [(x ^ dx) * nc + (c ^ dc) for dc in range(nc) for dx in range(nx)]
    ).astype(jnp.int32)

    first_row = place * rows
    o_t, o_f, lse = attn_fwd(
        q_rot, kv_sources, kv_place, doc_start, query_place,
        make_bounds(doc_start, first_row, rows, FWD_TQ, FWD_TK), FWD_TQ, FWD_TK,
    )

    chunk = lambda v, k: lax.dynamic_slice_in_dim(v, (z ^ k) * share, share, 1)
    att_t = jnp.concatenate(
        [chunk(o_t, 0)] + [swap(chunk(o_t, k), "tp", k) for k in range(1, nz)], axis=0
    )
    rows_own = own_rows(tokens[0]).astype(F32)
    resid = rows_own + dot(att_t, out_weights, 0, 1)
    scale_f, normed_f = norm_parts(resid)
    hidden_own = (normed_f * gain_mlp).astype(BF)
    dims = (nf, nx, nc)
    hidden_parts = everyone(hidden_own, "cx")
    done = []
    for k, h in enumerate(hidden_parts):
        hidden_parts[k] = after(h, done[-1]) if k else h
        done.append(ffn_forward(hidden_parts[k], ffn_weights, dims, BF if k else F32))
    slopes, acts, inners, outs = zip(*done)

    def returned(parts, *others):
        total = parts[0]
        for k in range(1, nx):
            back = swap(parts[k], "cx", k)
            total = total + (after(back, *others) if others else back).astype(F32)
        return total

    result = resid + returned(outs)
    target = own_rows(teacher[0]).astype(F32)
    valid = own_rows(valid_mask[0].astype(F32)[:, None])
    error = result - target
    grad_out = valid * error
    loss_part = jnp.sum(grad_out * error)
    grad_out_low, result_low = after((grad_out.astype(BF), result.astype(BF)), loss_part[None])
    ffn_grads = everyone(grad_out_low, "cx")
    where = jnp.stack([y, c]).astype(jnp.int32)
    mixed = lax.all_gather(result_low, "tp", axis=0, tiled=True)

    def both_cores(parts):
        return [v for part in parts for v in everyone(part, "cc")]

    def to_rows(parts):
        return parts[0], parts[1:], [swap(parts[k], "fsdp", k) for k in range(1, nf)]

    def scattered(own, given, hold):
        total = own.astype(F32)
        for k in range(1, nf):
            total = total + after(given[k - 1], hold).astype(F32)
        total = total.astype(BF)
        return (total,) + spread(total)

    def spread(total):
        done = lax.psum_scatter(
            total.reshape(nz * nx * feat, hs), "tp", scatter_dimension=0, tiled=True
        ).reshape(nx, feat, hs)
        piece = lambda k: lax.dynamic_index_in_dim(done, x ^ k, 0, keepdims=False)
        pieces = [piece(0)] + [swap(piece(k), "cx", k) for k in range(1, nx)]
        return done, jnp.concatenate(ordered(pieces, x), axis=1).astype(F32)

    done = []
    for k, g in enumerate(ffn_grads):
        ffn_grads[k] = after(g, done[-1]) if k else g
        done.append(ffn_backward(ffn_grads[k], ffn_weights, slopes[k], acts[k], dims, BF if k else F32))
    grad_gates, grad_ups, ffn_backs = zip(*done)
    inners = both_cores(inners)
    inners[0] = after(inners[0], ffn_backs[-1])
    part_down = weight_grad(both_cores(ffn_grads), [inners], where, nz, dims)
    grad_gates, grad_ups = both_cores(grad_gates), both_cores(grad_ups)
    grad_gates[0] = after(grad_gates[0], part_down)
    part_gate_up = weight_grad(both_cores(hidden_parts), [grad_gates, grad_ups], where, nz, dims)
    down_own, down_sends, down_given = to_rows(part_down)
    grad_hidden_f = returned(ffn_backs, down_sends, part_gate_up)
    part_gain_mlp = jnp.sum(grad_hidden_f * normed_f, axis=0)
    grad_mid = grad_out + norm_back(grad_hidden_f, normed_f, scale_f, gain_mlp)
    grad_attn = after(grad_mid.astype(BF), mixed)
    g_att = dot(out_weights, grad_attn, 0, 1).astype(BF).reshape(nz, q_cols, share)
    g_parts = [g_att[0]] + [swap(g_att[k], "tp", k) for k in range(1, nz)]
    down_total, down_done, shard_down_t = scattered(down_own, down_given, g_parts[1:])
    gate_own, gate_sends, gate_given = to_rows(part_gate_up[:nf])
    up_own, up_sends, up_given = to_rows(part_gate_up[nf:])
    grad_heads = jnp.concatenate(ordered(after(g_parts, down_total, gate_sends), z), axis=1)

    bounds = make_bounds(doc_start, first_row, rows, BWD_TQ, BWD_TK)
    dqs, kv_sends, kv_grads = [], [], []
    for head in range(heads_k):
        dq, *dkv = attn_bwd(
            q_rot, kv_sources, kv_place, doc_start, query_place, bounds, grad_heads, o_f, lse,
            BWD_TQ, BWD_TK, head,
        )
        if head == heads_k - 1 and head:
            dkv[-1] = after(dkv[-1], gate_done, [o for _, o in kv_sends])
        dkv_others = [swap(dkv[k], "cc", k) for k in range(1, nc)]

        def kv_over_cores(k):
            total = dkv[0][k].astype(F32)
            for other in dkv_others:
                total = total + other[k].astype(F32)
            return total

        sends = [kv_over_cores(k).astype(BF) for k in range(1, nx)]
        if head == 0 and heads_k > 1:
            gate_total, gate_done, shard_gate = scattered(gate_own, gate_given, sends)
            grad_heads = after(grad_heads, sends, gate_total, up_sends, down_done)
        dqs.append(dq)
        kv_sends.append((kv_over_cores(0), [swap(sends[k - 1], "cx", k) for k in range(1, nx)]))
    if heads_k == 1:
        gate_total, gate_done, shard_gate = scattered(gate_own, gate_given, sends)
    gq = jnp.concatenate([turned(d.reshape(-1, HD, rows) * att_scale, cos_table, -sin_table) for d in dqs])
    gq = gq.reshape(q_cols, rows).astype(BF)
    up_total, up_done, shard_up = scattered(up_own, up_given, [kv_sends[0][1], dq])
    for kv_grad, others in kv_sends:
        for other in others:
            kv_grad = kv_grad + after(other, up_total).astype(F32)
        kv_grads.append(kv_grad)
    kv_grad = jnp.stack(kv_grads, axis=1)
    gk = turned(kv_grad[0] * att_scale, cos_table, -sin_table)
    gkv = jnp.concatenate([gk, kv_grad[1]], axis=0).reshape(2 * kv_cols, rows).astype(BF)
    grad_qkv = jnp.concatenate([gq, gkv], axis=0)
    part_h1 = dot(grad_qkv, w_qkv, 0, 1).astype(BF)
    part_h1 = after(part_h1, up_done)
    grad_hidden_a = lax.psum_scatter(part_h1, "tp", scatter_dimension=0, tiled=True)
    part_out = dot(after(grad_attn, sends), att_t, 0, 1).astype(BF)
    part_qkv = dot(after(hidden_a, part_h1), grad_qkv, 0, 1).astype(BF)
    shard_out_t, out_y = scatter_rows(part_out)
    shard_qkv, qkv_y = scatter_rows(part_qkv)
    shard_out_t = summed(
        shard_out_t.astype(BF).reshape(feat, nz, q_cols), 1, "tp", 0
    )
    grad_hidden_a = after(grad_hidden_a, out_y, qkv_y).astype(F32)
    scale_share = own_rows(scale_a)
    normed_share = rows_own * scale_share
    part_gain_att = jnp.sum(grad_hidden_a * normed_share, axis=0)
    grad_share = grad_mid + norm_back(grad_hidden_a, normed_share, scale_share, gain_att)
    grad_share = grad_share.astype(BF)
    grad_tokens = lax.all_gather(grad_share, "tp", axis=0, tiled=True)

    small = jnp.stack([part_gain_att, part_gain_mlp, jnp.broadcast_to(loss_part, (width,))])
    small = after(small, grad_share)
    for axis in AXES:
        step = 1
        while step < lax.axis_size(axis):
            small = small + swap(small, axis, step)
            step *= 2
    small_own = lax.dynamic_slice_in_dim(small[:2], ((y * nx + x) * nc + c) * feat, feat, 1)
    loss = small[2, 0] / (valid_count.astype(F32) * width)

    grad_tokens = after(
        grad_tokens, small_own, shard_qkv, shard_out_t, shard_gate, shard_up, shard_down_t
    ).astype(F32)
    return (
        mixed[None],
        loss,
        grad_tokens[None],
        small_own[0],
        shard_qkv[:, :q_cols],
        shard_qkv[:, q_cols : q_cols + kv_cols],
        shard_qkv[:, q_cols + kv_cols :],
        shard_out_t.T,
        small_own[1],
        shard_gate,
        shard_up,
        shard_down_t.T,
    )


FWD_TQ, FWD_TK = 256, 1024
BWD_TQ, BWD_TK = 256, 512


def solution(mesh):
    nf, nctx, nz = (mesh.shape[a] for a in ("fsdp", "ctx", "tp"))
    nc = 2 if nctx % 2 == 0 else 1
    fine = Mesh(mesh.devices.reshape(nf, nctx // nc, nc, nz), AXES)
    ctx = ("cx", "cc")
    rows = ("fsdp", "cx", "cc")
    return jax.shard_map(
        on_device,
        mesh=fine,
        in_specs=(
            P("fsdp", ctx, None),
            P("fsdp", ctx, None),
            P("fsdp", ctx),
            P("fsdp", ctx),
            P("fsdp", ctx),
            P(),
            P(rows),
            P(rows, "tp"),
            P(rows, "tp"),
            P(rows, "tp"),
            P("tp", rows),
            P(rows),
            P(rows, "tp"),
            P(rows, "tp"),
            P("tp", rows),
        ),
        out_specs=(
            P("fsdp", ctx, None),
            P(),
            P("fsdp", ctx, None),
            P(rows),
            P(rows, "tp"),
            P(rows, "tp"),
            P(rows, "tp"),
            P("tp", rows),
            P(rows),
            P(rows, "tp"),
            P(rows, "tp"),
            P("tp", rows),
        ),
        check_vma=False,
    )
```

```python
import functools
import math

import jax
import jax.numpy as jnp
from jax import lax
from jax.experimental import pallas as pl
from jax.experimental.pallas import tpu as pltpu
from jax.sharding import Mesh
from jax.sharding import PartitionSpec as P

HD=96
NO_COST = pl.CostEstimate(flops=0, bytes_accessed=0, transcendentals=0)


def about(us):
    return pl.CostEstimate(flops=us*10**9, bytes_accessed=10**6, transcendentals=0)
NEG=-1e30
F32=jnp.float32; BF=jnp.bfloat16
def dot(a,b,ca,cb):
    return lax.dot_general(a,b,(((ca,),(cb,)),((),())),preferred_element_type=F32)

def load_blocks(place, sources, keys_t, keys, values_t, values):
    n = 0
    for source in sources:
        width = source.shape[3]
        for b in range(source.shape[0]):
            at = pl.ds(pl.multiple_of(place[n]*width, width), width)
            n += 1
            if keys_t is not None:
                keys_t[:, at] = source[b, 0]
            keys[at, :] = source[b, 0].astype(F32).T.astype(BF)
            if values_t is not None:
                values_t[:, at] = source[b, 1]
            if values is not None:
                values[at, :] = source[b, 1].astype(F32).T.astype(BF)

def fwd_kernel(scale2, tq, tk, group, count, bounds, place, q_ref, *refs):
    sources, (st_ref, qp_ref, o_ref, of_ref, lse_ref, ks, v_ref, m_s, l_s, acc) = refs[:count], refs[count:]
    i = pl.program_id(1)
    @pl.when(i == 0)
    def _():
        load_blocks(place, sources, None, ks, v_ref, None)
    q2 = jnp.concatenate([q_ref[h*HD:(h+1)*HD, :] for h in range(group)], axis=1)
    st = jnp.concatenate([st_ref[...]]*group, axis=1)
    qp = jnp.concatenate([qp_ref[...]]*group, axis=1)
    m_s[...] = jnp.full_like(m_s, NEG)
    l_s[...] = jnp.zeros_like(l_s)
    acc[...] = jnp.zeros_like(acc)
    def step(masked, j, _):
        off = pl.multiple_of(j*tk, tk)
        s = dot(ks[pl.ds(off, tk), :], q2, 1, 0)
        if masked:
            kid = off + lax.broadcasted_iota(jnp.int32, s.shape, 0)
            s = jnp.where((kid >= st) & (kid <= qp), s, NEG)
        m_old = m_s[...]
        m_new = jnp.maximum(m_old, jnp.max(s, axis=0, keepdims=True))
        p = jnp.exp2((s - m_new)*scale2)
        al = jnp.exp2((m_old - m_new)*scale2)
        l_s[...] = l_s[...]*al + jnp.sum(p, axis=0, keepdims=True)
        m_s[...] = m_new
        acc[...] = acc[...]*al + dot(v_ref[:, pl.ds(off, tk)], p.astype(BF), 1, 0)
        return 0
    lo, a, b, hi = bounds[i,0], bounds[i,1], bounds[i,2], bounds[i,3]
    lax.fori_loop(lo, a, functools.partial(step, True), 0)
    lax.fori_loop(a, b, functools.partial(step, False), 0)
    lax.fori_loop(b, hi, functools.partial(step, True), 0)
    o = acc[...]/l_s[...]
    lse = m_s[...]*scale2 + jnp.log2(l_s[...])
    for h in range(group):
        oh = o[:, h*tq:(h+1)*tq]
        of_ref[h*HD:(h+1)*HD, :] = oh
        o_ref[h*HD:(h+1)*HD, :] = oh.astype(BF)
        lse_ref[0, h:h+1, :] = lse[:, h*tq:(h+1)*tq]

def kv_spec(source):
    return pl.BlockSpec((source.shape[0], 2, HD, source.shape[3]), lambda g,i,*_:(0,0,g,0))

def attn_fwd(qT, kv_sources, place, start, qpos, bounds, tq=256, tk=512):
    T = qT.shape[1]; kv = kv_sources[0].shape[2]//HD; group = qT.shape[0]//HD//kv
    N = sum(s.shape[0] for s in kv_sources)*T
    scale2 = HD**-0.5*math.log2(math.e)
    qs = pl.BlockSpec((group*HD, tq), lambda g,i,*_:(g,i))
    row = pl.BlockSpec((1, tq), lambda g,i,*_:(0,i))
    return pl.pallas_call(
        functools.partial(fwd_kernel, scale2, tq, tk, group, len(kv_sources)),
        out_shape=(jax.ShapeDtypeStruct(qT.shape, BF), jax.ShapeDtypeStruct(qT.shape, F32), jax.ShapeDtypeStruct((kv, group, T), F32)),
        grid_spec=pltpu.PrefetchScalarGridSpec(num_scalar_prefetch=2, grid=(kv, T//tq),
            in_specs=[qs] + [kv_spec(s) for s in kv_sources] + [row, row],
            out_specs=[qs, qs, pl.BlockSpec((1, group, tq), lambda g,i,*_:(g,0,i))],
            scratch_shapes=[pltpu.VMEM((N,HD),BF), pltpu.VMEM((HD,N),BF), pltpu.VMEM((1,group*tq),F32), pltpu.VMEM((1,group*tq),F32), pltpu.VMEM((HD,group*tq),F32)]),
        compiler_params=pltpu.CompilerParams(vmem_limit_bytes=48*2**20),
        cost_estimate=about(12),
        name="attend",
    )(bounds, place, qT, *kv_sources, start, qpos)

def bwd_kernel(scale2, tq, tk, group, count, bounds, place, q_ref, *refs):
    sources, (st_ref, qp_ref, g_ref, of_ref, lse_ref, dq_ref) = refs[:count], refs[count:count+6]
    dkv_refs, (k_ref, ks, vs, dks, dvs, dqs) = refs[count+6:2*count+6], refs[2*count+6:]
    i = pl.program_id(1)
    @pl.when(i == 0)
    def _():
        load_blocks(place, sources, k_ref, ks, None, vs)
        dks[...] = jnp.zeros_like(dks)
        dvs[...] = jnp.zeros_like(dvs)
    cat = lambda f: jnp.concatenate([f(h) for h in range(group)], axis=1)
    q2 = cat(lambda h: q_ref[h*HD:(h+1)*HD, :])
    g2 = cat(lambda h: g_ref[h*HD:(h+1)*HD, :])
    lse = cat(lambda h: lse_ref[0, h:h+1, :])
    delta = cat(lambda h: jnp.sum(g_ref[h*HD:(h+1)*HD, :].astype(F32)*of_ref[h*HD:(h+1)*HD, :], axis=0, keepdims=True))
    st = cat(lambda h: st_ref[...])
    qp = cat(lambda h: qp_ref[...])
    dqs[...] = jnp.zeros_like(dqs)
    def step(masked, j, _):
        off = pl.multiple_of(j*tk, tk)
        s = dot(ks[pl.ds(off, tk), :], q2, 1, 0)
        if masked:
            kid = off + lax.broadcasted_iota(jnp.int32, s.shape, 0)
            s = jnp.where((kid >= st) & (kid <= qp), s, NEG)
        p = jnp.exp2(s*scale2 - lse)
        dp = dot(vs[pl.ds(off, tk), :], g2, 1, 0)
        ds = (p*(dp - delta)).astype(BF)
        dvs[:, pl.ds(off, tk)] += dot(g2, p.astype(BF), 1, 1)
        dks[:, pl.ds(off, tk)] += dot(q2, ds, 1, 1)
        dqs[...] += dot(k_ref[:, pl.ds(off, tk)], ds, 1, 0)
        return 0
    lo, a, b, hi = bounds[i,0], bounds[i,1], bounds[i,2], bounds[i,3]
    lax.fori_loop(lo, a, functools.partial(step, True), 0)
    lax.fori_loop(a, b, functools.partial(step, False), 0)
    lax.fori_loop(b, hi, functools.partial(step, True), 0)
    for h in range(group):
        dq_ref[h*HD:(h+1)*HD, :] = dqs[:, h*tq:(h+1)*tq]
    @pl.when(i == pl.num_programs(1)-1)
    def _():
        n = 0
        for dkv_ref in dkv_refs:
            width = dkv_ref.shape[3]
            for b in range(dkv_ref.shape[0]):
                at = pl.ds(pl.multiple_of(place[n]*width, width), width)
                n += 1
                dkv_ref[b, 0] = dks[:, at].astype(BF)
                dkv_ref[b, 1] = dvs[:, at].astype(BF)

def attn_bwd(qT, kv_sources, place, start, qpos, bounds, gT, of, lse, tq, tk, head):
    T = qT.shape[1]; kv = kv_sources[0].shape[2]//HD; group = qT.shape[0]//HD//kv
    N = sum(s.shape[0] for s in kv_sources)*T
    scale2 = HD**-0.5*math.log2(math.e)
    qs = pl.BlockSpec((group*HD, tq), lambda g,i,*_:(head,i))
    row = pl.BlockSpec((1, tq), lambda g,i,*_:(0,i))
    kv_in = [pl.BlockSpec((s.shape[0], 2, HD, T), lambda g,i,*_:(0,0,head,0)) for s in kv_sources]
    kv_out = [pl.BlockSpec((s.shape[0], 2, HD, T), lambda g,i,*_:(0,0,0,0)) for s in kv_sources]
    return pl.pallas_call(
        functools.partial(bwd_kernel, scale2, tq, tk, group, len(kv_sources)),
        out_shape=[jax.ShapeDtypeStruct((group*HD, T), F32)] + [jax.ShapeDtypeStruct((s.shape[0], 2, HD, T), BF) for s in kv_sources],
        grid_spec=pltpu.PrefetchScalarGridSpec(num_scalar_prefetch=2, grid=(1, T//tq),
            in_specs=[qs] + kv_in + [row, row, qs, qs, pl.BlockSpec((1, group, tq), lambda g,i,*_:(head,0,i))],
            out_specs=[pl.BlockSpec((group*HD, tq), lambda g,i,*_:(0,i))] + kv_out,
            scratch_shapes=[pltpu.VMEM((HD,N),BF), pltpu.VMEM((N,HD),BF), pltpu.VMEM((N,HD),BF), pltpu.VMEM((HD,N),F32), pltpu.VMEM((HD,N),F32), pltpu.VMEM((HD,group*tq),F32)]),
        compiler_params=pltpu.CompilerParams(vmem_limit_bytes=56*2**20),
        cost_estimate=about(4),
        name="attend_back",
    )(bounds, place, qT, *kv_sources, start, qpos, gT, of, lse)

def make_bounds(start, q_first, T, tq, tk):
    s = start.reshape(-1, tq)
    first = q_first + jnp.arange(T//tq, dtype=jnp.int32)*tq
    lo = s[:,0]//tk
    hi = (first + tq - 1)//tk + 1
    a = jnp.minimum((s[:,-1] + tk - 1)//tk, hi)
    b = jnp.maximum(first//tk, a)
    return jnp.stack([lo,a,b,hi],axis=1).astype(jnp.int32)

EPSILON = 1e-05
ROPE_BASE = 100000.0
AXES = ("fsdp", "cx", "cc", "tp")


def swap(values, axis, step=1):
    size = lax.axis_size(axis)
    return lax.ppermute(values, axis, [(i, i ^ step) for i in range(size)])


def after_kernel(*refs):
    pass


def after(values, *others):
    values, tree = jax.tree.flatten(values)
    others = jax.tree.leaves(others)
    done = pl.pallas_call(
        after_kernel,
        out_shape=[jax.ShapeDtypeStruct(v.shape, v.dtype) for v in values],
        in_specs=[pl.BlockSpec(memory_space=pl.ANY)] * (len(values) + len(others)),
        out_specs=[pl.BlockSpec(memory_space=pl.ANY)] * len(values),
        input_output_aliases={i: i for i in range(len(values))},
        cost_estimate=NO_COST,
        name="after",
    )(*values, *others)
    return jax.tree.unflatten(tree, list(done))


def ordered(parts, index):
    if len(parts) == 1:
        return list(parts)
    if len(parts) == 2:
        first = index == 0
        return [jnp.where(first, parts[0], parts[1]), jnp.where(first, parts[1], parts[0])]
    stacked = jnp.stack(parts)
    return [
        lax.dynamic_index_in_dim(stacked, jnp.bitwise_xor(index, a), 0, keepdims=False)
        for a in range(len(parts))
    ]


def everyone(values, axis):
    return [values] + [swap(values, axis, k) for k in range(1, lax.axis_size(axis))]


def place_kernel(plan, count, place, *refs):
    sources, outs, sems = refs[:count], refs[count:-1], refs[-1]
    copies = [
        pltpu.make_async_copy(
            sources[source].at[pl.ds(first, n)], outs[out].at[place[spot], pl.ds(row, n)], sems.at[i]
        )
        for i, (source, first, n, out, spot, row) in enumerate(plan)
    ]
    for copy in copies:
        copy.start()
    for copy in copies:
        copy.wait()


def put_blocks(pieces, place, rows, cut=None):
    width, kind = pieces[0][0].shape[1], pieces[0][0].dtype
    cuts = [0, rows] if cut is None else [0, cut, rows]
    sources, plan = [], []
    for array, first, n, spot, row in pieces:
        known = [i for i, s in enumerate(sources) if s is array]
        if not known:
            known = [len(sources)]
            sources.append(array)
        for out, (low, high) in enumerate(zip(cuts[:-1], cuts[1:])):
            a, b = max(row, low), min(row + n, high)
            if a < b:
                plan.append((known[0], first + a - row, b - a, out, spot, a - low))
    return pl.pallas_call(
        functools.partial(place_kernel, plan, len(sources)),
        out_shape=[
            jax.ShapeDtypeStruct((len(place), b - a, width), kind) for a, b in zip(cuts[:-1], cuts[1:])
        ],
        in_specs=[pl.BlockSpec(memory_space=pltpu.SMEM)]
        + [pl.BlockSpec(memory_space=pltpu.VMEM)] * len(sources),
        out_specs=[pl.BlockSpec(memory_space=pl.ANY)] * (len(cuts) - 1),
        scratch_shapes=[pltpu.SemaphoreType.DMA((len(plan),))],
        compiler_params=pltpu.CompilerParams(vmem_limit_bytes=32 * 2**20),
        cost_estimate=about(2),
        name="put_blocks",
    )(jnp.stack(place).astype(jnp.int32), *sources)


def gather_rows(shard, hold_near=None, hold_core=None, cut=None, from_y=None, hold_x=None):
    rows, width = shard.shape
    nf, nx, nc = (lax.axis_size(a) for a in ("fsdp", "cx", "cc"))
    y, x, c = (lax.axis_index(a) for a in ("fsdp", "cx", "cc"))
    if nf == 2 and nx == 2:
        half = rows // 2 // 16 * 16
        from_x = swap(shard if hold_x is None else after(shard, hold_x), "cx")
        if from_y is None:
            from_y = swap(shard, "fsdp")
        top = swap(from_y[:half], "cx")
        low = swap(from_x[half:], "fsdp")
        x_parts = [shard, from_x]
        came = [from_x, from_y, top, low]
        if hold_near is not None:
            top, low = after((top, low), hold_near)
        own = [
            (shard, 0, rows, 0, 0),
            (from_x, 0, rows, 1, 0),
            (from_y, 0, rows, 2, 0),
            (top, 0, half, 3, 0),
            (low, 0, rows - half, 3, half),
        ]
    else:
        x_parts = everyone(shard, "cx")
        near = jnp.concatenate(x_parts, axis=0)
        near = jnp.concatenate(everyone(near, "fsdp"), axis=0)
        came = [near]
        own = [(near, i * rows, rows, i, 0) for i in range(nf * nx)]
    pieces = list(own)
    for k in range(1, nc):
        given = {}
        for array, first, n, spot, row in own:
            if id(array) not in given:
                given[id(array)] = swap(array, "cc", k)
                last = id(array)
        if hold_core is not None:
            given[last] = after(given[last], hold_core)
        pieces += [(given[id(a)], first, n, spot + k * nf * nx, row) for a, first, n, spot, row in own]
    place = [
        ((y ^ dy) * nx + (x ^ dx)) * nc + (c ^ dc)
        for dc in range(nc)
        for dy in range(nf)
        for dx in range(nx)
    ]
    return put_blocks(pieces, place, rows, cut), x_parts, came


def scatter_rows(part):
    nf, nx, nc = (lax.axis_size(a) for a in ("fsdp", "cx", "cc"))
    y, x, c = (lax.axis_index(a) for a in ("fsdp", "cx", "cc"))
    width = part.shape[1]
    total = part.reshape(nf, nx, nc, -1, width)
    on_chip = summed(total, 2, "cc", c).astype(jnp.bfloat16)
    on_y = summed(on_chip, 0, "fsdp", y).astype(jnp.bfloat16)
    total = summed(on_y, 0, "cx", x)
    return total, on_y


def summed(part, dim, axis, index):
    take = lambda k: lax.dynamic_index_in_dim(part, index ^ k, dim, keepdims=False)
    total = take(0).astype(jnp.float32)
    for k in range(1, lax.axis_size(axis)):
        total = total + swap(take(k), axis, k).astype(jnp.float32)
    return total


def norm_parts(values):
    factor = lax.rsqrt(jnp.mean(values * values, axis=-1, keepdims=True) + EPSILON)
    return (factor, values * factor)


def norm_back(grad_normed_in, normed, factor, gain_vec):
    grad_normed = grad_normed_in * gain_vec
    return factor * (grad_normed - normed * jnp.mean(grad_normed * normed, axis=-1, keepdims=True))


def turned(values, cos_table, sin_table):
    half = values.shape[1] // 2
    low, high = values[:, :half], values[:, half:]
    return jnp.concatenate(
        [low * cos_table - high * sin_table, high * cos_table + low * sin_table], axis=1
    )


def whole_block(dims, ref):
    nf, nx, nc = dims
    feat = ref.shape[3] // nx
    return jnp.concatenate(
        [
            ref[0, f * nc + b, 0, a * feat : (a + 1) * feat, :]
            for f in range(nf)
            for a in range(nx)
            for b in range(nc)
        ],
        axis=0,
    )


def ffn_forward_kernel(dims, h_ref, wg_ref, wu_ref, wd_ref, slope_ref, act_ref, inner_ref, out_ref, acc):
    z = pl.program_id(0)
    hidden = h_ref[...]
    gate = dot(hidden, whole_block(dims, wg_ref), 1, 0)
    up = dot(hidden, whole_block(dims, wu_ref), 1, 0)
    sig = jax.nn.sigmoid(gate)
    act = gate * sig
    slope_ref[...] = up * (sig * (1.0 + gate * (1.0 - sig)))
    act_ref[...] = act
    inner = (act * up).astype(BF)
    inner_ref[...] = inner
    add_up(z, dot(inner, whole_block(dims, wd_ref), 1, 1), acc, out_ref)


def add_up(z, added, acc, out_ref):
    @pl.when(z == 0)
    def _():
        acc[...] = added

    @pl.when(z > 0)
    def _():
        acc[...] += added

    @pl.when(z == pl.num_programs(0) - 1)
    def _():
        out_ref[...] = acc[...].astype(out_ref.dtype)


def ffn_forward(hidden, weights, dims, kind):
    rows, width = hidden.shape
    nz, nb, _, nr, hs = weights.shape
    wspec = lambda m: pl.BlockSpec((1, nb, 1, nr, hs), lambda z: (z, 0, m, 0, 0))
    full = pl.BlockSpec((rows, width), lambda z: (0, 0))
    col = pl.BlockSpec((rows, hs), lambda z: (0, z))
    shape = jax.ShapeDtypeStruct
    return pl.pallas_call(
        functools.partial(ffn_forward_kernel, dims),
        out_shape=(
            shape((rows, nz * hs), F32),
            shape((rows, nz * hs), F32),
            shape((rows, nz * hs), BF),
            shape((rows, width), kind),
        ),
        grid=(nz,),
        in_specs=[full, wspec(0), wspec(1), wspec(2)],
        out_specs=[col, col, col, full],
        scratch_shapes=[pltpu.VMEM((rows, width), F32)],
        compiler_params=pltpu.CompilerParams(vmem_limit_bytes=56 * 2**20),
        cost_estimate=about(6),
        name="feed_forward",
    )(hidden, weights, weights, weights)


def ffn_backward_kernel(dims, g_ref, wg_ref, wu_ref, wd_ref, slope_ref, act_ref, gg_ref, gu_ref, out_ref, acc):
    z = pl.program_id(0)
    grad_inner = dot(g_ref[...], whole_block(dims, wd_ref), 1, 0)
    gg = (grad_inner * slope_ref[...]).astype(BF)
    gu = (grad_inner * act_ref[...]).astype(BF)
    gg_ref[...] = gg
    gu_ref[...] = gu
    added = dot(gg, whole_block(dims, wg_ref), 1, 1) + dot(gu, whole_block(dims, wu_ref), 1, 1)
    add_up(z, added, acc, out_ref)


def ffn_backward(grad, weights, slope, act, dims, kind):
    rows, width = grad.shape
    nz, nb, _, nr, hs = weights.shape
    wspec = lambda m: pl.BlockSpec((1, nb, 1, nr, hs), lambda z: (z, 0, m, 0, 0))
    full = pl.BlockSpec((rows, width), lambda z: (0, 0))
    col = pl.BlockSpec((rows, hs), lambda z: (0, z))
    shape = jax.ShapeDtypeStruct
    return pl.pallas_call(
        functools.partial(ffn_backward_kernel, dims),
        out_shape=(
            shape((rows, nz * hs), BF),
            shape((rows, nz * hs), BF),
            shape((rows, width), kind),
        ),
        grid=(nz,),
        in_specs=[full, wspec(0), wspec(1), wspec(2), col, col],
        out_specs=[col, col, full],
        scratch_shapes=[pltpu.VMEM((rows, width), F32)],
        compiler_params=pltpu.CompilerParams(vmem_limit_bytes=56 * 2**20),
        cost_estimate=about(6),
        name="feed_forward_back",
    )(grad, weights, weights, weights, slope, act)


def weight_grad_kernel(dims, pieces, count, where, *refs):
    nf, nx, nc = dims
    lefts, rights = refs[:pieces], refs[pieces : pieces * (count + 1)]
    outs, (plain, flipped) = refs[pieces * (count + 1) : -2], refs[-2:]
    feat = plain.shape[0] // (nf * nx * nc)
    tokens = lefts[0].shape[0]

    @pl.when(pl.program_id(0) == 0)
    def _():
        for p, left in enumerate(lefts):
            plain[:, p * tokens : (p + 1) * tokens] = left[...].astype(F32).T.astype(BF)
        n = 0
        for dy in range(nf):
            for a in range(nx):
                row = ((where[0] ^ dy) * nx + a) * nc + where[1]
                flipped[n * feat : (n + 1) * feat, :] = plain[
                    pl.ds(pl.multiple_of(row * feat, feat), feat), :
                ]
                n += 1

    for i in range(count):
        right = jnp.concatenate([rights[i * pieces + p][...] for p in range(pieces)], axis=0)
        done = dot(flipped[...], right, 1, 0).astype(BF)
        for f in range(nf):
            outs[i * nf + f][0] = done[f * nx * feat : (f + 1) * nx * feat]


def weight_grad(lefts, rights, where, nz, dims):
    rows, width = lefts[0].shape
    nf, nx, nc = dims
    hs = rights[0][0].shape[1] // nz
    count, pieces = len(rights), len(lefts)
    shape = (nz, width // (nf * nc), hs)
    return pl.pallas_call(
        functools.partial(weight_grad_kernel, dims, pieces, count),
        out_shape=(jax.ShapeDtypeStruct(shape, BF),) * (count * nf),
        grid_spec=pltpu.PrefetchScalarGridSpec(
            num_scalar_prefetch=1,
            grid=(nz,),
            in_specs=[pl.BlockSpec((rows, width), lambda z, w: (0, 0))] * pieces
            + [pl.BlockSpec((rows, hs), lambda z, w: (0, z))] * (count * pieces),
            out_specs=[pl.BlockSpec((1,) + shape[1:], lambda z, w: (z, 0, 0))] * (count * nf),
            scratch_shapes=[
                pltpu.VMEM((width, rows * pieces), BF),
                pltpu.VMEM((width // nc, rows * pieces), BF),
            ],
        ),
        compiler_params=pltpu.CompilerParams(vmem_limit_bytes=56 * 2**20),
        cost_estimate=about(5),
        name="weight_grad",
    )(where, *lefts, *[r for right in rights for r in right])


def on_device(
    tokens, teacher, segment_ids, positions, valid_mask, valid_count, gain_attn, w_query, w_key,
    w_value, w_out, gain_ffn, w_gate, w_up, w_down,
):
    nf, nx, nc, nz = (lax.axis_size(a) for a in AXES)
    y, x, c, z = (lax.axis_index(a) for a in AXES)
    place = x * nc + c
    rows, width = tokens.shape[1:]
    share = rows // nz
    feat = w_query.shape[0]
    q_cols, kv_cols = w_query.shape[1], w_key.shape[1]
    heads_k = kv_cols // HD
    hidden_dev = w_gate.shape[1]
    hs = hidden_dev // nx
    own_rows = lambda v: lax.dynamic_slice_in_dim(v, z * share, share, 0)
    att_scale = HD ** (-0.5)

    qkv_cols = q_cols + 2 * kv_cols
    gains = jnp.pad(jnp.stack([gain_attn, gain_ffn]), ((0, 14), (0, qkv_cols - feat)))
    in_shard = jnp.concatenate([jnp.concatenate([w_query, w_key, w_value], axis=1), gains], axis=0)
    scale_a, normed_a = norm_parts(tokens[0].astype(F32))
    out_parts = everyone(w_out.T, "tp")
    out_shard = jnp.concatenate(out_parts, axis=1)
    out_y = swap(out_shard, "fsdp") if nf == 2 else out_shard
    (w_qkv, gain_rows), x_parts, came = gather_rows(in_shard, out_parts[1:] or None, (scale_a, out_y), feat)
    w_qkv = w_qkv.reshape(-1, qkv_cols)
    gain_rows = gain_rows[:, :2, :feat].astype(F32)
    gain_att, gain_mlp = (gain_rows[:, i].reshape(1, -1) for i in range(2))

    ffn_stack = after(jnp.stack([w_gate, w_up, w_down.T]), came[:2])
    hidden_part = lambda k: lax.dynamic_slice_in_dim(ffn_stack, (x ^ k) * hs, hs, 2)
    pieces = [hidden_part(0)] + [swap(hidden_part(k), "cx", k) for k in range(1, nx)]
    swapped = pieces[1:]
    pieces[1:] = after(pieces[1:], w_qkv) if nx > 1 else []
    ffn_shard = jnp.stack(ordered(pieces, x), axis=1).reshape(3 * nx * feat, hs)
    ffn_weights = lax.all_gather(ffn_shard, ("tp", "fsdp", "cc"), axis=0, tiled=True)
    ffn_weights = ffn_weights.reshape(nz, nf * nc, 3, nx * feat, hs)

    half = HD // 2
    frequency = jnp.exp(
        jnp.arange(half).astype(F32) * (-2.0 * math.log(ROPE_BASE) / HD)
    )
    angles = frequency[:, None] * positions[0].astype(F32)[None]
    cos_table, sin_table = jnp.cos(angles)[None], jnp.sin(angles)[None]

    hidden_a = (normed_a * gain_att).astype(BF)
    kv_lin = dot(w_qkv[:, q_cols:], hidden_a, 0, 1)
    k_rot = turned(kv_lin[:kv_cols].reshape(heads_k, HD, rows), cos_table, sin_table)
    kv_own = jnp.concatenate([k_rot.reshape(kv_cols, rows), kv_lin[kv_cols:]], axis=0).astype(BF)
    q_lin = dot(w_qkv[:, :q_cols], hidden_a, 0, 1)
    q_rot = turned(q_lin.reshape(-1, HD, rows), cos_table, sin_table).reshape(q_cols, rows).astype(BF)
    (out_weights,), out_x, out_came = gather_rows(out_shard, from_y=out_y, hold_x=came)
    out_weights = out_weights.reshape(width, -1)
    kv_parts = everyone(kv_own.reshape(2, kv_cols, rows), "cx")

    seg_own = after(segment_ids[0][None], kv_own)
    seg_parts = everyone(seg_own, "cx")
    seg_near = jnp.concatenate(ordered(seg_parts, x), axis=0)
    seg_all = jnp.stack(ordered(everyone(seg_near, "cc"), c), axis=1).reshape(1, -1)
    doc_start = jnp.sum((seg_all < segment_ids[0][:, None]).astype(jnp.int32), axis=1)[None]
    query_place = place * rows + jnp.arange(rows, dtype=jnp.int32)[None]

    q_rot = after(q_rot, out_weights)
    if nx > 1:
        kv_parts[1:] = after(kv_parts[1:], q_rot, doc_start)
    kv_near = jnp.stack(kv_parts)
    kv_sources = everyone(kv_near, "cc")
    kv_place = jnp.stack(
        [(x ^ dx) * nc + (c ^ dc) for dc in range(nc) for dx in range(nx)]
    ).astype(jnp.int32)

    first_row = place * rows
    o_t, o_f, lse = attn_fwd(
        q_rot, kv_sources, kv_place, doc_start, query_place,
        make_bounds(doc_start, first_row, rows, FWD_TQ, FWD_TK), FWD_TQ, FWD_TK,
    )

    chunk = lambda v, k: lax.dynamic_slice_in_dim(v, (z ^ k) * share, share, 1)
    att_t = jnp.concatenate(
        [chunk(o_t, 0)] + [swap(chunk(o_t, k), "tp", k) for k in range(1, nz)], axis=0
    )
    rows_own = own_rows(tokens[0]).astype(F32)
    resid = rows_own + dot(att_t, out_weights, 0, 1)
    scale_f, normed_f = norm_parts(resid)
    hidden_own = (normed_f * gain_mlp).astype(BF)
    dims = (nf, nx, nc)
    hidden_parts = everyone(hidden_own, "cx")
    done = []
    for k, h in enumerate(hidden_parts):
        hidden_parts[k] = after(h, done[-1]) if k else h
        done.append(ffn_forward(hidden_parts[k], ffn_weights, dims, BF if k else F32))
    slopes, acts, inners, outs = zip(*done)

    def returned(parts, *others):
        total = parts[0]
        for k in range(1, nx):
            back = swap(parts[k], "cx", k)
            total = total + (after(back, *others) if others else back).astype(F32)
        return total

    result = resid + returned(outs)
    target = own_rows(teacher[0]).astype(F32)
    valid = own_rows(valid_mask[0].astype(F32)[:, None])
    error = result - target
    grad_out = valid * error
    loss_part = jnp.sum(grad_out * error)
    grad_out_low, result_low = after((grad_out.astype(BF), result.astype(BF)), loss_part[None])
    ffn_grads = everyone(grad_out_low, "cx")
    where = jnp.stack([y, c]).astype(jnp.int32)
    mixed = lax.all_gather(result_low, "tp", axis=0, tiled=True)

    def both_cores(parts):
        return [v for part in parts for v in everyone(part, "cc")]

    def to_rows(parts, *others):
        own, sends = parts[0], list(parts[1:])
        if others and sends:
            sends = after(sends, *others)
        return own, sends, [swap(sends[k - 1], "fsdp", k) for k in range(1, nf)]

    def scattered(own, given, hold):
        total = own.astype(F32)
        for k in range(1, nf):
            total = total + after(given[k - 1], hold).astype(F32)
        total = total.astype(BF)
        return (total,) + spread(total)

    def spread(total):
        done = lax.psum_scatter(
            total.reshape(nz * nx * feat, hs), "tp", scatter_dimension=0, tiled=True
        ).reshape(nx, feat, hs)
        piece = lambda k: lax.dynamic_index_in_dim(done, x ^ k, 0, keepdims=False)
        pieces = [piece(0)] + [swap(piece(k), "cx", k) for k in range(1, nx)]
        return done, jnp.concatenate(ordered(pieces, x), axis=1).astype(F32)

    done = []
    for k, g in enumerate(ffn_grads):
        ffn_grads[k] = after(g, done[-1]) if k else g
        done.append(ffn_backward(ffn_grads[k], ffn_weights, slopes[k], acts[k], dims, BF if k else F32))
    grad_gates, grad_ups, ffn_backs = zip(*done)
    inners = both_cores(inners)
    inners[0] = after(inners[0], ffn_backs[-1])
    part_down = weight_grad(both_cores(ffn_grads), [inners], where, nz, dims)
    grad_gates, grad_ups = both_cores(grad_gates), both_cores(grad_ups)
    grad_gates[0] = after(grad_gates[0], part_down)
    part_gate_up = weight_grad(both_cores(hidden_parts), [grad_gates, grad_ups], where, nz, dims)
    down_own, down_sends, down_given = to_rows(part_down)
    grad_hidden_f = returned(ffn_backs, down_sends, part_gate_up)
    part_gain_mlp = jnp.sum(grad_hidden_f * normed_f, axis=0)
    grad_mid = grad_out + norm_back(grad_hidden_f, normed_f, scale_f, gain_mlp)
    grad_attn = after(grad_mid.astype(BF), mixed)
    g_att = dot(out_weights, grad_attn, 0, 1).astype(BF).reshape(nz, q_cols, share)
    g_parts = [g_att[0]] + [swap(g_att[k], "tp", k) for k in range(1, nz)]
    down_total, down_done, shard_down_t = scattered(down_own, down_given, g_parts[1:])
    gate_own, gate_sends, gate_given = to_rows(part_gate_up[:nf], down_given)
    up_own, up_sends, up_given = to_rows(part_gate_up[nf:], gate_given)
    grad_heads = jnp.concatenate(ordered(after(g_parts, down_total, gate_sends), z), axis=1)

    bounds = make_bounds(doc_start, first_row, rows, BWD_TQ, BWD_TK)
    dqs, kv_sends, kv_grads = [], [], []
    for head in range(heads_k):
        dq, *dkv = attn_bwd(
            q_rot, kv_sources, kv_place, doc_start, query_place, bounds, grad_heads, o_f, lse,
            BWD_TQ, BWD_TK, head,
        )
        if head == heads_k - 1 and head:
            dkv[-1] = after(dkv[-1], gate_done, [o for _, o in kv_sends])
        dkv_others = [swap(dkv[k], "cc", k) for k in range(1, nc)]

        def kv_over_cores(k):
            total = dkv[0][k].astype(F32)
            for other in dkv_others:
                total = total + other[k].astype(F32)
            return total

        sends = [kv_over_cores(k).astype(BF) for k in range(1, nx)]
        if head == 0 and heads_k > 1:
            gate_total, gate_done, shard_gate = scattered(gate_own, gate_given, sends)
            grad_heads = after(grad_heads, sends, gate_total, up_sends, down_done)
        dqs.append(dq)
        kv_sends.append((kv_over_cores(0), [swap(sends[k - 1], "cx", k) for k in range(1, nx)]))
    if heads_k == 1:
        gate_total, gate_done, shard_gate = scattered(gate_own, gate_given, sends)
    gq = jnp.concatenate([turned(d.reshape(-1, HD, rows) * att_scale, cos_table, -sin_table) for d in dqs])
    gq = gq.reshape(q_cols, rows).astype(BF)
    up_total, up_done, shard_up = scattered(up_own, up_given, [kv_sends[0][1], dq])
    for kv_grad, others in kv_sends:
        for other in others:
            kv_grad = kv_grad + after(other, up_total).astype(F32)
        kv_grads.append(kv_grad)
    kv_grad = jnp.stack(kv_grads, axis=1)
    gk = turned(kv_grad[0] * att_scale, cos_table, -sin_table)
    gkv = jnp.concatenate([gk, kv_grad[1]], axis=0).reshape(2 * kv_cols, rows).astype(BF)
    grad_qkv = jnp.concatenate([gq, gkv], axis=0)
    part_h1 = dot(grad_qkv, w_qkv, 0, 1).astype(BF)
    part_h1 = after(part_h1, up_done)
    grad_hidden_a = lax.psum_scatter(part_h1, "tp", scatter_dimension=0, tiled=True)
    part_out = dot(after(grad_attn, sends), att_t, 0, 1).astype(BF)
    part_qkv = dot(after(hidden_a, part_h1), grad_qkv, 0, 1).astype(BF)
    shard_out_t, out_y = scatter_rows(part_out)
    shard_qkv, qkv_y = scatter_rows(part_qkv)
    shard_out_t = summed(
        shard_out_t.astype(BF).reshape(feat, nz, q_cols), 1, "tp", 0
    )
    grad_hidden_a = after(grad_hidden_a, out_y, qkv_y).astype(F32)
    scale_share = own_rows(scale_a)
    normed_share = rows_own * scale_share
    part_gain_att = jnp.sum(grad_hidden_a * normed_share, axis=0)
    grad_share = grad_mid + norm_back(grad_hidden_a, normed_share, scale_share, gain_att)
    grad_share = grad_share.astype(BF)
    grad_tokens = lax.all_gather(grad_share, "tp", axis=0, tiled=True)

    small = jnp.stack([part_gain_att, part_gain_mlp, jnp.broadcast_to(loss_part, (width,))])
    small = after(small, grad_share)
    for axis in AXES:
        step = 1
        while step < lax.axis_size(axis):
            small = small + swap(small, axis, step)
            step *= 2
    small_own = lax.dynamic_slice_in_dim(small[:2], ((y * nx + x) * nc + c) * feat, feat, 1)
    loss = small[2, 0] / (valid_count.astype(F32) * width)

    grad_tokens = after(
        grad_tokens, small_own, shard_qkv, shard_out_t, shard_gate, shard_up, shard_down_t
    ).astype(F32)
    return (
        mixed[None],
        loss,
        grad_tokens[None],
        small_own[0],
        shard_qkv[:, :q_cols],
        shard_qkv[:, q_cols : q_cols + kv_cols],
        shard_qkv[:, q_cols + kv_cols :],
        shard_out_t.T,
        small_own[1],
        shard_gate,
        shard_up,
        shard_down_t.T,
    )


FWD_TQ, FWD_TK = 256, 1024
BWD_TQ, BWD_TK = 256, 512


def solution(mesh):
    nf, nctx, nz = (mesh.shape[a] for a in ("fsdp", "ctx", "tp"))
    nc = 2 if nctx % 2 == 0 else 1
    fine = Mesh(mesh.devices.reshape(nf, nctx // nc, nc, nz), AXES)
    ctx = ("cx", "cc")
    rows = ("fsdp", "cx", "cc")
    return jax.shard_map(
        on_device,
        mesh=fine,
        in_specs=(
            P("fsdp", ctx, None),
            P("fsdp", ctx, None),
            P("fsdp", ctx),
            P("fsdp", ctx),
            P("fsdp", ctx),
            P(),
            P(rows),
            P(rows, "tp"),
            P(rows, "tp"),
            P(rows, "tp"),
            P("tp", rows),
            P(rows),
            P(rows, "tp"),
            P(rows, "tp"),
            P("tp", rows),
        ),
        out_specs=(
            P("fsdp", ctx, None),
            P(),
            P("fsdp", ctx, None),
            P(rows),
            P(rows, "tp"),
            P(rows, "tp"),
            P(rows, "tp"),
            P("tp", rows),
            P(rows),
            P(rows, "tp"),
            P(rows, "tp"),
            P("tp", rows),
        ),
        check_vma=False,
    )
```

```python
import functools
import math

import jax
import jax.numpy as jnp
from jax import lax
from jax.experimental import pallas as pl
from jax.experimental.pallas import tpu as pltpu
from jax.sharding import Mesh
from jax.sharding import PartitionSpec as P

HD=96
NO_COST = pl.CostEstimate(flops=0, bytes_accessed=0, transcendentals=0)


def about(us):
    return pl.CostEstimate(flops=us*10**9, bytes_accessed=10**6, transcendentals=0)
NEG=-1e30
F32=jnp.float32; BF=jnp.bfloat16
def dot(a,b,ca,cb):
    return lax.dot_general(a,b,(((ca,),(cb,)),((),())),preferred_element_type=F32)

def load_blocks(place, sources, keys_t, keys, values_t, values):
    n = 0
    for source in sources:
        width = source.shape[3]
        for b in range(source.shape[0]):
            at = pl.ds(pl.multiple_of(place[n]*width, width), width)
            n += 1
            if keys_t is not None:
                keys_t[:, at] = source[b, 0]
            keys[at, :] = source[b, 0].astype(F32).T.astype(BF)
            if values_t is not None:
                values_t[:, at] = source[b, 1]
            if values is not None:
                values[at, :] = source[b, 1].astype(F32).T.astype(BF)

def fwd_kernel(scale2, tq, tk, group, count, bounds, place, q_ref, *refs):
    sources, (st_ref, qp_ref, o_ref, of_ref, lse_ref, ks, v_ref, m_s, l_s, acc) = refs[:count], refs[count:]
    i = pl.program_id(1)
    @pl.when(i == 0)
    def _():
        load_blocks(place, sources, None, ks, v_ref, None)
    q2 = jnp.concatenate([q_ref[h*HD:(h+1)*HD, :] for h in range(group)], axis=1)
    st = jnp.concatenate([st_ref[...]]*group, axis=1)
    qp = jnp.concatenate([qp_ref[...]]*group, axis=1)
    m_s[...] = jnp.full_like(m_s, NEG)
    l_s[...] = jnp.zeros_like(l_s)
    acc[...] = jnp.zeros_like(acc)
    def step(masked, j, _):
        off = pl.multiple_of(j*tk, tk)
        s = dot(ks[pl.ds(off, tk), :], q2, 1, 0)
        if masked:
            kid = off + lax.broadcasted_iota(jnp.int32, s.shape, 0)
            s = jnp.where((kid >= st) & (kid <= qp), s, NEG)
        m_old = m_s[...]
        m_new = jnp.maximum(m_old, jnp.max(s, axis=0, keepdims=True))
        p = jnp.exp2((s - m_new)*scale2)
        al = jnp.exp2((m_old - m_new)*scale2)
        l_s[...] = l_s[...]*al + jnp.sum(p, axis=0, keepdims=True)
        m_s[...] = m_new
        acc[...] = acc[...]*al + dot(v_ref[:, pl.ds(off, tk)], p.astype(BF), 1, 0)
        return 0
    lo, a, b, hi = bounds[i,0], bounds[i,1], bounds[i,2], bounds[i,3]
    lax.fori_loop(lo, a, functools.partial(step, True), 0)
    lax.fori_loop(a, b, functools.partial(step, False), 0)
    lax.fori_loop(b, hi, functools.partial(step, True), 0)
    o = acc[...]/l_s[...]
    lse = m_s[...]*scale2 + jnp.log2(l_s[...])
    for h in range(group):
        oh = o[:, h*tq:(h+1)*tq]
        of_ref[h*HD:(h+1)*HD, :] = oh
        o_ref[h*HD:(h+1)*HD, :] = oh.astype(BF)
        lse_ref[0, h:h+1, :] = lse[:, h*tq:(h+1)*tq]

def kv_spec(source):
    return pl.BlockSpec((source.shape[0], 2, HD, source.shape[3]), lambda g,i,*_:(0,0,g,0))

def attn_fwd(qT, kv_sources, place, start, qpos, bounds, tq=256, tk=512):
    T = qT.shape[1]; kv = kv_sources[0].shape[2]//HD; group = qT.shape[0]//HD//kv
    N = sum(s.shape[0] for s in kv_sources)*T
    scale2 = HD**-0.5*math.log2(math.e)
    qs = pl.BlockSpec((group*HD, tq), lambda g,i,*_:(g,i))
    row = pl.BlockSpec((1, tq), lambda g,i,*_:(0,i))
    return pl.pallas_call(
        functools.partial(fwd_kernel, scale2, tq, tk, group, len(kv_sources)),
        out_shape=(jax.ShapeDtypeStruct(qT.shape, BF), jax.ShapeDtypeStruct(qT.shape, F32), jax.ShapeDtypeStruct((kv, group, T), F32)),
        grid_spec=pltpu.PrefetchScalarGridSpec(num_scalar_prefetch=2, grid=(kv, T//tq),
            in_specs=[qs] + [kv_spec(s) for s in kv_sources] + [row, row],
            out_specs=[qs, qs, pl.BlockSpec((1, group, tq), lambda g,i,*_:(g,0,i))],
            scratch_shapes=[pltpu.VMEM((N,HD),BF), pltpu.VMEM((HD,N),BF), pltpu.VMEM((1,group*tq),F32), pltpu.VMEM((1,group*tq),F32), pltpu.VMEM((HD,group*tq),F32)]),
        compiler_params=pltpu.CompilerParams(vmem_limit_bytes=48*2**20),
        cost_estimate=about(12),
        name="attend",
    )(bounds, place, qT, *kv_sources, start, qpos)

def bwd_kernel(scale2, tq, tk, group, count, bounds, place, q_ref, *refs):
    sources, (st_ref, qp_ref, g_ref, of_ref, lse_ref, dq_ref) = refs[:count], refs[count:count+6]
    dkv_refs, (k_ref, ks, vs, dks, dvs, dqs) = refs[count+6:2*count+6], refs[2*count+6:]
    i = pl.program_id(1)
    @pl.when(i == 0)
    def _():
        load_blocks(place, sources, k_ref, ks, None, vs)
        dks[...] = jnp.zeros_like(dks)
        dvs[...] = jnp.zeros_like(dvs)
    cat = lambda f: jnp.concatenate([f(h) for h in range(group)], axis=1)
    q2 = cat(lambda h: q_ref[h*HD:(h+1)*HD, :])
    g2 = cat(lambda h: g_ref[h*HD:(h+1)*HD, :])
    lse = cat(lambda h: lse_ref[0, h:h+1, :])
    delta = cat(lambda h: jnp.sum(g_ref[h*HD:(h+1)*HD, :].astype(F32)*of_ref[h*HD:(h+1)*HD, :], axis=0, keepdims=True))
    st = cat(lambda h: st_ref[...])
    qp = cat(lambda h: qp_ref[...])
    dqs[...] = jnp.zeros_like(dqs)
    def step(masked, j, _):
        off = pl.multiple_of(j*tk, tk)
        s = dot(ks[pl.ds(off, tk), :], q2, 1, 0)
        if masked:
            kid = off + lax.broadcasted_iota(jnp.int32, s.shape, 0)
            s = jnp.where((kid >= st) & (kid <= qp), s, NEG)
        p = jnp.exp2(s*scale2 - lse)
        dp = dot(vs[pl.ds(off, tk), :], g2, 1, 0)
        ds = (p*(dp - delta)).astype(BF)
        dvs[:, pl.ds(off, tk)] += dot(g2, p.astype(BF), 1, 1)
        dks[:, pl.ds(off, tk)] += dot(q2, ds, 1, 1)
        dqs[...] += dot(k_ref[:, pl.ds(off, tk)], ds, 1, 0)
        return 0
    lo, a, b, hi = bounds[i,0], bounds[i,1], bounds[i,2], bounds[i,3]
    lax.fori_loop(lo, a, functools.partial(step, True), 0)
    lax.fori_loop(a, b, functools.partial(step, False), 0)
    lax.fori_loop(b, hi, functools.partial(step, True), 0)
    for h in range(group):
        dq_ref[h*HD:(h+1)*HD, :] = dqs[:, h*tq:(h+1)*tq]
    @pl.when(i == pl.num_programs(1)-1)
    def _():
        n = 0
        for dkv_ref in dkv_refs:
            width = dkv_ref.shape[3]
            for b in range(dkv_ref.shape[0]):
                at = pl.ds(pl.multiple_of(place[n]*width, width), width)
                n += 1
                dkv_ref[b, 0] = dks[:, at].astype(BF)
                dkv_ref[b, 1] = dvs[:, at].astype(BF)

def attn_bwd(qT, kv_sources, place, start, qpos, bounds, gT, of, lse, tq, tk, head):
    T = qT.shape[1]; kv = kv_sources[0].shape[2]//HD; group = qT.shape[0]//HD//kv
    N = sum(s.shape[0] for s in kv_sources)*T
    scale2 = HD**-0.5*math.log2(math.e)
    qs = pl.BlockSpec((group*HD, tq), lambda g,i,*_:(head,i))
    row = pl.BlockSpec((1, tq), lambda g,i,*_:(0,i))
    kv_in = [pl.BlockSpec((s.shape[0], 2, HD, T), lambda g,i,*_:(0,0,head,0)) for s in kv_sources]
    kv_out = [pl.BlockSpec((s.shape[0], 2, HD, T), lambda g,i,*_:(0,0,0,0)) for s in kv_sources]
    return pl.pallas_call(
        functools.partial(bwd_kernel, scale2, tq, tk, group, len(kv_sources)),
        out_shape=[jax.ShapeDtypeStruct((group*HD, T), F32)] + [jax.ShapeDtypeStruct((s.shape[0], 2, HD, T), BF) for s in kv_sources],
        grid_spec=pltpu.PrefetchScalarGridSpec(num_scalar_prefetch=2, grid=(1, T//tq),
            in_specs=[qs] + kv_in + [row, row, qs, qs, pl.BlockSpec((1, group, tq), lambda g,i,*_:(head,0,i))],
            out_specs=[pl.BlockSpec((group*HD, tq), lambda g,i,*_:(0,i))] + kv_out,
            scratch_shapes=[pltpu.VMEM((HD,N),BF), pltpu.VMEM((N,HD),BF), pltpu.VMEM((N,HD),BF), pltpu.VMEM((HD,N),F32), pltpu.VMEM((HD,N),F32), pltpu.VMEM((HD,group*tq),F32)]),
        compiler_params=pltpu.CompilerParams(vmem_limit_bytes=56*2**20),
        cost_estimate=about(12),
        name="attend_back",
    )(bounds, place, qT, *kv_sources, start, qpos, gT, of, lse)

def make_bounds(start, q_first, T, tq, tk):
    s = start.reshape(-1, tq)
    first = q_first + jnp.arange(T//tq, dtype=jnp.int32)*tq
    lo = s[:,0]//tk
    hi = (first + tq - 1)//tk + 1
    a = jnp.minimum((s[:,-1] + tk - 1)//tk, hi)
    b = jnp.maximum(first//tk, a)
    return jnp.stack([lo,a,b,hi],axis=1).astype(jnp.int32)

EPSILON = 1e-05
ROPE_BASE = 100000.0
AXES = ("fsdp", "cx", "cc", "tp")


def swap(values, axis, step=1):
    size = lax.axis_size(axis)
    return lax.ppermute(values, axis, [(i, i ^ step) for i in range(size)])


def after_kernel(*refs):
    pass


def after(values, *others):
    values, tree = jax.tree.flatten(values)
    others = jax.tree.leaves(others)
    done = pl.pallas_call(
        after_kernel,
        out_shape=[jax.ShapeDtypeStruct(v.shape, v.dtype) for v in values],
        in_specs=[pl.BlockSpec(memory_space=pl.ANY)] * (len(values) + len(others)),
        out_specs=[pl.BlockSpec(memory_space=pl.ANY)] * len(values),
        input_output_aliases={i: i for i in range(len(values))},
        cost_estimate=NO_COST,
        name="after",
    )(*values, *others)
    return jax.tree.unflatten(tree, list(done))


def ordered(parts, index):
    if len(parts) == 1:
        return list(parts)
    if len(parts) == 2:
        first = index == 0
        return [jnp.where(first, parts[0], parts[1]), jnp.where(first, parts[1], parts[0])]
    stacked = jnp.stack(parts)
    return [
        lax.dynamic_index_in_dim(stacked, jnp.bitwise_xor(index, a), 0, keepdims=False)
        for a in range(len(parts))
    ]


def everyone(values, axis):
    return [values] + [swap(values, axis, k) for k in range(1, lax.axis_size(axis))]


def place_kernel(plan, count, place, *refs):
    sources, outs, sems = refs[:count], refs[count:-1], refs[-1]
    copies = [
        pltpu.make_async_copy(
            sources[source].at[pl.ds(first, n)], outs[out].at[place[spot], pl.ds(row, n)], sems.at[i]
        )
        for i, (source, first, n, out, spot, row) in enumerate(plan)
    ]
    for copy in copies:
        copy.start()
    for copy in copies:
        copy.wait()


def put_blocks(pieces, place, rows, cut=None):
    width, kind = pieces[0][0].shape[1], pieces[0][0].dtype
    cuts = [0, rows] if cut is None else [0, cut, rows]
    sources, plan = [], []
    for array, first, n, spot, row in pieces:
        known = [i for i, s in enumerate(sources) if s is array]
        if not known:
            known = [len(sources)]
            sources.append(array)
        for out, (low, high) in enumerate(zip(cuts[:-1], cuts[1:])):
            a, b = max(row, low), min(row + n, high)
            if a < b:
                plan.append((known[0], first + a - row, b - a, out, spot, a - low))
    return pl.pallas_call(
        functools.partial(place_kernel, plan, len(sources)),
        out_shape=[
            jax.ShapeDtypeStruct((len(place), b - a, width), kind) for a, b in zip(cuts[:-1], cuts[1:])
        ],
        in_specs=[pl.BlockSpec(memory_space=pltpu.SMEM)]
        + [pl.BlockSpec(memory_space=pltpu.VMEM)] * len(sources),
        out_specs=[pl.BlockSpec(memory_space=pl.ANY)] * (len(cuts) - 1),
        scratch_shapes=[pltpu.SemaphoreType.DMA((len(plan),))],
        compiler_params=pltpu.CompilerParams(vmem_limit_bytes=32 * 2**20),
        cost_estimate=about(2),
        name="put_blocks",
    )(jnp.stack(place).astype(jnp.int32), *sources)


def gather_rows(shard, hold_near=None, hold_core=None, cut=None, from_y=None, hold_x=None):
    rows, width = shard.shape
    nf, nx, nc = (lax.axis_size(a) for a in ("fsdp", "cx", "cc"))
    y, x, c = (lax.axis_index(a) for a in ("fsdp", "cx", "cc"))
    if nf == 2 and nx == 2:
        half = rows // 2 // 16 * 16
        from_x = swap(shard if hold_x is None else after(shard, hold_x), "cx")
        if from_y is None:
            from_y = swap(shard, "fsdp")
        top = swap(from_y[:half], "cx")
        low = swap(from_x[half:], "fsdp")
        x_parts = [shard, from_x]
        came = [from_x, from_y, top, low]
        if hold_near is not None:
            top, low = after((top, low), hold_near)
        own = [
            (shard, 0, rows, 0, 0),
            (from_x, 0, rows, 1, 0),
            (from_y, 0, rows, 2, 0),
            (top, 0, half, 3, 0),
            (low, 0, rows - half, 3, half),
        ]
    else:
        x_parts = everyone(shard, "cx")
        near = jnp.concatenate(x_parts, axis=0)
        near = jnp.concatenate(everyone(near, "fsdp"), axis=0)
        came = [near]
        own = [(near, i * rows, rows, i, 0) for i in range(nf * nx)]
    pieces = list(own)
    for k in range(1, nc):
        given = {}
        for array, first, n, spot, row in own:
            if id(array) not in given:
                given[id(array)] = swap(array, "cc", k)
                last = id(array)
        if hold_core is not None:
            given[last] = after(given[last], hold_core)
        pieces += [(given[id(a)], first, n, spot + k * nf * nx, row) for a, first, n, spot, row in own]
    place = [
        ((y ^ dy) * nx + (x ^ dx)) * nc + (c ^ dc)
        for dc in range(nc)
        for dy in range(nf)
        for dx in range(nx)
    ]
    return put_blocks(pieces, place, rows, cut), x_parts, came


def scatter_rows(part):
    nf, nx, nc = (lax.axis_size(a) for a in ("fsdp", "cx", "cc"))
    y, x, c = (lax.axis_index(a) for a in ("fsdp", "cx", "cc"))
    width = part.shape[1]
    total = part.reshape(nf, nx, nc, -1, width)
    on_chip = summed(total, 2, "cc", c).astype(jnp.bfloat16)
    on_y = summed(on_chip, 0, "fsdp", y).astype(jnp.bfloat16)
    total = summed(on_y, 0, "cx", x)
    return total, on_y


def summed(part, dim, axis, index):
    take = lambda k: lax.dynamic_index_in_dim(part, index ^ k, dim, keepdims=False)
    total = take(0).astype(jnp.float32)
    for k in range(1, lax.axis_size(axis)):
        total = total + swap(take(k), axis, k).astype(jnp.float32)
    return total


def norm_parts(values):
    factor = lax.rsqrt(jnp.mean(values * values, axis=-1, keepdims=True) + EPSILON)
    return (factor, values * factor)


def norm_back(grad_normed_in, normed, factor, gain_vec):
    grad_normed = grad_normed_in * gain_vec
    return factor * (grad_normed - normed * jnp.mean(grad_normed * normed, axis=-1, keepdims=True))


def turned(values, cos_table, sin_table):
    half = values.shape[1] // 2
    low, high = values[:, :half], values[:, half:]
    return jnp.concatenate(
        [low * cos_table - high * sin_table, high * cos_table + low * sin_table], axis=1
    )


def whole_block(dims, ref):
    nf, nx, nc = dims
    feat = ref.shape[3] // nx
    return jnp.concatenate(
        [
            ref[0, f * nc + b, 0, a * feat : (a + 1) * feat, :]
            for f in range(nf)
            for a in range(nx)
            for b in range(nc)
        ],
        axis=0,
    )


def ffn_forward_kernel(dims, h_ref, wg_ref, wu_ref, wd_ref, slope_ref, act_ref, inner_ref, out_ref, acc):
    z = pl.program_id(0)
    hidden = h_ref[...]
    gate = dot(hidden, whole_block(dims, wg_ref), 1, 0)
    up = dot(hidden, whole_block(dims, wu_ref), 1, 0)
    sig = jax.nn.sigmoid(gate)
    act = gate * sig
    slope_ref[...] = (up * (sig * (1.0 + gate * (1.0 - sig)))).astype(BF)
    act_ref[...] = act.astype(BF)
    inner = (act * up).astype(BF)
    inner_ref[...] = inner
    add_up(z, dot(inner, whole_block(dims, wd_ref), 1, 1), acc, out_ref)


def add_up(z, added, acc, out_ref):
    @pl.when(z == 0)
    def _():
        acc[...] = added

    @pl.when(z > 0)
    def _():
        acc[...] += added

    @pl.when(z == pl.num_programs(0) - 1)
    def _():
        out_ref[...] = acc[...].astype(out_ref.dtype)


def ffn_forward(hidden, weights, dims, kind):
    rows, width = hidden.shape
    nz, nb, _, nr, hs = weights.shape
    wspec = lambda m: pl.BlockSpec((1, nb, 1, nr, hs), lambda z: (z, 0, m, 0, 0))
    full = pl.BlockSpec((rows, width), lambda z: (0, 0))
    col = pl.BlockSpec((rows, hs), lambda z: (0, z))
    shape = jax.ShapeDtypeStruct
    return pl.pallas_call(
        functools.partial(ffn_forward_kernel, dims),
        out_shape=(
            shape((rows, nz * hs), BF),
            shape((rows, nz * hs), BF),
            shape((rows, nz * hs), BF),
            shape((rows, width), kind),
        ),
        grid=(nz,),
        in_specs=[full, wspec(0), wspec(1), wspec(2)],
        out_specs=[col, col, col, full],
        scratch_shapes=[pltpu.VMEM((rows, width), F32)],
        compiler_params=pltpu.CompilerParams(vmem_limit_bytes=56 * 2**20),
        cost_estimate=about(6),
        name="feed_forward",
    )(hidden, weights, weights, weights)


def ffn_backward_kernel(dims, g_ref, wg_ref, wu_ref, wd_ref, slope_ref, act_ref, gg_ref, gu_ref, out_ref, acc):
    z = pl.program_id(0)
    grad_inner = dot(g_ref[...], whole_block(dims, wd_ref), 1, 0)
    gg = (grad_inner * slope_ref[...]).astype(BF)
    gu = (grad_inner * act_ref[...]).astype(BF)
    gg_ref[...] = gg
    gu_ref[...] = gu
    added = dot(gg, whole_block(dims, wg_ref), 1, 1) + dot(gu, whole_block(dims, wu_ref), 1, 1)
    add_up(z, added, acc, out_ref)


def ffn_backward(grad, weights, slope, act, dims, kind):
    rows, width = grad.shape
    nz, nb, _, nr, hs = weights.shape
    wspec = lambda m: pl.BlockSpec((1, nb, 1, nr, hs), lambda z: (z, 0, m, 0, 0))
    full = pl.BlockSpec((rows, width), lambda z: (0, 0))
    col = pl.BlockSpec((rows, hs), lambda z: (0, z))
    shape = jax.ShapeDtypeStruct
    return pl.pallas_call(
        functools.partial(ffn_backward_kernel, dims),
        out_shape=(
            shape((rows, nz * hs), BF),
            shape((rows, nz * hs), BF),
            shape((rows, width), kind),
        ),
        grid=(nz,),
        in_specs=[full, wspec(0), wspec(1), wspec(2), col, col],
        out_specs=[col, col, full],
        scratch_shapes=[pltpu.VMEM((rows, width), F32)],
        compiler_params=pltpu.CompilerParams(vmem_limit_bytes=56 * 2**20),
        cost_estimate=about(6),
        name="feed_forward_back",
    )(grad, weights, weights, weights, slope, act)


def weight_grad_kernel(dims, pieces, count, where, *refs):
    nf, nx, nc = dims
    lefts, rights = refs[:pieces], refs[pieces : pieces * (count + 1)]
    outs, (plain, flipped) = refs[pieces * (count + 1) : -2], refs[-2:]
    feat = plain.shape[0] // (nf * nx * nc)
    tokens = lefts[0].shape[0]

    @pl.when(pl.program_id(0) == 0)
    def _():
        for p, left in enumerate(lefts):
            plain[:, p * tokens : (p + 1) * tokens] = left[...].astype(F32).T.astype(BF)
        n = 0
        for dy in range(nf):
            for a in range(nx):
                row = ((where[0] ^ dy) * nx + a) * nc + where[1]
                flipped[n * feat : (n + 1) * feat, :] = plain[
                    pl.ds(pl.multiple_of(row * feat, feat), feat), :
                ]
                n += 1

    for i in range(count):
        right = jnp.concatenate([rights[i * pieces + p][...] for p in range(pieces)], axis=0)
        done = dot(flipped[...], right, 1, 0).astype(BF)
        for f in range(nf):
            outs[i * nf + f][0] = done[f * nx * feat : (f + 1) * nx * feat]


def weight_grad(lefts, rights, where, nz, dims):
    rows, width = lefts[0].shape
    nf, nx, nc = dims
    hs = rights[0][0].shape[1] // nz
    count, pieces = len(rights), len(lefts)
    shape = (nz, width // (nf * nc), hs)
    return pl.pallas_call(
        functools.partial(weight_grad_kernel, dims, pieces, count),
        out_shape=(jax.ShapeDtypeStruct(shape, BF),) * (count * nf),
        grid_spec=pltpu.PrefetchScalarGridSpec(
            num_scalar_prefetch=1,
            grid=(nz,),
            in_specs=[pl.BlockSpec((rows, width), lambda z, w: (0, 0))] * pieces
            + [pl.BlockSpec((rows, hs), lambda z, w: (0, z))] * (count * pieces),
            out_specs=[pl.BlockSpec((1,) + shape[1:], lambda z, w: (z, 0, 0))] * (count * nf),
            scratch_shapes=[
                pltpu.VMEM((width, rows * pieces), BF),
                pltpu.VMEM((width // nc, rows * pieces), BF),
            ],
        ),
        compiler_params=pltpu.CompilerParams(vmem_limit_bytes=56 * 2**20),
        cost_estimate=about(5),
        name="weight_grad",
    )(where, *lefts, *[r for right in rights for r in right])


def on_device(
    tokens, teacher, segment_ids, positions, valid_mask, valid_count, gain_attn, w_query, w_key,
    w_value, w_out, gain_ffn, w_gate, w_up, w_down,
):
    nf, nx, nc, nz = (lax.axis_size(a) for a in AXES)
    y, x, c, z = (lax.axis_index(a) for a in AXES)
    place = x * nc + c
    rows, width = tokens.shape[1:]
    share = rows // nz
    feat = w_query.shape[0]
    q_cols, kv_cols = w_query.shape[1], w_key.shape[1]
    heads_k = kv_cols // HD
    hidden_dev = w_gate.shape[1]
    hs = hidden_dev // nx
    own_rows = lambda v: lax.dynamic_slice_in_dim(v, z * share, share, 0)
    att_scale = HD ** (-0.5)

    qkv_cols = q_cols + 2 * kv_cols
    gains = jnp.pad(jnp.stack([gain_attn, gain_ffn]), ((0, 14), (0, qkv_cols - feat)))
    in_shard = jnp.concatenate([jnp.concatenate([w_query, w_key, w_value], axis=1), gains], axis=0)
    scale_a, normed_a = norm_parts(tokens[0].astype(F32))
    out_parts = everyone(w_out.T, "tp")
    out_shard = jnp.concatenate(out_parts, axis=1)
    out_y = swap(out_shard, "fsdp") if nf == 2 else out_shard
    (w_qkv, gain_rows), x_parts, came = gather_rows(in_shard, out_parts[1:] or None, (scale_a, out_y), feat)
    w_qkv = w_qkv.reshape(-1, qkv_cols)
    gain_rows = gain_rows[:, :2, :feat].astype(F32)
    gain_att, gain_mlp = (gain_rows[:, i].reshape(1, -1) for i in range(2))

    ffn_stack = after(jnp.stack([w_gate, w_up, w_down.T]), came[:2])
    hidden_part = lambda k: lax.dynamic_slice_in_dim(ffn_stack, (x ^ k) * hs, hs, 2)
    pieces = [hidden_part(0)] + [swap(hidden_part(k), "cx", k) for k in range(1, nx)]
    swapped = pieces[1:]
    pieces[1:] = after(pieces[1:], w_qkv) if nx > 1 else []
    ffn_shard = jnp.stack(ordered(pieces, x), axis=1).reshape(3 * nx * feat, hs)
    ffn_weights = lax.all_gather(ffn_shard, ("tp", "fsdp", "cc"), axis=0, tiled=True)
    ffn_weights = ffn_weights.reshape(nz, nf * nc, 3, nx * feat, hs)

    half = HD // 2
    frequency = jnp.exp(
        jnp.arange(half).astype(F32) * (-2.0 * math.log(ROPE_BASE) / HD)
    )
    angles = frequency[:, None] * positions[0].astype(F32)[None]
    cos_table, sin_table = jnp.cos(angles)[None], jnp.sin(angles)[None]

    hidden_a = (normed_a * gain_att).astype(BF)
    kv_lin = dot(w_qkv[:, q_cols:], hidden_a, 0, 1)
    k_rot = turned(kv_lin[:kv_cols].reshape(heads_k, HD, rows), cos_table, sin_table)
    kv_own = jnp.concatenate([k_rot.reshape(kv_cols, rows), kv_lin[kv_cols:]], axis=0).astype(BF)
    q_lin = dot(w_qkv[:, :q_cols], hidden_a, 0, 1)
    q_rot = turned(q_lin.reshape(-1, HD, rows), cos_table, sin_table).reshape(q_cols, rows).astype(BF)
    (out_weights,), out_x, out_came = gather_rows(out_shard, from_y=out_y, hold_x=came)
    out_weights = out_weights.reshape(width, -1)
    kv_parts = everyone(kv_own.reshape(2, kv_cols, rows), "cx")

    seg_own = after(segment_ids[0][None], kv_own)
    seg_parts = everyone(seg_own, "cx")
    seg_near = jnp.concatenate(ordered(seg_parts, x), axis=0)
    seg_all = jnp.stack(ordered(everyone(seg_near, "cc"), c), axis=1).reshape(1, -1)
    doc_start = jnp.sum((seg_all < segment_ids[0][:, None]).astype(jnp.int32), axis=1)[None]
    query_place = place * rows + jnp.arange(rows, dtype=jnp.int32)[None]

    q_rot = after(q_rot, out_weights)
    if nx > 1:
        kv_parts[1:] = after(kv_parts[1:], q_rot, doc_start)
    kv_near = jnp.stack(kv_parts)
    kv_sources = everyone(kv_near, "cc")
    kv_place = jnp.stack(
        [(x ^ dx) * nc + (c ^ dc) for dc in range(nc) for dx in range(nx)]
    ).astype(jnp.int32)

    first_row = place * rows
    o_t, o_f, lse = attn_fwd(
        q_rot, kv_sources, kv_place, doc_start, query_place,
        make_bounds(doc_start, first_row, rows, FWD_TQ, FWD_TK), FWD_TQ, FWD_TK,
    )

    chunk = lambda v, k: lax.dynamic_slice_in_dim(v, (z ^ k) * share, share, 1)
    att_t = jnp.concatenate(
        [chunk(o_t, 0)] + [swap(chunk(o_t, k), "tp", k) for k in range(1, nz)], axis=0
    )
    rows_own = own_rows(tokens[0]).astype(F32)
    resid = rows_own + dot(att_t, out_weights, 0, 1)
    scale_f, normed_f = norm_parts(resid)
    hidden_own = (normed_f * gain_mlp).astype(BF)
    dims = (nf, nx, nc)
    hidden_parts = everyone(hidden_own, "cx")
    done = []
    for k, h in enumerate(hidden_parts):
        hidden_parts[k] = after(h, done[-1]) if k else h
        done.append(ffn_forward(hidden_parts[k], ffn_weights, dims, BF if k else F32))
    slopes, acts, inners, outs = zip(*done)

    def returned(parts, *others):
        total = parts[0]
        for k in range(1, nx):
            back = swap(parts[k], "cx", k)
            total = total + (after(back, *others) if others else back).astype(F32)
        return total

    result = resid + returned(outs)
    target = own_rows(teacher[0]).astype(F32)
    valid = own_rows(valid_mask[0].astype(F32)[:, None])
    error = result - target
    grad_out = valid * error
    loss_part = jnp.sum(grad_out * error)
    grad_out_low, result_low = after((grad_out.astype(BF), result.astype(BF)), loss_part[None])
    ffn_grads = everyone(grad_out_low, "cx")
    where = jnp.stack([y, c]).astype(jnp.int32)
    mixed = lax.all_gather(result_low, "tp", axis=0, tiled=True)

    def both_cores(parts):
        return [v for part in parts for v in everyone(part, "cc")]

    def to_rows(parts):
        return parts[0], parts[1:], [swap(parts[k], "fsdp", k) for k in range(1, nf)]

    def scattered(own, given, hold):
        total = own.astype(F32)
        for k in range(1, nf):
            total = total + after(given[k - 1], hold).astype(F32)
        total = total.astype(BF)
        return (total,) + spread(total)

    def spread(total):
        done = lax.psum_scatter(
            total.reshape(nz * nx * feat, hs), "tp", scatter_dimension=0, tiled=True
        ).reshape(nx, feat, hs)
        piece = lambda k: lax.dynamic_index_in_dim(done, x ^ k, 0, keepdims=False)
        pieces = [piece(0)] + [swap(piece(k), "cx", k) for k in range(1, nx)]
        return done, jnp.concatenate(ordered(pieces, x), axis=1).astype(F32)

    done = []
    for k, g in enumerate(ffn_grads):
        ffn_grads[k] = after(g, done[-1]) if k else g
        done.append(ffn_backward(ffn_grads[k], ffn_weights, slopes[k], acts[k], dims, BF if k else F32))
    grad_gates, grad_ups, ffn_backs = zip(*done)
    inners = both_cores(inners)
    inners[0] = after(inners[0], ffn_backs[-1])
    part_down = weight_grad(both_cores(ffn_grads), [inners], where, nz, dims)
    grad_gates, grad_ups = both_cores(grad_gates), both_cores(grad_ups)
    grad_gates[0] = after(grad_gates[0], part_down)
    part_gate_up = weight_grad(both_cores(hidden_parts), [grad_gates, grad_ups], where, nz, dims)
    down_own, down_sends, down_given = to_rows(part_down)
    grad_hidden_f = returned(ffn_backs, down_sends, part_gate_up)
    part_gain_mlp = jnp.sum(grad_hidden_f * normed_f, axis=0)
    grad_mid = grad_out + norm_back(grad_hidden_f, normed_f, scale_f, gain_mlp)
    grad_attn = after(grad_mid.astype(BF), mixed)
    g_att = dot(out_weights, grad_attn, 0, 1).astype(BF).reshape(nz, q_cols, share)
    g_parts = [g_att[0]] + [swap(g_att[k], "tp", k) for k in range(1, nz)]
    down_total, down_done, shard_down_t = scattered(down_own, down_given, g_parts[1:])
    gate_own, gate_sends, gate_given = to_rows(part_gate_up[:nf])
    up_own, up_sends, up_given = to_rows(part_gate_up[nf:])
    grad_heads = jnp.concatenate(ordered(after(g_parts, down_total, gate_sends), z), axis=1)

    bounds = make_bounds(doc_start, first_row, rows, BWD_TQ, BWD_TK)
    dqs, kv_sends, kv_grads = [], [], []
    for head in range(heads_k):
        dq, *dkv = attn_bwd(
            q_rot, kv_sources, kv_place, doc_start, query_place, bounds, grad_heads, o_f, lse,
            BWD_TQ, BWD_TK, head,
        )
        if head == heads_k - 1 and head:
            dkv[-1] = after(dkv[-1], gate_done, [o for _, o in kv_sends])
        dkv_others = [swap(dkv[k], "cc", k) for k in range(1, nc)]

        def kv_over_cores(k):
            total = dkv[0][k].astype(F32)
            for other in dkv_others:
                total = total + other[k].astype(F32)
            return total

        sends = [kv_over_cores(k).astype(BF) for k in range(1, nx)]
        if head == 0 and heads_k > 1:
            gate_total, gate_done, shard_gate = scattered(gate_own, gate_given, sends)
            grad_heads = after(grad_heads, sends, gate_total, up_sends, down_done)
        dqs.append(dq)
        kv_sends.append((kv_over_cores(0), [swap(sends[k - 1], "cx", k) for k in range(1, nx)]))
    if heads_k == 1:
        gate_total, gate_done, shard_gate = scattered(gate_own, gate_given, sends)
    gq = jnp.concatenate([turned(d.reshape(-1, HD, rows) * att_scale, cos_table, -sin_table) for d in dqs])
    gq = gq.reshape(q_cols, rows).astype(BF)
    up_total, up_done, shard_up = scattered(up_own, up_given, [kv_sends[0][1], dq])
    for kv_grad, others in kv_sends:
        for other in others:
            kv_grad = kv_grad + after(other, up_total).astype(F32)
        kv_grads.append(kv_grad)
    kv_grad = jnp.stack(kv_grads, axis=1)
    gk = turned(kv_grad[0] * att_scale, cos_table, -sin_table)
    gkv = jnp.concatenate([gk, kv_grad[1]], axis=0).reshape(2 * kv_cols, rows).astype(BF)
    grad_qkv = jnp.concatenate([gq, gkv], axis=0)
    part_h1 = dot(grad_qkv, w_qkv, 0, 1).astype(BF)
    part_h1 = after(part_h1, up_done)
    grad_hidden_a = lax.psum_scatter(part_h1, "tp", scatter_dimension=0, tiled=True)
    part_out = dot(after(grad_attn, sends), att_t, 0, 1).astype(BF)
    part_qkv = dot(after(hidden_a, part_h1), grad_qkv, 0, 1).astype(BF)
    shard_out_t, out_y = scatter_rows(part_out)
    shard_qkv, qkv_y = scatter_rows(part_qkv)
    shard_out_t = summed(
        shard_out_t.astype(BF).reshape(feat, nz, q_cols), 1, "tp", 0
    )
    grad_hidden_a = after(grad_hidden_a, out_y, qkv_y).astype(F32)
    scale_share = own_rows(scale_a)
    normed_share = rows_own * scale_share
    part_gain_att = jnp.sum(grad_hidden_a * normed_share, axis=0)
    grad_share = grad_mid + norm_back(grad_hidden_a, normed_share, scale_share, gain_att)
    grad_share = grad_share.astype(BF)
    grad_tokens = lax.all_gather(grad_share, "tp", axis=0, tiled=True)

    small = jnp.stack([part_gain_att, part_gain_mlp, jnp.broadcast_to(loss_part, (width,))])
    small = after(small, grad_share)
    for axis in AXES:
        step = 1
        while step < lax.axis_size(axis):
            small = small + swap(small, axis, step)
            step *= 2
    small_own = lax.dynamic_slice_in_dim(small[:2], ((y * nx + x) * nc + c) * feat, feat, 1)
    loss = small[2, 0] / (valid_count.astype(F32) * width)

    grad_tokens = after(
        grad_tokens, small_own, shard_qkv, shard_out_t, shard_gate, shard_up, shard_down_t
    ).astype(F32)
    return (
        mixed[None],
        loss,
        grad_tokens[None],
        small_own[0],
        shard_qkv[:, :q_cols],
        shard_qkv[:, q_cols : q_cols + kv_cols],
        shard_qkv[:, q_cols + kv_cols :],
        shard_out_t.T,
        small_own[1],
        shard_gate,
        shard_up,
        shard_down_t.T,
    )


FWD_TQ, FWD_TK = 256, 1024
BWD_TQ, BWD_TK = 256, 512


def solution(mesh):
    nf, nctx, nz = (mesh.shape[a] for a in ("fsdp", "ctx", "tp"))
    nc = 2 if nctx % 2 == 0 else 1
    fine = Mesh(mesh.devices.reshape(nf, nctx // nc, nc, nz), AXES)
    ctx = ("cx", "cc")
    rows = ("fsdp", "cx", "cc")
    return jax.shard_map(
        on_device,
        mesh=fine,
        in_specs=(
            P("fsdp", ctx, None),
            P("fsdp", ctx, None),
            P("fsdp", ctx),
            P("fsdp", ctx),
            P("fsdp", ctx),
            P(),
            P(rows),
            P(rows, "tp"),
            P(rows, "tp"),
            P(rows, "tp"),
            P("tp", rows),
            P(rows),
            P(rows, "tp"),
            P(rows, "tp"),
            P("tp", rows),
        ),
        out_specs=(
            P("fsdp", ctx, None),
            P(),
            P("fsdp", ctx, None),
            P(rows),
            P(rows, "tp"),
            P(rows, "tp"),
            P(rows, "tp"),
            P("tp", rows),
            P(rows),
            P(rows, "tp"),
            P(rows, "tp"),
            P("tp", rows),
        ),
        check_vma=False,
    )
```
